128 devices in a mesh: section: 2 (over core), dp: 16 (over z, y), mp: 4 (over x).
Axes of the slice: x: 4, y: 4, z: 4, core: 2. Of those that a mesh axis runs over, the one named last changes fastest.
Arguments:
- tokens: bfloat16 [64, 128, 1024], P('dp'), may hold values from -6 to 6
- cotangent: bfloat16 [64, 128, 1024], P('dp'), may hold values from -6 to 6
- seq_lengths: int32 [64, 4], P('dp'), may hold values from 1 to 125, as said below
- attn_gain: float32 [2, 1024], P('section'), may hold values from 0.5 to 1.5
- attn_shift: float32 [2, 1024], P('section'), may hold values from -3 to 3
- attn_weight: bfloat16 [2, 1024, 3, 1024], P('section', None, None, 'mp'), may hold values from -0.1875 to 0.1875
- attn_bias: float32 [2, 2, 1024], P('section', None, 'mp'), may hold values from -4 to 4
- dense_weight: bfloat16 [2, 1024, 1024], P('section', 'mp'), may hold values from -0.75 to 0.75
- dense_bias: float32 [2, 1024], P('section'), may hold values from -4 to 4
- mlp_gain: float32 [2, 1024], P('section'), may hold values from 0.5 to 1.5
- mlp_shift: float32 [2, 1024], P('section'), may hold values from -3 to 3
- expand_weight: bfloat16 [2, 1024, 4096], P('section', None, 'mp'), may hold values from -0.1875 to 0.1875
- expand_bias: float32 [2, 4096], P('section', 'mp'), may hold values from -4 to 4
- shrink_weight: bfloat16 [2, 4096, 1024], P('section', 'mp'), may hold values from -0.09375 to 0.09375
- shrink_bias: float32 [2, 1024], P('section'), may hold values from -4 to 4
Outputs:
- layer_out: bfloat16 [2, 64, 128, 1024], P('section', 'dp', 'mp')
- input_grad: bfloat16 [2, 64, 128, 1024], P('section', 'dp', 'mp')
- attn_gain_grad: float32 [2, 1024], P('section')
- attn_shift_grad: float32 [2, 1024], P('section')
- attn_weight_grad: float32 [2, 1024, 3, 1024], P('section', None, None, 'mp')
- attn_bias_grad: float32 [2, 2, 1024], P('section', None, 'mp')
- dense_weight_grad: float32 [2, 1024, 1024], P('section', 'mp')
- dense_bias_grad: float32 [2, 1024], P('section')
- mlp_gain_grad: float32 [2, 1024], P('section')
- mlp_shift_grad: float32 [2, 1024], P('section')
- expand_weight_grad: float32 [2, 1024, 4096], P('section', None, 'mp')
- expand_bias_grad: float32 [2, 4096], P('section', 'mp')
- shrink_weight_grad: float32 [2, 4096, 1024], P('section', 'mp')
- shrink_bias_grad: float32 [2, 1024], P('section')
The draws below stay inside these ranges and needn't reach their ends.
Inputs may be any that keep to these rules, and one draw needn't show every extreme that they name: `seq_lengths`: row 4 * g + j lists the lengths of the 4 sequences packed into micro-batch j of data group g; a row's lengths sum to at most 128, and in every data group one row sums to exactly 128.
All inputs are finite; a program needn't handle non-finite values.
Results may differ from the reference program's by a relative error of at most 0.03.
Values may be sent and summed in bfloat16 or wider, within the bound.
No kernel may reach another device: no remote copies, remote signals or barrier semaphores. Data moves between devices by JAX's collectives and lax.ppermute only.
A program may use at most 128 MiB of HBM per device.

```python
import jax
import jax.numpy as jnp
from jax import lax

D = 1024
HEADS = 16
HEAD = 64
FF = 4096
LAYERS = 2
MICRO_BATCHES = 4
MICRO_ROWS = 128
SEQUENCES_PACKED = 4
SLOTS = 64
N_DP = 16


def draw_seq_lengths(key, part):
    key = jax.random.fold_in(key, 7)
    key_total, key_full, key_matrix_full = jax.random.split(key, 3)
    length_totals = jax.random.randint(key_total, (N_DP, MICRO_BATCHES), MICRO_ROWS // 2, MICRO_ROWS + 1)
    full_slot = jax.random.randint(key_full, (N_DP,), 0, MICRO_BATCHES)
    is_full = jnp.arange(MICRO_BATCHES)[None, :] == full_slot[:, None]
    row_portions = jax.random.randint(key_matrix_full, (N_DP, MICRO_BATCHES, SEQUENCES_PACKED), 1, 9)
    spread_lengths = 1 + (length_totals[:, :, None] - SEQUENCES_PACKED) * row_portions // jnp.sum(row_portions, axis=2, keepdims=True)
    leftover_rows = length_totals - jnp.sum(spread_lengths, axis=2)
    spread_lengths = spread_lengths.at[:, :, SEQUENCES_PACKED - 1].add(leftover_rows)
    longest_length = jnp.concatenate([jnp.full((1,), MICRO_ROWS - SEQUENCES_PACKED + 1, jnp.int32), jnp.ones((SEQUENCES_PACKED - 1,), jnp.int32)])
    sequence_lengths = jnp.where(is_full[:, :, None], longest_length[None, None, :], spread_lengths)
    return sequence_lengths.reshape(N_DP * MICRO_BATCHES, SEQUENCES_PACKED).astype(jnp.int32)


def levels(rng, shape, cuts, smallest, high):
    level = 1.0
    for dim, blocks in cuts:
        steps = jax.random.uniform(jax.random.fold_in(jax.random.fold_in(rng, 6), dim), (blocks,), jnp.float32, smallest / len(cuts), high / len(cuts))
        level = level * jnp.repeat(jnp.exp(steps), shape[dim] // blocks).reshape((-1,) + (1,) * (len(shape) - 1 - dim))
    return level


def noise(stream_key, extent, spread, bound, shards=(), kind=jnp.bfloat16):
    entries = jax.random.normal(stream_key, extent, jnp.float32) * spread
    if len(shards) > 0:
        entries = levels(stream_key, extent, shards, -0.22, 0.18) * entries
    return jnp.clip(entries, min=-bound, max=bound).astype(kind)


def setup_inputs(seed: int = 0) -> dict:
    keys = jax.random.split(jax.random.key(seed), 16)
    tokens = noise(keys[0], (SLOTS, MICRO_ROWS, D), 1.0, 6.0, ((0, 16),))
    cotangent = noise(keys[1], (SLOTS, MICRO_ROWS, D), 1.0, 6.0, ((0, 16),))
    seq_lengths = draw_seq_lengths(jax.random.fold_in(keys[15], 71), 0)
    attn_gain = jnp.clip(1.0 + 0.1 * jax.random.normal(keys[3], (LAYERS, D), jnp.float32), 0.5, 1.5)
    attn_shift = noise(keys[4], (LAYERS, D), 0.2, 3.0, ((0, 2),), jnp.float32)
    attn_weight = noise(keys[5], (LAYERS, D, 3, D), D ** -0.5, 0.1875, ((0, 2), (3, 4)))
    attn_bias = noise(keys[6], (LAYERS, 2, D), 0.3, 4.0, ((0, 2), (2, 4)), jnp.float32)
    dense_weight = noise(keys[7], (LAYERS, D, D), (D // 16) ** -0.5, 0.75, ((0, 2), (1, 4)))
    dense_bias = noise(keys[8], (LAYERS, D), 0.3, 4.0, ((0, 2),), jnp.float32)
    mlp_gain = jnp.clip(1.0 + 0.1 * jax.random.normal(keys[9], (LAYERS, D), jnp.float32), 0.5, 1.5)
    mlp_shift = noise(keys[10], (LAYERS, D), 0.2, 3.0, ((0, 2),), jnp.float32)
    expand_weight = noise(keys[11], (LAYERS, D, FF), D ** -0.5, 0.1875, ((0, 2), (2, 4)))
    expand_bias = noise(keys[12], (LAYERS, FF), 0.3, 4.0, ((0, 2), (1, 4)), jnp.float32)
    shrink_weight = noise(keys[13], (LAYERS, FF, D), FF ** -0.5, 0.09375, ((0, 2), (1, 4)))
    shrink_bias = noise(keys[14], (LAYERS, D), 0.3, 4.0, ((0, 2),), jnp.float32)
    return dict(tokens=tokens, cotangent=cotangent, seq_lengths=seq_lengths, attn_gain=attn_gain, attn_shift=attn_shift, attn_weight=attn_weight, attn_bias=attn_bias, dense_weight=dense_weight, dense_bias=dense_bias, mlp_gain=mlp_gain, mlp_shift=mlp_shift, expand_weight=expand_weight, expand_bias=expand_bias, shrink_weight=shrink_weight, shrink_bias=shrink_bias)


@jax.custom_vjp
def low(v):
    return lax.optimization_barrier(v.astype(jnp.bfloat16)).astype(jnp.float32)

@jax.custom_vjp
def low_back(v):
    return v

def low_keep(v):
    return (low(v), None)

def low_pass(kept, grad):
    return (grad,)

def back_keep(v):
    return (v, None)

def back_low(kept, grad):
    return (low(grad),)
low.defvjp(low_keep, low_pass)
low_back.defvjp(back_keep, back_low)
epsilon = 1e-05
highest = lax.Precision.HIGHEST

def norm_rows(hidden, gain, shift):
    center = hidden - lax.optimization_barrier(jnp.mean(hidden, axis=-1, keepdims=True))
    variance = lax.optimization_barrier(jnp.mean(center * center, axis=-1, keepdims=True))
    return center * lax.rsqrt(variance + epsilon) * gain + shift

def layout_rows(lengths_row):
    bounds = jnp.cumsum(lengths_row.astype(jnp.int32))
    position = jnp.arange(MICRO_ROWS, dtype=jnp.int32)
    segment = lax.optimization_barrier(jnp.sum((position[:, None] >= bounds[None, :]).astype(jnp.int32), axis=1))
    live_rows = (position < bounds[-1]).astype(jnp.float32)
    allowed = (segment[:, None] == segment[None, :]) & (position[None, :] <= position[:, None])
    distance = (position[:, None] - position[None, :]).astype(jnp.float32)
    return (live_rows, allowed, distance)

def layer_apply(layer_in, params, live_rows, allowed, distance):
    gain_one, shift_one, attn_matrix, attn_offset, dense_matrix, dense_offset, gain_two, shift_two, expand_matrix, expand_offset, shrink_matrix, shrink_offset = params
    slopes = jnp.exp2(-8.0 * (jnp.arange(HEADS).astype(jnp.float32) + 1.0) / HEADS)
    first_in = low(norm_rows(layer_in, gain_one, shift_one))
    mixed_rows = jnp.einsum('sd,dce->sce', first_in, attn_matrix, precision=highest)
    bias_rows = jnp.stack([attn_offset[0], jnp.zeros_like(attn_offset[0]), attn_offset[1]])
    projected = low_back(low(mixed_rows + bias_rows[None]))
    query_rows = projected[:, 0].reshape(MICRO_ROWS, HEADS, HEAD)
    key_rows = projected[:, 1].reshape(MICRO_ROWS, HEADS, HEAD)
    value_rows = projected[:, 2].reshape(MICRO_ROWS, HEADS, HEAD)
    scores = jnp.einsum('qhd,khd->hqk', query_rows, key_rows, precision=highest) * HEAD ** (-0.5)
    scores = scores - slopes[:, None, None] * distance[None]
    scores = low_back(scores)
    scores = jnp.where(allowed[None], scores, -1e+30)
    row_top = lax.optimization_barrier(jnp.max(scores, axis=-1, keepdims=True))
    exponent = jnp.exp(scores - row_top)
    prob_rows = exponent / lax.optimization_barrier(jnp.sum(exponent, axis=-1, keepdims=True))
    context = jnp.einsum('hqk,khd->qhd', low(prob_rows), value_rows, precision=highest).reshape(MICRO_ROWS, D)
    context = low_back(low(context))
    attn_out = low_back(jnp.dot(context, dense_matrix, precision=highest) + dense_offset)
    hidden_one = layer_in + attn_out
    second = low(norm_rows(hidden_one, gain_two, shift_two))
    up_rows = low_back(jnp.dot(second, expand_matrix, precision=highest) + expand_offset)
    activated = low(jax.nn.gelu(up_rows, approximate=True))
    mlp_out = low_back(jnp.dot(activated, shrink_matrix, precision=highest) + shrink_offset)
    return live_rows[:, None] * (hidden_one + mlp_out)

def forward_pair(layer_in, stacked, offset, live_rows, allowed, distance):
    first_layer = tuple((param_array[0] for param_array in stacked))
    second_layer = tuple((param_array[1] for param_array in stacked))
    middle = low_back(low(layer_apply(layer_in, first_layer, live_rows, allowed, distance)) + offset)
    final = low(layer_apply(middle, second_layer, live_rows, allowed, distance))
    return (middle, final)

def reference(tokens, cotangent, seq_lengths, attn_gain, attn_shift, attn_weight, attn_bias, dense_weight, dense_bias, mlp_gain, mlp_shift, expand_weight, expand_bias, shrink_weight, shrink_bias):
    params = tuple((param_array.astype(jnp.float32) for param_array in (attn_gain, attn_shift, attn_weight, attn_bias, dense_weight, dense_bias, mlp_gain, mlp_shift, expand_weight, expand_bias, shrink_weight, shrink_bias)))

    def one_slot(carry, item):
        slot_tokens, slot_cot, lengths_row = item
        live_rows, allowed, distance = layout_rows(lengths_row)

        def run_pair(layer_in, stacked, offset):
            return forward_pair(layer_in, stacked, offset, live_rows, allowed, distance)
        outputs, pull = jax.vjp(run_pair, slot_tokens.astype(jnp.float32), params, jnp.zeros((MICRO_ROWS, D), jnp.float32))
        grad_tokens, grad_params, grad_middle = pull((jnp.zeros((MICRO_ROWS, D), jnp.float32), slot_cot.astype(jnp.float32)))
        carry = jax.tree.map(jnp.add, carry, grad_params)
        return (carry, (outputs[0].astype(jnp.bfloat16), outputs[1].astype(jnp.bfloat16), grad_tokens.astype(jnp.bfloat16), grad_middle.astype(jnp.bfloat16)))
    start = jax.tree.map(jnp.zeros_like, params)
    length_totals, stacked_out = lax.scan(one_slot, start, (tokens, cotangent, seq_lengths))
    layer_out = jnp.stack([stacked_out[0], stacked_out[1]])
    input_grad = jnp.stack([stacked_out[2], stacked_out[3]])
    return (layer_out, input_grad, length_totals[0], length_totals[1], length_totals[2], length_totals[3], length_totals[4], length_totals[5], length_totals[6], length_totals[7], length_totals[8], length_totals[9], length_totals[10], length_totals[11])
```

```python
import jax
import jax.numpy as jnp
from jax import lax
from jax.sharding import PartitionSpec as P

HEADS = 16
HEAD = 64
EPS = 1e-05
BF = jnp.bfloat16
F32 = jnp.float32


def dot(a, b):
    return jnp.dot(a, b, preferred_element_type=F32)


def dot_t(a, b):
    return lax.dot_general(a, b, (((1,), (1,)), ((), ())), preferred_element_type=F32)


def t_dot(a, b):
    return lax.dot_general(a, b, (((0,), (0,)), ((), ())), preferred_element_type=F32)


def normalize(h):
    center = h - jnp.mean(h, axis=-1, keepdims=True)
    inverse = lax.rsqrt(jnp.mean(center * center, axis=-1, keepdims=True) + EPS)
    return center * inverse, inverse


def norm_back(normed, inverse, gain, grad):
    z = grad * gain
    return inverse * (
        z
        - jnp.mean(z, axis=-1, keepdims=True)
        - normed * jnp.mean(z * normed, axis=-1, keepdims=True)
    )


def ring(axis, steps):
    n = lax.axis_size(axis)
    return [(i, (i + steps) % n) for i in range(n)]


def swap(x):
    return lax.ppermute(x, "section", [(0, 1), (1, 0)])


def gather_rows(own):
    parts = [own] + [lax.ppermute(own, "mp", ring("mp", k)) for k in (1, 2, 3)]
    return jnp.concatenate(parts, axis=0)


def scatter_sum(partial):
    rows = partial.shape[0] // 4
    low = partial.astype(BF)
    total = partial[:rows].astype(F32)
    for k in (1, 2, 3):
        total = total + lax.ppermute(
            low[k * rows : (k + 1) * rows], "mp", ring("mp", -k)
        ).astype(F32)
    return total


def to_heads(x):
    return x.reshape(4, 2, 32, -1, HEAD).transpose(1, 3, 0, 2, 4).reshape(2, -1, 128, HEAD)


def from_heads(x):
    return x.reshape(2, -1, 4, 32, HEAD).transpose(2, 0, 3, 1, 4).reshape(256, -1)


def bdot(a, b, ca, cb):
    return lax.dot_general(a, b, (((ca,), (cb,)), ((0, 1), (0, 1))), preferred_element_type=F32)


GELU_C = 0.7978845608
GELU_A = 0.044715


def gelu_pair(u):
    t = jnp.tanh(GELU_C * (u + GELU_A * u * u * u))
    act = 0.5 * u * (1 + t)
    grad = 0.5 * (1 + t) + 0.5 * u * (1 - t * t) * (GELU_C * (1 + 3 * GELU_A * u * u))
    return act, grad


def attn_forward(first, qkv, bias, dense, info):
    slopes, allowed, distance = info
    proj = [
        dot(first, qkv[0]) + bias[0],
        dot(first, qkv[1]),
        dot(first, qkv[2]) + bias[1],
    ]
    proj = [p.astype(BF) for p in proj]
    q, k, v = [to_heads(p) for p in proj]
    scores = bdot(q, k, 3, 3) * HEAD**-0.5 - slopes[None, :, None, None] * distance
    scores = jnp.where(allowed[:, None], scores, -1e30)
    top = jnp.max(scores, axis=-1, keepdims=True)
    e = jnp.exp(scores - top)
    probs = e / jnp.sum(e, axis=-1, keepdims=True)
    context = from_heads(bdot(probs.astype(BF), v, 3, 2).astype(BF))
    return dot(context, dense), (q, k, v, probs, context)


def attn_backward(dense_full, saved, qkv, dense):
    q, k, v, probs, context = saved
    grad_context = to_heads(dot_t(dense_full, dense).astype(BF))
    grad_v = bdot(probs.astype(BF), grad_context, 2, 2)
    grad_probs = bdot(grad_context, v, 3, 3)
    grad_scores = (
        probs * (grad_probs - jnp.sum(probs * grad_probs, axis=-1, keepdims=True))
    ).astype(BF)
    grad_q = bdot(grad_scores, k, 3, 2) * HEAD**-0.5
    grad_k = bdot(grad_scores, q, 2, 2) * HEAD**-0.5
    grads = [from_heads(g.astype(BF)) for g in (grad_q, grad_k, grad_v)]
    partial = dot_t(grads[0], qkv[0]) + dot_t(grads[1], qkv[1]) + dot_t(grads[2], qkv[2])
    return partial, grads


def dp_total(x):
    n = lax.axis_size("dp")
    shape = x.shape
    parts = x.reshape((n, shape[0] // n) + shape[1:])
    got = lax.all_to_all(parts, "dp", 0, 0)
    share = jnp.sum(got.astype(F32), axis=0).astype(BF)
    full = lax.all_to_all(jnp.broadcast_to(share[None], parts.shape), "dp", 0, 0)
    return full.reshape(shape)


def dp_total_far(x):
    return lax.psum(x, "dp")


def dp_perm(axis, steps):
    n = lax.axis_size("dp")
    w = 4
    h = n // w
    if axis == "y":
        return [(i, (i // w) * w + (i % w + steps) % w) for i in range(n)]
    return [(i, ((i // w + steps) % h) * w + i % w) for i in range(n)]


def small_total(x):
    mixed = lax.broadcasted_iota(jnp.int32, x.shape, 0) < 6
    got = sum(lax.ppermute(x, "mp", ring("mp", k)) for k in (1, 2, 3))
    x = x + jnp.where(mixed, got, 0.0)
    n = lax.axis_size("dp")
    for axis, size in (("y", 4), ("z", n // 4)):
        x = x + sum(lax.ppermute(x, "dp", dp_perm(axis, k)) for k in range(1, size))
    return x


def per_device(
    tokens,
    cotangent,
    seq_lengths,
    attn_gain,
    attn_shift,
    attn_weight,
    attn_bias,
    dense_weight,
    dense_bias,
    mlp_gain,
    mlp_shift,
    expand_weight,
    expand_bias,
    shrink_weight,
    shrink_bias,
):
    sec = lax.axis_index("section")
    mp = lax.axis_index("mp")
    on0 = sec == 0

    own_qkv = jnp.transpose(attn_weight[0], (1, 0, 2))
    own_w = [own_qkv, dense_weight[0], expand_weight[0], shrink_weight[0]]
    vectors = jnp.concatenate(
        [attn_gain, attn_shift, dense_bias, mlp_gain, mlp_shift, shrink_bias, expand_bias]
        + [jnp.pad(attn_bias.reshape(1, -1), ((0, 0), (0, 512)))],
        axis=0,
    )
    got_vec = swap(vectors)
    got_w = [swap(w) for w in own_w]

    def pick(layer, own, got):
        return jnp.where(on0, own, got) if layer == 0 else jnp.where(on0, got, own)

    def layer_weights(layer):
        w = [pick(layer, o, g) for o, g in zip(own_w, got_w)]
        vec = pick(layer, vectors, got_vec)
        return w, vec

    def rel(x):
        x = lax.dynamic_slice_in_dim(x, 2 * sec, 2, 0).reshape(2, 4, 32, -1)
        parts = [lax.dynamic_index_in_dim(x, (mp - k) % 4, 1, keepdims=False) for k in range(4)]
        return jnp.concatenate(parts, axis=0).reshape(256, -1)

    lengths = lax.dynamic_slice_in_dim(seq_lengths, 2 * sec, 2, 0)
    bounds = jnp.cumsum(lengths, axis=1)
    pos = (32 * ((mp - jnp.arange(4)) % 4)[:, None] + jnp.arange(32)[None]).reshape(128)
    segment = jnp.sum((pos[None, :, None] >= bounds[:, None, :]).astype(jnp.int32), axis=2)
    allowed = (segment[:, :, None] == segment[:, None, :]) & (pos[None, None, :] <= pos[None, :, None])
    distance = (pos[:, None] - pos[None, :]).astype(F32)
    live = (pos[None] < bounds[:, -1:]).astype(F32)
    live_rows = live.reshape(2, 4, 32).transpose(1, 0, 2).reshape(256, 1)
    live_own = live_rows[:64]
    heads_local = attn_weight.shape[3] // HEAD
    head_ids = mp * heads_local + jnp.arange(heads_local)
    slopes = jnp.exp2(-8.0 * (head_ids + 1).astype(F32) / HEADS)
    info = (slopes, allowed, distance)

    x_all = rel(tokens).astype(F32)
    cot = rel(cotangent)

    def forward(layer, x_own, first, last):
        (qkv, dense, expand, shrink), vec = layer_weights(layer)
        bias = vec[7].reshape(4, 256)[:2]
        partial, saved = attn_forward(first, qkv, bias, dense, info)
        hidden = x_own + scatter_sum(partial) + vec[2]
        normed_two, inverse_two = normalize(hidden)
        second = gather_rows((normed_two * vec[3] + vec[4]).astype(BF))
        up = dot(second, expand) + vec[6]
        act, act_grad = gelu_pair(up)
        act = act.astype(BF)
        out = live_own * (hidden + scatter_sum(dot(act, shrink)) + vec[5])
        keep = dict(
            first=first,
            attn=saved,
            normed_two=normed_two,
            inverse_two=inverse_two,
            second=second,
            act=act,
            act_grad=act_grad,
        )
        return out.astype(BF), keep

    def exchange(send, keep):
        return [jnp.concatenate([k, swap(s)], axis=0) for k, s in zip(keep, send)]

    def backward(layer, keep, grad_own, branch, normed, inverse):
        (qkv, dense, expand, shrink), vec = layer_weights(layer)
        grad_act = dot_t(branch, shrink)
        grad_up = (grad_act * keep["act_grad"]).astype(BF)
        second, act = keep["second"], keep["act"]
        grad_second = scatter_sum(dot_t(grad_up, expand))
        send = [jnp.where(on0, act, second), jnp.where(on0, branch, grad_up)]
        hold = [jnp.where(on0, second, act), jnp.where(on0, grad_up, branch)]
        left, right = exchange(send, hold)
        mlp_grad = t_dot(left, right).astype(BF)
        normed_two = keep["normed_two"]
        grad_hidden = grad_own + norm_back(normed_two, keep["inverse_two"], vec[3], grad_second)
        dense_low = grad_hidden.astype(BF)
        dense_full = gather_rows(dense_low)
        partial, grads = attn_backward(dense_full, keep["attn"], qkv, dense)
        first, context = keep["first"], keep["attn"][4]
        half = [first[:, :512], first[:, 512:]]
        dhalf = [dense_full[:, :512], dense_full[:, 512:]]
        shared = jnp.concatenate(grads + [context], axis=1)
        left, right_d, both = exchange(
            [jnp.where(on0, half[1], half[0]), jnp.where(on0, dhalf[1], dhalf[0]), shared],
            [jnp.where(on0, half[0], half[1]), jnp.where(on0, dhalf[0], dhalf[1]), shared],
        )
        qkv_grad = [t_dot(left, both[:, 256 * c : 256 * c + 256]) for c in range(3)]
        dense_grad = t_dot(both[:, 768:], right_d)
        attn_grad = jnp.concatenate(
            qkv_grad + [dense_grad[:, :256], dense_grad[:, 256:]], axis=0
        ).astype(BF)
        grad_first = scatter_sum(partial)
        grad_in = grad_hidden + norm_back(normed, inverse, vec[0], grad_first)
        rows = [
            jnp.sum(grad_first * normed, axis=0),
            jnp.sum(grad_first, axis=0),
            jnp.sum(dense_low.astype(F32), axis=0),
            jnp.sum(grad_second * normed_two, axis=0),
            jnp.sum(grad_second, axis=0),
            jnp.sum(branch[:64].astype(F32), axis=0),
            jnp.sum(grad_up.astype(F32), axis=0),
            jnp.concatenate(
                [
                    jnp.sum(grads[0].astype(F32), axis=0),
                    jnp.sum(grads[2].astype(F32), axis=0),
                    jnp.zeros((512,), F32),
                ]
            ),
        ]
        return grad_in.astype(BF), mlp_grad, attn_grad, jnp.stack(rows)

    vec0 = pick(0, vectors, got_vec)
    normed0, inverse0 = normalize(x_all)
    first0 = (normed0 * vec0[0] + vec0[1]).astype(BF)
    x_own0 = x_all[:64]
    out0, keep0 = forward(0, x_own0, first0, False)
    vec1 = pick(1, vectors, got_vec)
    x_own1 = out0.astype(F32)
    normed1, inverse1 = normalize(x_own1)
    first1 = gather_rows((normed1 * vec1[0] + vec1[1]).astype(BF))
    out1, keep1 = forward(1, x_own1, first1, True)
    branch1 = cot * live_rows.astype(BF)
    g1, mlp1, attn1, small1 = backward(
        1, keep1, branch1[:64].astype(F32), branch1, normed1, inverse1
    )
    mlp1 = dp_total_far(mlp1)
    attn1 = dp_total_far(attn1)
    pre0 = live_own * g1.astype(F32)
    branch0 = gather_rows(pre0.astype(BF))
    g0, mlp0, attn0, small0 = backward(0, keep0, pre0, branch0, normed0[:64], inverse0[:64])
    mlp0 = dp_total(mlp0)
    attn0 = dp_total(attn0)

    small = jnp.where(on0, small0, small1) + swap(jnp.where(on0, small1, small0))
    small = small_total(small)

    def both_halves(held0, held1):
        mine = jnp.where(on0, held0, held1)
        other = swap(jnp.where(on0, held1, held0))
        return jnp.where(on0, mine, other).astype(F32), jnp.where(on0, other, mine).astype(F32)

    expand_grad, shrink_grad = both_halves(mlp0, mlp1)
    lower, upper = both_halves(attn0, attn1)
    qkv_grad = jnp.concatenate(
        [lower[:1536].reshape(3, 512, 256), upper[:1536].reshape(3, 512, 256)], axis=1
    )
    dense_grad = jnp.concatenate(
        [lower[1536:1792], lower[1792:], upper[1536:1792], upper[1792:]], axis=1
    )

    def all_slots(held0, held1):
        mine = jnp.where(on0, held0, held1).reshape(2, 32, -1)
        other = swap(jnp.where(on0, held1, held0)).reshape(2, 32, -1)
        return jnp.concatenate(
            [jnp.where(on0, mine, other), jnp.where(on0, other, mine)], axis=0
        )

    layer_out = all_slots(out0, out1)
    input_grad = all_slots(g0, g1)
    return (
        layer_out[None],
        input_grad[None],
        small[0:1],
        small[1:2],
        jnp.transpose(qkv_grad, (1, 0, 2))[None],
        small[7, :512].reshape(1, 2, 256),
        dense_grad[None],
        small[2:3],
        small[3:4],
        small[4:5],
        expand_grad[None],
        small[6:7],
        shrink_grad[None],
        small[5:6],
    )


def solution(mesh):
    return jax.shard_map(
        per_device,
        mesh=mesh,
        in_specs=(
            P("dp", None, None),
            P("dp", None, None),
            P("dp", None),
            P("section", None),
            P("section", None),
            P("section", None, None, "mp"),
            P("section", None, "mp"),
            P("section", "mp", None),
            P("section", None),
            P("section", None),
            P("section", None),
            P("section", None, "mp"),
            P("section", "mp"),
            P("section", "mp", None),
            P("section", None),
        ),
        out_specs=(
            P("section", "dp", "mp", None),
            P("section", "dp", "mp", None),
            P("section", None),
            P("section", None),
            P("section", None, None, "mp"),
            P("section", None, "mp"),
            P("section", "mp", None),
            P("section", None),
            P("section", None),
            P("section", None),
            P("section", None, "mp"),
            P("section", "mp"),
            P("section", "mp", None),
            P("section", None),
        ),
        check_vma=False,
    )
```

```python
import jax
import jax.numpy as jnp
from jax import lax
from jax.experimental import pallas as pl
from jax.experimental.pallas import tpu as pltpu
from jax.sharding import PartitionSpec as P

HEADS = 16
HEAD = 64
EPS = 1e-05
BF = jnp.bfloat16
F32 = jnp.float32


def dot(a, b):
    return jnp.dot(a, b, preferred_element_type=F32)


def dot_t(a, b):
    return lax.dot_general(a, b, (((1,), (1,)), ((), ())), preferred_element_type=F32)


def t_dot(a, b):
    return lax.dot_general(a, b, (((0,), (0,)), ((), ())), preferred_element_type=F32)


def normalize(h):
    center = h - jnp.mean(h, axis=-1, keepdims=True)
    inverse = lax.rsqrt(jnp.mean(center * center, axis=-1, keepdims=True) + EPS)
    return center * inverse, inverse


def norm_back(normed, inverse, gain, grad):
    z = grad * gain
    return inverse * (
        z
        - jnp.mean(z, axis=-1, keepdims=True)
        - normed * jnp.mean(z * normed, axis=-1, keepdims=True)
    )


def ring(axis, steps):
    n = lax.axis_size(axis)
    return [(i, (i + steps) % n) for i in range(n)]


def swap(x):
    return lax.ppermute(x, "section", [(0, 1), (1, 0)])


def dp_total(x):
    n = lax.axis_size("dp")
    shape = x.shape
    parts = x.reshape((n, shape[0] // n) + shape[1:])
    got = lax.all_to_all(parts, "dp", 0, 0)
    share = jnp.sum(got.astype(F32), axis=0).astype(BF)
    full = lax.all_to_all(jnp.broadcast_to(share[None], parts.shape), "dp", 0, 0)
    return full.reshape(shape)


def dp_total_far(x):
    return lax.psum(x, "dp")


def dp_perm(axis, steps):
    n = lax.axis_size("dp")
    w = 4
    h = n // w
    if axis == "y":
        return [(i, (i // w) * w + (i % w + steps) % w) for i in range(n)]
    return [(i, ((i // w + steps) % h) * w + i % w) for i in range(n)]


def small_total(x):
    mixed = lax.broadcasted_iota(jnp.int32, x.shape, 0) < 6
    got = sum(lax.ppermute(x, "mp", ring("mp", k)) for k in (1, 2, 3))
    x = x + jnp.where(mixed, got, 0.0)
    n = lax.axis_size("dp")
    for axis, size in (("y", 4), ("z", n // 4)):
        x = x + sum(lax.ppermute(x, "dp", dp_perm(axis, k)) for k in range(1, size))
    return x


def gather_rows(own):
    return [own] + [lax.ppermute(own, "mp", ring("mp", k)) for k in (1, 2, 3)]


def scatter_rows(blocks):
    return [blocks[0]] + [lax.ppermute(blocks[k], "mp", ring("mp", -k)) for k in (1, 2, 3)]


GELU_C = 0.7978845608
GELU_A = 0.044715
ROWS = 256
OWN = 64
D = 1024
FF = 1024
TILE = 256
SCALE = HEAD**-0.5


def gelu_pair(u):
    t = jnp.tanh(GELU_C * (u + GELU_A * u * u * u))
    act = 0.5 * u * (1 + t)
    grad = 0.5 * (1 + t) + 0.5 * u * (1 - t * t) * (GELU_C * (1 + 3 * GELU_A * u * u))
    return act, grad


def sds(shape, dtype):
    return jax.ShapeDtypeStruct(shape, dtype)


PARTIAL = [sds((OWN, D), F32)] + [sds((OWN, D), BF)] * 3
VM = pl.BlockSpec(memory_space=pltpu.VMEM)
SM = pl.BlockSpec(memory_space=pltpu.SMEM)
HB = pl.BlockSpec(memory_space=pl.ANY)


def call(kernel, outs, ins, scratch=(), flops=1e9, limit=28):
    specs = [HB if kind == "h" else SM if kind == "s" else VM for kind, _ in ins]
    arrays = [a for _, a in ins]
    size = sum(a.size * a.dtype.itemsize for a in arrays) + sum(
        o.size * o.dtype.itemsize for o in outs
    )
    return pl.pallas_call(
        kernel,
        out_shape=list(outs),
        in_specs=specs,
        out_specs=[VM] * len(outs),
        scratch_shapes=list(scratch),
        compiler_params=pltpu.CompilerParams(vmem_limit_bytes=limit * 2**20),
        cost_estimate=pl.CostEstimate(
            flops=int(flops), bytes_accessed=int(size), transcendentals=0
        ),
    )(*arrays)


def fetch(sec, layer, own, got, dst, sem):
    mine = sec[0] == layer

    @pl.when(mine)
    def _():
        pltpu.make_async_copy(own, dst, sem).start()

    @pl.when(jnp.logical_not(mine))
    def _():
        pltpu.make_async_copy(got, dst, sem).start()

    return pltpu.make_async_copy(own, dst, sem)


def put_partial(outs, cols, value):
    outs[0][:, cols] = value[:OWN]
    for k in (1, 2, 3):
        outs[k][:, cols] = value[OWN * k : OWN * (k + 1)].astype(BF)


def tiles(width):
    return [pl.ds(i * TILE, TILE) for i in range(width // TILE)]


def lane_low():
    return lax.broadcasted_iota(jnp.int32, (ROWS, 128), 1) < HEAD


def attn_forward(layer, sec, slopes, source, vec, dist, qkv, dense):
    def kernel(*refs):
        n = len(source)
        sec, slopes, src = refs[0], refs[1], refs[2 : 2 + n]
        vec, dist, qo, qg, do, dg = refs[2 + n : 8 + n]
        o0, o1, o2, o3, proj, probs, context, hold, send = refs[8 + n : 17 + n]
        first, wq, wd, sem = refs[17 + n :]
        get_q = fetch(sec, layer, qo, qg, wq, sem.at[0])
        get_d = fetch(sec, layer, do, dg, wd, sem.at[1])
        if n == 1:
            normed, _ = normalize(src[0][...].astype(F32))
            first[...] = (normed * vec[0:1] + vec[1:2]).astype(BF)
        else:
            for k in range(4):
                first[pl.ds(OWN * k, OWN)] = src[k][...]
        on0 = sec[0] == 0
        hold[...] = jnp.where(on0, first[:, :512], first[:, 512:])
        send[...] = jnp.where(on0, first[:, 512:], first[:, :512])
        get_q.wait()
        f = first[...]
        proj[0] = (dot(f, wq[0]) + vec[7:8, 0:256]).astype(BF)
        proj[1] = dot(f, wq[1]).astype(BF)
        proj[2] = (dot(f, wq[2]) + vec[7:8, 256:512]).astype(BF)
        low = lane_low()
        for pair in range(2):
            cols = pl.ds(128 * pair, 128)
            q, k, v = proj[0, :, cols], proj[1, :, cols], proj[2, :, cols]
            ctx = []
            for h in range(2):
                picked = jnp.where(low if h == 0 else jnp.logical_not(low), q, jnp.zeros_like(q))
                s = dot_t(picked, k) * SCALE - slopes[2 * pair + h] * dist[...]
                e = jnp.exp(s - jnp.max(s, axis=-1, keepdims=True))
                p = e / jnp.sum(e, axis=-1, keepdims=True)
                probs[2 * pair + h] = p
                ctx.append(dot(p.astype(BF), v))
            context[:, cols] = jnp.where(low, ctx[0], ctx[1]).astype(BF)
        get_d.wait()
        c = context[...]
        for cols in tiles(D):
            put_partial((o0, o1, o2, o3), cols, dot(c, wd[:, cols]))

    outs = PARTIAL + [
        sds((3, ROWS, 256), BF),
        sds((4, ROWS, ROWS), F32),
        sds((ROWS, 256), BF),
        sds((ROWS, 512), BF),
        sds((ROWS, 512), BF),
    ]
    ins = [("s", sec), ("s", slopes)] + [("v", a) for a in source]
    ins += [("v", vec), ("v", dist), ("h", qkv[0]), ("h", qkv[1]), ("h", dense[0]), ("h", dense[1])]
    scratch = [
        pltpu.VMEM((ROWS, D), BF),
        pltpu.VMEM((3, D, 256), BF),
        pltpu.VMEM((256, D), BF),
        pltpu.SemaphoreType.DMA((2,)),
    ]
    r = call(kernel, outs, ins, scratch, 8e8)
    return r[:4], dict(proj=r[4], probs=r[5], context=r[6], hold_f=r[7], send_f=r[8])


def total(refs):
    return refs[0][...] + refs[1][...].astype(F32) + refs[2][...].astype(F32) + refs[3][...].astype(F32)


def after_attn(blocks, x_own, vec):
    def kernel(a, b, c, d, x, vec, hidden, second):
        h = x[...].astype(F32) + total((a, b, c, d)) + vec[2:3]
        hidden[...] = h
        normed, _ = normalize(h)
        second[...] = (normed * vec[3:4] + vec[4:5]).astype(BF)

    return call(
        kernel,
        [sds((OWN, D), F32), sds((OWN, D), BF)],
        [("v", a) for a in (*blocks, x_own, vec)],
        flops=2e6,
    )


def mlp_forward(layer, sec, blocks, vec, expand, shrink):
    def kernel(sec, b0, b1, b2, b3, vec, eo, eg, so, sg, o0, o1, o2, o3, act_grad, hold, send, second, act, we, ws, sem):
        get_e = fetch(sec, layer, eo, eg, we, sem.at[0])
        get_s = fetch(sec, layer, so, sg, ws, sem.at[1])
        for k, b in enumerate((b0, b1, b2, b3)):
            second[pl.ds(OWN * k, OWN)] = b[...]
        get_e.wait()
        x = second[...]
        for cols in tiles(FF):
            a, g = gelu_pair(dot(x, we[:, cols]) + vec[6:7, cols])
            act[:, cols] = a.astype(BF)
            act_grad[:, cols] = g
        get_s.wait()
        a = act[...]
        on0 = sec[0] == 0
        for cols in tiles(D):
            put_partial((o0, o1, o2, o3), cols, dot(a, ws[:, cols]))
            hold[:, cols] = jnp.where(on0, second[:, cols], act[:, cols])
            send[:, cols] = jnp.where(on0, act[:, cols], second[:, cols])

    wide = sds((ROWS, FF), BF)
    ins = [("s", sec)] + [("v", a) for a in (*blocks, vec)]
    ins += [("h", a) for a in (*expand, *shrink)]
    big = pltpu.VMEM((D, FF), BF)
    r = call(
        kernel,
        PARTIAL + [sds((ROWS, FF), F32), wide, wide],
        ins,
        [pltpu.VMEM((ROWS, D), BF), pltpu.VMEM((ROWS, FF), BF), big, big, pltpu.SemaphoreType.DMA((2,))],
        1.1e9,
    )
    return r[:4], r[4], r[5], r[6]


def mlp_out(layer, sec, act, shrink):
    def kernel(sec, act, so, sg, o0, o1, o2, o3, ws, sem):
        fetch(sec, layer, so, sg, ws, sem.at[0]).wait()
        a = act[...]
        for cols in tiles(D):
            put_partial((o0, o1, o2, o3), cols, dot(a, ws[:, cols]))

    return call(
        kernel,
        PARTIAL,
        [("s", sec), ("v", act), ("h", shrink[0]), ("h", shrink[1])],
        [pltpu.VMEM((D, FF), BF), pltpu.SemaphoreType.DMA((1,))],
        5.4e8,
    )


def after_mlp(blocks, hidden, live, vec, vec_next):
    def kernel(a, b, c, d, hidden, live, vec, vec_next, out, first):
        o = (live[...] * (hidden[...] + total((a, b, c, d)) + vec[5:6])).astype(BF)
        out[...] = o
        normed, _ = normalize(o.astype(F32))
        first[...] = (normed * vec_next[0:1] + vec_next[1:2]).astype(BF)

    return call(
        kernel,
        [sds((OWN, D), BF), sds((OWN, D), BF)],
        [("v", a) for a in (*blocks, hidden, live, vec, vec_next)],
        flops=2e6,
    )


def mlp_backward_last(layer, sec, blocks, branch, vec, expand, shrink):
    def kernel(
        sec, b0, b1, b2, b3, branch, vec, eo, eg, so, sg,
        o0, o1, o2, o3, act, hold_l, send_l, hold_r, send_r, bias, second, up_grad, we, ws, sem,
    ):
        get_e = fetch(sec, layer, eo, eg, we, sem.at[0])
        get_s = fetch(sec, layer, so, sg, ws, sem.at[1])
        for k, b in enumerate((b0, b1, b2, b3)):
            second[pl.ds(OWN * k, OWN)] = b[...]
        get_e.wait()
        get_s.wait()
        x = second[...]
        br = branch[...]
        on0 = sec[0] == 0
        for cols in tiles(FF):
            a, g = gelu_pair(dot(x, we[:, cols]) + vec[6:7, cols])
            a = a.astype(BF)
            act[:, cols] = a
            u = (dot_t(br, ws[cols, :]) * g).astype(BF)
            up_grad[:, cols] = u
            bias[:, cols] = jnp.sum(u.astype(F32), axis=0, keepdims=True)
            hold_l[:, cols] = jnp.where(on0, x_tile(second, cols), a)
            send_l[:, cols] = jnp.where(on0, a, x_tile(second, cols))
            hold_r[:, cols] = jnp.where(on0, u, x_tile(branch, cols))
            send_r[:, cols] = jnp.where(on0, x_tile(branch, cols), u)
        u = up_grad[...]
        for cols in tiles(D):
            put_partial((o0, o1, o2, o3), cols, dot_t(u, we[cols, :]))

    wide = sds((ROWS, FF), BF)
    ins = [("s", sec)] + [("v", a) for a in (*blocks, branch, vec)]
    ins += [("h", a) for a in (*expand, *shrink)]
    big = pltpu.VMEM((D, FF), BF)
    r = call(
        kernel,
        PARTIAL + [wide] * 5 + [sds((1, FF), F32)],
        ins,
        [pltpu.VMEM((ROWS, D), BF), pltpu.VMEM((ROWS, FF), BF), big, big, pltpu.SemaphoreType.DMA((2,))],
        1.6e9,
    )
    return r[:4], r[4:]


def x_tile(ref, cols):
    return ref[:, cols]


def mlp_backward(layer, sec, blocks, act_grad, expand, shrink):
    def kernel(
        sec, b0, b1, b2, b3, act_grad, eo, eg, so, sg,
        o0, o1, o2, o3, hold_r, send_r, bias, branch, up_grad, we, ws, sem,
    ):
        get_s = fetch(sec, layer, so, sg, ws, sem.at[1])
        get_e = fetch(sec, layer, eo, eg, we, sem.at[0])
        for k, b in enumerate((b0, b1, b2, b3)):
            branch[pl.ds(OWN * k, OWN)] = b[...]
        get_s.wait()
        br = branch[...]
        on0 = sec[0] == 0
        for cols in tiles(FF):
            u = (dot_t(br, ws[cols, :]) * act_grad[:, cols]).astype(BF)
            up_grad[:, cols] = u
            bias[:, cols] = jnp.sum(u.astype(F32), axis=0, keepdims=True)
            hold_r[:, cols] = jnp.where(on0, u, branch[:, cols])
            send_r[:, cols] = jnp.where(on0, branch[:, cols], u)
        get_e.wait()
        u = up_grad[...]
        for cols in tiles(D):
            put_partial((o0, o1, o2, o3), cols, dot_t(u, we[cols, :]))

    wide = sds((ROWS, FF), BF)
    ins = [("s", sec)] + [("v", a) for a in (*blocks, act_grad)]
    ins += [("h", a) for a in (*expand, *shrink)]
    big = pltpu.VMEM((D, FF), BF)
    r = call(
        kernel,
        PARTIAL + [wide] * 2 + [sds((1, FF), F32)],
        ins,
        [pltpu.VMEM((ROWS, D), BF), pltpu.VMEM((ROWS, FF), BF), big, big, pltpu.SemaphoreType.DMA((2,))],
        1.1e9,
    )
    return r[:4], r[4:]


def after_mlp_backward(blocks, hidden, grad_own, vec):
    def kernel(a, b, c, d, hidden, grad_own, vec, grad_hidden, low, sums):
        gs = total((a, b, c, d))
        pre = grad_own[...].astype(F32)
        normed, inverse = normalize(hidden[...])
        gh = pre + norm_back(normed, inverse, vec[3:4], gs)
        grad_hidden[...] = gh
        lo = gh.astype(BF)
        low[...] = lo
        sums[0:1] = jnp.sum(lo.astype(F32), axis=0, keepdims=True)
        sums[1:2] = jnp.sum(gs * normed, axis=0, keepdims=True)
        sums[2:3] = jnp.sum(gs, axis=0, keepdims=True)
        sums[3:4] = jnp.sum(pre, axis=0, keepdims=True)

    return call(
        kernel,
        [sds((OWN, D), F32), sds((OWN, D), BF), sds((4, D), F32)],
        [("v", a) for a in (*blocks, hidden, grad_own, vec)],
        flops=2e6,
    )


def attn_backward(layer, sec, blocks, keep, qkv, dense):
    def kernel(
        sec, b0, b1, b2, b3, proj, probs, qo, qg, do, dg,
        o0, o1, o2, o3, grads, hold, send, bias, full, wq, wd, sem,
    ):
        get_d = fetch(sec, layer, do, dg, wd, sem.at[1])
        get_q = fetch(sec, layer, qo, qg, wq, sem.at[0])
        for k, b in enumerate((b0, b1, b2, b3)):
            full[pl.ds(OWN * k, OWN)] = b[...]
        on0 = sec[0] == 0
        hold[...] = jnp.where(on0, full[:, :512], full[:, 512:])
        send[...] = jnp.where(on0, full[:, 512:], full[:, :512])
        get_d.wait()
        gc = dot_t(full[...], wd[...]).astype(BF)
        low = lane_low()
        for pair in range(2):
            cols = pl.ds(128 * pair, 128)
            q, k, v = proj[0, :, cols], proj[1, :, cols], proj[2, :, cols]
            g = gc[:, 128 * pair : 128 * pair + 128]
            parts = []
            for h in range(2):
                p = probs[2 * pair + h]
                picked = jnp.where(low if h == 0 else jnp.logical_not(low), g, jnp.zeros_like(g))
                gp = dot_t(picked, v)
                gs = (p * (gp - jnp.sum(p * gp, axis=-1, keepdims=True))).astype(BF)
                parts.append((dot(gs, k) * SCALE, t_dot(gs, q) * SCALE, t_dot(p.astype(BF), g)))
            for c in range(3):
                grads[:, pl.ds(256 * c + 128 * pair, 128)] = jnp.where(
                    low, parts[0][c], parts[1][c]
                ).astype(BF)
        bias[0:1] = jnp.sum(grads[:, 0:256].astype(F32), axis=0, keepdims=True)
        bias[1:2] = jnp.sum(grads[:, 512:768].astype(F32), axis=0, keepdims=True)
        get_q.wait()
        gr = [grads[:, 256 * c : 256 * c + 256] for c in range(3)]
        for cols in tiles(D):
            o = dot_t(gr[0], wq[0, cols]) + dot_t(gr[1], wq[1, cols]) + dot_t(gr[2], wq[2, cols])
            put_partial((o0, o1, o2, o3), cols, o)

    half = sds((ROWS, 512), BF)
    ins = [("s", sec)] + [("v", a) for a in (*blocks, keep["proj"], keep["probs"])]
    ins += [("h", a) for a in (*qkv, *dense)]
    r = call(
        kernel,
        PARTIAL + [sds((ROWS, 768), BF), half, half, sds((2, 256), F32)],
        ins,
        [
            pltpu.VMEM((ROWS, D), BF),
            pltpu.VMEM((3, D, 256), BF),
            pltpu.VMEM((256, D), BF),
            pltpu.SemaphoreType.DMA((2,)),
        ],
        1.2e9,
    )
    return r[:4], r[4:]


def after_attn_backward(blocks, grad_hidden, x_own, live, vec):
    def kernel(a, b, c, d, grad_hidden, x, live, vec, out, pre, sums):
        gf = total((a, b, c, d))
        normed, inverse = normalize(x[...].astype(F32))
        g = (grad_hidden[...] + norm_back(normed, inverse, vec[0:1], gf)).astype(BF)
        out[...] = g
        pre[...] = (live[...] * g.astype(F32)).astype(BF)
        sums[0:1] = jnp.sum(gf * normed, axis=0, keepdims=True)
        sums[1:2] = jnp.sum(gf, axis=0, keepdims=True)

    return call(
        kernel,
        [sds((OWN, D), BF), sds((OWN, D), BF), sds((2, D), F32)],
        [("v", a) for a in (*blocks, grad_hidden, x_own, live, vec)],
        flops=2e6,
    )


def mlp_weight_grad(left, got_left, right, got_right):
    def kernel(l, gl, r, gr, out):
        rv, grv = r[...], gr[...]
        for rows in tiles(D):
            out[rows, :] = (t_dot(l[:, rows], rv) + t_dot(gl[:, rows], grv)).astype(BF)

    return call(
        kernel,
        [sds((D, FF), BF)],
        [("v", a) for a in (left, got_left, right, got_right)],
        flops=1.1e9,
    )[0]


def attn_weight_grad(first, got_first, grads, got_grads, ctx, got_ctx, low, got_low):
    def kernel(f, gf, g, gg, c, gc, d, gd, out):
        for half in range(2):
            rows = slice(256 * half, 256 * half + 256)
            for part in range(3):
                cols = slice(256 * part, 256 * part + 256)
                out[pl.ds(512 * part + 256 * half, 256), :] = (
                    t_dot(f[:, rows], g[:, cols]) + t_dot(gf[:, rows], gg[:, cols])
                ).astype(BF)
            out[pl.ds(1536 + 256 * half, 256), :] = (
                t_dot(c[...], d[:, rows]) + t_dot(gc[...], gd[:, rows])
            ).astype(BF)

    return call(
        kernel,
        [sds((2048, 256), BF)],
        [("v", a) for a in (first, got_first, grads, got_grads, ctx, got_ctx, low, got_low)],
        flops=5.4e8,
    )[0]


def per_device(
    tokens,
    cotangent,
    seq_lengths,
    attn_gain,
    attn_shift,
    attn_weight,
    attn_bias,
    dense_weight,
    dense_bias,
    mlp_gain,
    mlp_shift,
    expand_weight,
    expand_bias,
    shrink_weight,
    shrink_bias,
):
    sec = lax.axis_index("section")
    mp = lax.axis_index("mp")
    on0 = sec == 0

    own_qkv = jnp.transpose(attn_weight[0], (1, 0, 2))
    own_w = [own_qkv, dense_weight[0], expand_weight[0], shrink_weight[0]]
    vectors = jnp.concatenate(
        [attn_gain, attn_shift, dense_bias, mlp_gain, mlp_shift, shrink_bias, expand_bias]
        + [jnp.pad(attn_bias.reshape(1, -1), ((0, 0), (0, 512)))],
        axis=0,
    )
    got_vec = swap(vectors)
    got_w = [swap(w) for w in own_w]

    def pick(layer, own, got):
        return jnp.where(on0, own, got) if layer == 0 else jnp.where(on0, got, own)

    vec0 = pick(0, vectors, got_vec)
    vec1 = pick(1, vectors, got_vec)
    qkv, dense, expand, shrink = [(o, g) for o, g in zip(own_w, got_w)]
    sec_flag = sec.astype(jnp.int32).reshape(1)

    def rel(x):
        x = lax.dynamic_slice_in_dim(x, 2 * sec, 2, 0).reshape(2, 4, 32, -1)
        parts = [lax.dynamic_index_in_dim(x, (mp - k) % 4, 1, keepdims=False) for k in range(4)]
        return jnp.concatenate(parts, axis=0).reshape(256, -1)

    lengths = lax.dynamic_slice_in_dim(seq_lengths, 2 * sec, 2, 0)
    bounds = jnp.cumsum(lengths, axis=1)
    pos = (32 * ((mp - jnp.arange(4)) % 4)[:, None] + jnp.arange(32)[None]).reshape(128)
    segment = jnp.sum((pos[None, :, None] >= bounds[:, None, :]).astype(jnp.int32), axis=2)
    segment = segment + jnp.array([0, 8], jnp.int32)[:, None]

    def spread(x):
        return jnp.broadcast_to(x, (2, 128)).reshape(2, 4, 32).transpose(1, 0, 2).reshape(256)

    seg_rows, pos_rows = spread(segment), spread(pos[None])
    allowed = (seg_rows[:, None] == seg_rows[None, :]) & (pos_rows[None, :] <= pos_rows[:, None])
    dist = jnp.where(allowed, (pos_rows[:, None] - pos_rows[None, :]).astype(F32), 1e33)
    live = (pos[None] < bounds[:, -1:]).astype(F32)
    live_rows = live.reshape(2, 4, 32).transpose(1, 0, 2).reshape(256, 1)
    live_own = live_rows[:64]
    heads_local = attn_weight.shape[3] // HEAD
    head_ids = mp * heads_local + jnp.arange(heads_local)
    slopes = jnp.exp2(-8.0 * (head_ids + 1).astype(F32) / HEADS)

    x_all = rel(tokens)
    x_own0 = x_all[:OWN]
    branch1 = rel(cotangent) * live_rows.astype(BF)

    partial, keep0 = attn_forward(0, sec_flag, slopes, [x_all], vec0, dist, qkv, dense)
    hidden0, second = after_attn(scatter_rows(partial), x_own0, vec0)
    got_f0, got_c0 = swap(keep0["send_f"]), swap(keep0["context"])
    partial, act_grad0, hold_l0, send_l0 = mlp_forward(
        0, sec_flag, gather_rows(second), vec0, expand, shrink
    )
    got_l0 = swap(send_l0)
    out0, first = after_mlp(scatter_rows(partial), hidden0, live_own, vec0, vec1)
    partial, keep1 = attn_forward(
        1, sec_flag, slopes, gather_rows(first), vec1, dist, qkv, dense
    )
    got_f1, got_c1 = swap(keep1["send_f"]), swap(keep1["context"])
    hidden1, second = after_attn(scatter_rows(partial), out0, vec1)
    pre1 = branch1[:OWN]
    partial, (act1, hold_l1, send_l1, hold_r1, send_r1, ebias1) = mlp_backward_last(
        1, sec_flag, gather_rows(second), branch1, vec1, expand, shrink
    )
    got_l1, got_r1 = swap(send_l1), swap(send_r1)
    grad_hidden, low1, sums_f1 = after_mlp_backward(scatter_rows(partial), hidden1, pre1, vec1)
    mlp1 = mlp_weight_grad(hold_l1, got_l1, hold_r1, got_r1)
    partial, (grads1, hold_d1, send_d1, abias1) = attn_backward(
        1, sec_flag, gather_rows(low1), keep1, qkv, dense
    )
    got_g1, got_d1 = swap(grads1), swap(send_d1)
    g1, pre0, sums_i1 = after_attn_backward(
        scatter_rows(partial), grad_hidden, out0, live_own, vec1
    )
    attn1 = attn_weight_grad(
        keep1["hold_f"], got_f1, grads1, got_g1, keep1["context"], got_c1, hold_d1, got_d1
    )
    branch0 = gather_rows(pre0)
    branch0, mlp1, attn1 = lax.optimization_barrier((branch0, mlp1, attn1))
    mlp1, attn1 = dp_total_far(mlp1), dp_total_far(attn1)
    partial, (hold_r0, send_r0, ebias0) = mlp_backward(
        0, sec_flag, branch0, act_grad0, expand, shrink
    )
    got_r0 = swap(send_r0)
    grad_hidden, low0, sums_f0 = after_mlp_backward(scatter_rows(partial), hidden0, pre0, vec0)
    mlp0 = mlp_weight_grad(hold_l0, got_l0, hold_r0, got_r0)
    low_blocks = gather_rows(low0)
    partial, (grads0, hold_d0, send_d0, abias0) = attn_backward(
        0, sec_flag, low_blocks, keep0, qkv, dense
    )
    got_g0, got_d0 = swap(grads0), swap(send_d0)
    g0, _, sums_i0 = after_attn_backward(
        scatter_rows(partial), grad_hidden, x_own0, live_own, vec0
    )
    attn0 = attn_weight_grad(
        keep0["hold_f"], got_f0, grads0, got_g0, keep0["context"], got_c0, hold_d0, got_d0
    )
    partial = mlp_out(1, sec_flag, act1, shrink)
    out1, _ = after_mlp(scatter_rows(partial), hidden1, live_own, vec1, vec1)

    mlp0 = dp_total(mlp0)
    attn0 = dp_total(attn0)

    def small_rows(sums_i, sums_f, ebias, abias):
        last = jnp.pad(abias.reshape(1, 512), ((0, 0), (0, 512)))
        return jnp.concatenate([sums_i, sums_f, ebias, last], axis=0)

    small0 = small_rows(sums_i0, sums_f0, ebias0, abias0)
    small1 = small_rows(sums_i1, sums_f1, ebias1, abias1)
    small = jnp.where(on0, small0, small1) + swap(jnp.where(on0, small1, small0))
    small = small_total(small)

    def both_halves(held0, held1):
        mine = jnp.where(on0, held0, held1)
        other = swap(jnp.where(on0, held1, held0))
        return jnp.where(on0, mine, other).astype(F32), jnp.where(on0, other, mine).astype(F32)

    expand_grad, shrink_grad = both_halves(mlp0, mlp1)
    lower, upper = both_halves(attn0, attn1)
    qkv_grad = jnp.concatenate(
        [lower[:1536].reshape(3, 512, 256), upper[:1536].reshape(3, 512, 256)], axis=1
    )
    dense_grad = jnp.concatenate(
        [lower[1536:1792], lower[1792:], upper[1536:1792], upper[1792:]], axis=1
    )

    def all_slots(held0, held1):
        mine = jnp.where(on0, held0, held1).reshape(2, 32, -1)
        other = swap(jnp.where(on0, held1, held0)).reshape(2, 32, -1)
        return jnp.concatenate(
            [jnp.where(on0, mine, other), jnp.where(on0, other, mine)], axis=0
        )

    layer_out = all_slots(out0, out1)
    input_grad = all_slots(g0, g1)
    return (
        layer_out[None],
        input_grad[None],
        small[0:1],
        small[1:2],
        jnp.transpose(qkv_grad, (1, 0, 2))[None],
        small[7, :512].reshape(1, 2, 256),
        dense_grad[None],
        small[2:3],
        small[3:4],
        small[4:5],
        expand_grad[None],
        small[6:7],
        shrink_grad[None],
        small[5:6],
    )


def solution(mesh):
    return jax.shard_map(
        per_device,
        mesh=mesh,
        in_specs=(
            P("dp", None, None),
            P("dp", None, None),
            P("dp", None),
            P("section", None),
            P("section", None),
            P("section", None, None, "mp"),
            P("section", None, "mp"),
            P("section", "mp", None),
            P("section", None),
            P("section", None),
            P("section", None),
            P("section", None, "mp"),
            P("section", "mp"),
            P("section", "mp", None),
            P("section", None),
        ),
        out_specs=(
            P("section", "dp", "mp", None),
            P("section", "dp", "mp", None),
            P("section", None),
            P("section", None),
            P("section", None, None, "mp"),
            P("section", None, "mp"),
            P("section", "mp", None),
            P("section", None),
            P("section", None),
            P("section", None),
            P("section", None, "mp"),
            P("section", "mp"),
            P("section", "mp", None),
            P("section", None),
        ),
        check_vma=False,
    )
```

```python
import jax
import jax.numpy as jnp
from jax import lax
from jax.experimental import pallas as pl
from jax.experimental.pallas import tpu as pltpu
from jax.sharding import PartitionSpec as P

HEADS = 16
HEAD = 64
EPS = 1e-05
BF = jnp.bfloat16
F32 = jnp.float32


def dot(a, b):
    return jnp.dot(a, b, preferred_element_type=F32)


def dot_t(a, b):
    return lax.dot_general(a, b, (((1,), (1,)), ((), ())), preferred_element_type=F32)


def t_dot(a, b):
    return lax.dot_general(a, b, (((0,), (0,)), ((), ())), preferred_element_type=F32)


def normalize(h):
    center = h - jnp.mean(h, axis=-1, keepdims=True)
    inverse = lax.rsqrt(jnp.mean(center * center, axis=-1, keepdims=True) + EPS)
    return center * inverse, inverse


def norm_back(normed, inverse, gain, grad):
    z = grad * gain
    return inverse * (
        z
        - jnp.mean(z, axis=-1, keepdims=True)
        - normed * jnp.mean(z * normed, axis=-1, keepdims=True)
    )


def ring(axis, steps):
    n = lax.axis_size(axis)
    return [(i, (i + steps) % n) for i in range(n)]


def swap(x):
    return lax.ppermute(x, "section", [(0, 1), (1, 0)])


FLOPS_FAR = 2e11


def dp_total_far(x):
    return lax.psum(x, "dp")


def gather_rows(own):
    return [own] + [lax.ppermute(own, "mp", ring("mp", k)) for k in (1, 2, 3)]


def scatter_rows(blocks):
    return [blocks[0]] + [lax.ppermute(blocks[k], "mp", ring("mp", -k)) for k in (1, 2, 3)]


GELU_C = 0.7978845608
GELU_A = 0.044715
ROWS = 256
OWN = 64
D = 1024
FF = 1024
TILE = 256
SCALE = HEAD**-0.5


def gelu_pair(u):
    t = jnp.tanh(GELU_C * (u + GELU_A * u * u * u))
    act = 0.5 * u * (1 + t)
    grad = 0.5 * (1 + t) + 0.5 * u * (1 - t * t) * (GELU_C * (1 + 3 * GELU_A * u * u))
    return act, grad


def sds(shape, dtype):
    return jax.ShapeDtypeStruct(shape, dtype)


PARTIAL = [sds((OWN, D), F32)] + [sds((OWN, D), BF)] * 3
VM = pl.BlockSpec(memory_space=pltpu.VMEM)
SM = pl.BlockSpec(memory_space=pltpu.SMEM)
HB = pl.BlockSpec(memory_space=pltpu.HBM)


def call(kernel, outs, ins, scratch=(), flops=1e9, limit=52):
    specs = [HB if kind == "h" else SM if kind == "s" else VM for kind, _ in ins]
    arrays = [a for _, a in ins]
    size = sum(a.size * a.dtype.itemsize for a in arrays) + sum(
        o.size * o.dtype.itemsize for o in outs
    )
    return pl.pallas_call(
        kernel,
        out_shape=list(outs),
        in_specs=specs,
        out_specs=[VM] * len(outs),
        scratch_shapes=list(scratch),
        compiler_params=pltpu.CompilerParams(vmem_limit_bytes=limit * 2**20),
        cost_estimate=pl.CostEstimate(
            flops=int(flops), bytes_accessed=int(size), transcendentals=0
        ),
    )(*arrays)


def fetch(sec, layer, own, got, dst, sem):
    mine = sec[0] == layer

    @pl.when(mine)
    def _():
        pltpu.make_async_copy(own, dst, sem).start()

    @pl.when(jnp.logical_not(mine))
    def _():
        pltpu.make_async_copy(got, dst, sem).start()

    return pltpu.make_async_copy(own, dst, sem)


def put_partial(outs, cols, value):
    outs[0][:, cols] = value[:OWN]
    for k in (1, 2, 3):
        outs[k][:, cols] = value[OWN * k : OWN * (k + 1)].astype(BF)


def tiles(width):
    return [pl.ds(i * TILE, TILE) for i in range(width // TILE)]


def lane_low():
    return lax.broadcasted_iota(jnp.int32, (ROWS, 128), 1) < HEAD


def attn_forward(layer, sec, slopes, source, vec, dist, qkv, dense):
    def kernel(*refs):
        n = len(source)
        sec, slopes, src = refs[0], refs[1], refs[2 : 2 + n]
        vec, dist, qo, qg, do, dg = refs[2 + n : 8 + n]
        o0, o1, o2, o3, proj, probs, context, hold, send = refs[8 + n : 17 + n]
        first, wq, wd, sem = refs[17 + n :]
        get_q = fetch(sec, layer, qo, qg, wq, sem.at[0])
        get_d = fetch(sec, layer, do, dg, wd, sem.at[1])
        if n == 1:
            normed, _ = normalize(src[0][...].astype(F32))
            first[...] = (normed * vec[0:1] + vec[1:2]).astype(BF)
        else:
            for k in range(4):
                first[pl.ds(OWN * k, OWN)] = src[k][...]
        on0 = sec[0] == 0
        hold[...] = jnp.where(on0, first[:, :512], first[:, 512:])
        send[...] = jnp.where(on0, first[:, 512:], first[:, :512])
        get_q.wait()
        f = first[...]
        proj[0] = (dot(f, wq[0]) + vec[7:8, 0:256]).astype(BF)
        proj[1] = dot(f, wq[1]).astype(BF)
        proj[2] = (dot(f, wq[2]) + vec[7:8, 256:512]).astype(BF)
        low = lane_low()
        for pair in range(2):
            cols = pl.ds(128 * pair, 128)
            q, k, v = proj[0, :, cols], proj[1, :, cols], proj[2, :, cols]
            ctx = []
            for h in range(2):
                picked = jnp.where(low if h == 0 else jnp.logical_not(low), q, jnp.zeros_like(q))
                s = dot_t(picked, k) * SCALE - slopes[2 * pair + h] * dist[...]
                e = jnp.exp(s - jnp.max(s, axis=-1, keepdims=True))
                p = e / jnp.sum(e, axis=-1, keepdims=True)
                p = p.astype(BF)
                probs[2 * pair + h] = p
                ctx.append(dot(p, v))
            context[:, cols] = jnp.where(low, ctx[0], ctx[1]).astype(BF)
        get_d.wait()
        c = context[...]
        for cols in tiles(D):
            put_partial((o0, o1, o2, o3), cols, dot(c, wd[:, cols]))

    outs = PARTIAL + [
        sds((3, ROWS, 256), BF),
        sds((4, ROWS, ROWS), BF),
        sds((ROWS, 256), BF),
        sds((ROWS, 512), BF),
        sds((ROWS, 512), BF),
    ]
    ins = [("s", sec), ("s", slopes)] + [("v", a) for a in source]
    ins += [("v", vec), ("v", dist), ("h", qkv[0]), ("h", qkv[1]), ("h", dense[0]), ("h", dense[1])]
    scratch = [
        pltpu.VMEM((ROWS, D), BF),
        pltpu.VMEM((3, D, 256), BF),
        pltpu.VMEM((256, D), BF),
        pltpu.SemaphoreType.DMA((2,)),
    ]
    r = call(kernel, outs, ins, scratch, 8e8)
    return r[:4], dict(proj=r[4], probs=r[5], context=r[6], hold_f=r[7], send_f=r[8])


def total(refs):
    return refs[0][...] + refs[1][...].astype(F32) + refs[2][...].astype(F32) + refs[3][...].astype(F32)


def after_attn(blocks, x_own, vec):
    def kernel(a, b, c, d, x, vec, hidden, second):
        h = x[...].astype(F32) + total((a, b, c, d)) + vec[2:3]
        hidden[...] = h
        normed, _ = normalize(h)
        second[...] = (normed * vec[3:4] + vec[4:5]).astype(BF)

    return call(
        kernel,
        [sds((OWN, D), F32), sds((OWN, D), BF)],
        [("v", a) for a in (*blocks, x_own, vec)],
        flops=2e6,
    )


def mlp_forward(layer, sec, blocks, vec, expand, shrink):
    def kernel(sec, b0, b1, b2, b3, vec, eo, eg, so, sg, o0, o1, o2, o3, act_grad, hold, send, second, act, we, ws, sem):
        get_e = fetch(sec, layer, eo, eg, we, sem.at[0])
        get_s = fetch(sec, layer, so, sg, ws, sem.at[1])
        for k, b in enumerate((b0, b1, b2, b3)):
            second[pl.ds(OWN * k, OWN)] = b[...]
        get_e.wait()
        x = second[...]
        for cols in tiles(FF):
            a, g = gelu_pair(dot(x, we[:, cols]) + vec[6:7, cols])
            act[:, cols] = a.astype(BF)
            act_grad[:, cols] = g.astype(BF)
        get_s.wait()
        a = act[...]
        on0 = sec[0] == 0
        for cols in tiles(D):
            put_partial((o0, o1, o2, o3), cols, dot(a, ws[:, cols]))
            hold[:, cols] = jnp.where(on0, second[:, cols], act[:, cols])
            send[:, cols] = jnp.where(on0, act[:, cols], second[:, cols])

    wide = sds((ROWS, FF), BF)
    ins = [("s", sec)] + [("v", a) for a in (*blocks, vec)]
    ins += [("h", a) for a in (*expand, *shrink)]
    big = pltpu.VMEM((D, FF), BF)
    r = call(
        kernel,
        PARTIAL + [wide, wide, wide],
        ins,
        [pltpu.VMEM((ROWS, D), BF), pltpu.VMEM((ROWS, FF), BF), big, big, pltpu.SemaphoreType.DMA((2,))],
        1.1e9,
    )
    return r[:4], r[4], r[5], r[6]


def mlp_out(layer, sec, act, shrink):
    def kernel(sec, act, so, sg, o0, o1, o2, o3, ws, sem):
        fetch(sec, layer, so, sg, ws, sem.at[0]).wait()
        a = act[...]
        for cols in tiles(D):
            put_partial((o0, o1, o2, o3), cols, dot(a, ws[:, cols]))

    return call(
        kernel,
        PARTIAL,
        [("s", sec), ("v", act), ("h", shrink[0]), ("h", shrink[1])],
        [pltpu.VMEM((D, FF), BF), pltpu.SemaphoreType.DMA((1,))],
        5.4e8,
    )


def after_mlp(blocks, hidden, live, vec, vec_next):
    def kernel(a, b, c, d, hidden, live, vec, vec_next, out, first):
        o = (live[...] * (hidden[...] + total((a, b, c, d)) + vec[5:6])).astype(BF)
        out[...] = o
        normed, _ = normalize(o.astype(F32))
        first[...] = (normed * vec_next[0:1] + vec_next[1:2]).astype(BF)

    return call(
        kernel,
        [sds((OWN, D), BF), sds((OWN, D), BF)],
        [("v", a) for a in (*blocks, hidden, live, vec, vec_next)],
        flops=2e6,
    )


def mlp_backward_last(layer, sec, blocks, branch, vec, expand, shrink):
    def kernel(
        sec, b0, b1, b2, b3, branch, vec, eo, eg, so, sg,
        o0, o1, o2, o3, act, hold_l, send_l, hold_r, send_r, bias, second, up_grad, we, ws, sem,
    ):
        get_e = fetch(sec, layer, eo, eg, we, sem.at[0])
        get_s = fetch(sec, layer, so, sg, ws, sem.at[1])
        for k, b in enumerate((b0, b1, b2, b3)):
            second[pl.ds(OWN * k, OWN)] = b[...]
        get_e.wait()
        get_s.wait()
        x = second[...]
        br = branch[...]
        on0 = sec[0] == 0
        for cols in tiles(FF):
            a, g = gelu_pair(dot(x, we[:, cols]) + vec[6:7, cols])
            a = a.astype(BF)
            act[:, cols] = a
            u = (dot_t(br, ws[cols, :]) * g).astype(BF)
            up_grad[:, cols] = u
            bias[:, cols] = jnp.sum(u.astype(F32), axis=0, keepdims=True)
            hold_l[:, cols] = jnp.where(on0, x_tile(second, cols), a)
            send_l[:, cols] = jnp.where(on0, a, x_tile(second, cols))
            hold_r[:, cols] = jnp.where(on0, u, x_tile(branch, cols))
            send_r[:, cols] = jnp.where(on0, x_tile(branch, cols), u)
        u = up_grad[...]
        for cols in tiles(D):
            put_partial((o0, o1, o2, o3), cols, dot_t(u, we[cols, :]))

    wide = sds((ROWS, FF), BF)
    ins = [("s", sec)] + [("v", a) for a in (*blocks, branch, vec)]
    ins += [("h", a) for a in (*expand, *shrink)]
    big = pltpu.VMEM((D, FF), BF)
    r = call(
        kernel,
        PARTIAL + [wide] * 5 + [sds((1, FF), F32)],
        ins,
        [pltpu.VMEM((ROWS, D), BF), pltpu.VMEM((ROWS, FF), BF), big, big, pltpu.SemaphoreType.DMA((2,))],
        1.6e9,
    )
    return r[:4], r[4:]


def x_tile(ref, cols):
    return ref[:, cols]


def mlp_backward(layer, sec, blocks, act_grad, expand, shrink):
    def kernel(
        sec, b0, b1, b2, b3, act_grad, eo, eg, so, sg,
        o0, o1, o2, o3, hold_r, send_r, bias, branch, up_grad, we, ws, sem,
    ):
        get_s = fetch(sec, layer, so, sg, ws, sem.at[1])
        get_e = fetch(sec, layer, eo, eg, we, sem.at[0])
        for k, b in enumerate((b0, b1, b2, b3)):
            branch[pl.ds(OWN * k, OWN)] = b[...]
        get_s.wait()
        br = branch[...]
        on0 = sec[0] == 0
        for cols in tiles(FF):
            u = (dot_t(br, ws[cols, :]) * act_grad[:, cols].astype(F32)).astype(BF)
            up_grad[:, cols] = u
            bias[:, cols] = jnp.sum(u.astype(F32), axis=0, keepdims=True)
            hold_r[:, cols] = jnp.where(on0, u, branch[:, cols])
            send_r[:, cols] = jnp.where(on0, branch[:, cols], u)
        get_e.wait()
        u = up_grad[...]
        for cols in tiles(D):
            put_partial((o0, o1, o2, o3), cols, dot_t(u, we[cols, :]))

    wide = sds((ROWS, FF), BF)
    ins = [("s", sec)] + [("v", a) for a in (*blocks, act_grad)]
    ins += [("h", a) for a in (*expand, *shrink)]
    big = pltpu.VMEM((D, FF), BF)
    r = call(
        kernel,
        PARTIAL + [wide] * 2 + [sds((1, FF), F32)],
        ins,
        [pltpu.VMEM((ROWS, D), BF), pltpu.VMEM((ROWS, FF), BF), big, big, pltpu.SemaphoreType.DMA((2,))],
        1.1e9,
    )
    return r[:4], r[4:]


def after_mlp_backward(blocks, hidden, grad_own, vec):
    def kernel(a, b, c, d, hidden, grad_own, vec, grad_hidden, low, sums):
        gs = total((a, b, c, d))
        pre = grad_own[...].astype(F32)
        normed, inverse = normalize(hidden[...])
        gh = pre + norm_back(normed, inverse, vec[3:4], gs)
        grad_hidden[...] = gh
        lo = gh.astype(BF)
        low[...] = lo
        sums[0:1] = jnp.sum(lo.astype(F32), axis=0, keepdims=True)
        sums[1:2] = jnp.sum(gs * normed, axis=0, keepdims=True)
        sums[2:3] = jnp.sum(gs, axis=0, keepdims=True)
        sums[3:4] = jnp.sum(pre, axis=0, keepdims=True)

    return call(
        kernel,
        [sds((OWN, D), F32), sds((OWN, D), BF), sds((4, D), F32)],
        [("v", a) for a in (*blocks, hidden, grad_own, vec)],
        flops=2e6,
    )


def attn_backward(layer, sec, blocks, keep, qkv, dense):
    def kernel(
        sec, b0, b1, b2, b3, proj, probs, qo, qg, do, dg,
        o0, o1, o2, o3, grads, hold, send, bias, full, wq, wd, sem,
    ):
        get_d = fetch(sec, layer, do, dg, wd, sem.at[1])
        get_q = fetch(sec, layer, qo, qg, wq, sem.at[0])
        for k, b in enumerate((b0, b1, b2, b3)):
            full[pl.ds(OWN * k, OWN)] = b[...]
        on0 = sec[0] == 0
        hold[...] = jnp.where(on0, full[:, :512], full[:, 512:])
        send[...] = jnp.where(on0, full[:, 512:], full[:, :512])
        get_d.wait()
        gc = dot_t(full[...], wd[...]).astype(BF)
        low = lane_low()
        for pair in range(2):
            cols = pl.ds(128 * pair, 128)
            q, k, v = proj[0, :, cols], proj[1, :, cols], proj[2, :, cols]
            g = gc[:, 128 * pair : 128 * pair + 128]
            parts = []
            for h in range(2):
                p_low = probs[2 * pair + h]
                p = p_low.astype(F32)
                picked = jnp.where(low if h == 0 else jnp.logical_not(low), g, jnp.zeros_like(g))
                gp = dot_t(picked, v)
                gs = (p * (gp - jnp.sum(p * gp, axis=-1, keepdims=True))).astype(BF)
                parts.append((dot(gs, k) * SCALE, t_dot(gs, q) * SCALE, t_dot(p_low, g)))
            for c in range(3):
                grads[:, pl.ds(256 * c + 128 * pair, 128)] = jnp.where(
                    low, parts[0][c], parts[1][c]
                ).astype(BF)
        bias[0:1] = jnp.sum(grads[:, 0:256].astype(F32), axis=0, keepdims=True)
        bias[1:2] = jnp.sum(grads[:, 512:768].astype(F32), axis=0, keepdims=True)
        get_q.wait()
        gr = [grads[:, 256 * c : 256 * c + 256] for c in range(3)]
        for cols in tiles(D):
            o = dot_t(gr[0], wq[0, cols]) + dot_t(gr[1], wq[1, cols]) + dot_t(gr[2], wq[2, cols])
            put_partial((o0, o1, o2, o3), cols, o)

    half = sds((ROWS, 512), BF)
    ins = [("s", sec)] + [("v", a) for a in (*blocks, keep["proj"], keep["probs"])]
    ins += [("h", a) for a in (*qkv, *dense)]
    r = call(
        kernel,
        PARTIAL + [sds((ROWS, 768), BF), half, half, sds((2, 256), F32)],
        ins,
        [
            pltpu.VMEM((ROWS, D), BF),
            pltpu.VMEM((3, D, 256), BF),
            pltpu.VMEM((256, D), BF),
            pltpu.SemaphoreType.DMA((2,)),
        ],
        1.2e9,
    )
    return r[:4], r[4:]


def after_attn_backward(blocks, grad_hidden, x_own, live, vec):
    def kernel(a, b, c, d, grad_hidden, x, live, vec, out, pre, sums):
        gf = total((a, b, c, d))
        normed, inverse = normalize(x[...].astype(F32))
        g = (grad_hidden[...] + norm_back(normed, inverse, vec[0:1], gf)).astype(BF)
        out[...] = g
        pre[...] = (live[...] * g.astype(F32)).astype(BF)
        sums[0:1] = jnp.sum(gf * normed, axis=0, keepdims=True)
        sums[1:2] = jnp.sum(gf, axis=0, keepdims=True)

    return call(
        kernel,
        [sds((OWN, D), BF), sds((OWN, D), BF), sds((2, D), F32)],
        [("v", a) for a in (*blocks, grad_hidden, x_own, live, vec)],
        flops=2e6,
    )


def mlp_weight_grad(left, got_left, right, got_right):
    def kernel(l, gl, r, gr, out):
        rv, grv = r[...], gr[...]
        for t in range(4):
            rows = pl.ds(t * TILE, TILE)
            g = (t_dot(l[:, rows], rv) + t_dot(gl[:, rows], grv)).astype(BF)
            for i in range(4):
                for c in range(4):
                    out[4 * t + i, pl.ds(64 * c, 64), :] = g[
                        64 * i : 64 * i + 64, 256 * c : 256 * c + 256
                    ]

    return call(
        kernel,
        [sds((16, 256, 256), BF)],
        [("v", a) for a in (left, got_left, right, got_right)],
        flops=1.1e9,
    )[0]


def attn_weight_grad(first, got_first, grads, got_grads, ctx, got_ctx, low, got_low):
    def kernel(f, gf, g, gg, c, gc, d, gd, out):
        def put(at, value):
            value = value.astype(BF)
            out[at // 128] = value[:128]
            out[at // 128 + 1] = value[128:]

        for half in range(2):
            rows = slice(256 * half, 256 * half + 256)
            for part in range(3):
                cols = slice(256 * part, 256 * part + 256)
                put(
                    512 * part + 256 * half,
                    t_dot(f[:, rows], g[:, cols]) + t_dot(gf[:, rows], gg[:, cols]),
                )
            put(1536 + 256 * half, t_dot(c[...], d[:, rows]) + t_dot(gc[...], gd[:, rows]))

    return call(
        kernel,
        [sds((16, 128, 256), BF)],
        [("v", a) for a in (first, got_first, grads, got_grads, ctx, got_ctx, low, got_low)],
        flops=5.4e8,
    )[0]


JOINT = 400


def attn_weight_grad_joint(parts, mlp, small):
    def kernel(f, gf, g, gg, c, gc, d, gd, sm, mlp, out):
        out[:, pl.ds(0, 256)] = mlp[...]
        out[:, pl.ds(384, 16)] = sm[...]

        def put(at, value):
            value = value.astype(BF)
            out[at // 128, pl.ds(256, 128)] = value[:128]
            out[at // 128 + 1, pl.ds(256, 128)] = value[128:]

        for half in range(2):
            rows = slice(256 * half, 256 * half + 256)
            for part in range(3):
                cols = slice(256 * part, 256 * part + 256)
                put(
                    512 * part + 256 * half,
                    t_dot(f[:, rows], g[:, cols]) + t_dot(gf[:, rows], gg[:, cols]),
                )
            put(1536 + 256 * half, t_dot(c[...], d[:, rows]) + t_dot(gc[...], gd[:, rows]))

    return call(
        kernel,
        [sds((16, JOINT, 256), BF)],
        [("v", a) for a in (*parts, small, mlp)],
        flops=5.4e8,
    )[0]


def spread_sums(got):
    def kernel(m, out):
        share = jnp.sum(m[...].astype(F32), axis=0).astype(BF)
        for i in range(16):
            out[i] = share

    return call(kernel, [sds((16, JOINT, 256), BF)], [("v", got)], flops=1e6)[0]


WIDE_OUT = [sds((D, FF), F32), sds((D, FF), F32), sds((3, D, 256), F32), sds((256, D), F32)]


def write_out(layer, sec, far, grads, held, flops):
    n = len(grads)

    def kernel(sec, *refs):
        src = refs[:n]
        outs = refs[n + len(held) : n + len(held) + 4]
        wide, tall, sem = refs[n + len(held) + 4 :]

        @pl.when(sec[0] == layer)
        def _():
            which = (1 - layer) if far else layer
            target = outs[which]
            copies = []
            for i in range(16):
                for c in range(4):
                    wide[pl.ds(64 * i, 64), pl.ds(256 * c, 256)] = src[0][
                        i, pl.ds(64 * c, 64), :
                    ].astype(F32)
                tail = src[0][i, 256:384, :] if n == 1 else src[1][i]
                tall[pl.ds(128 * i, 128)] = tail.astype(F32)
                if i % 4 == 3:
                    rows = pl.ds(256 * (i // 4), 256)
                    copies.append(
                        pltpu.make_async_copy(wide.at[rows], target.at[rows], sem.at[i // 4])
                    )
                    copies[-1].start()
            for p in range(3):
                copies.append(
                    pltpu.make_async_copy(
                        tall.at[pl.ds(512 * p, 512)],
                        outs[2].at[p, pl.ds(512 * which, 512)],
                        sem.at[4 + p],
                    )
                )
                copies[-1].start()
            for h in range(2):
                copies.append(
                    pltpu.make_async_copy(
                        tall.at[pl.ds(1536 + 256 * h, 256)],
                        outs[3].at[:, pl.ds(512 * which + 256 * h, 256)],
                        sem.at[7 + h],
                    )
                )
                copies[-1].start()
            for c in copies:
                c.wait()

    return pl.pallas_call(
        kernel,
        out_shape=WIDE_OUT,
        in_specs=[SM] + [VM] * n + [HB] * len(held),
        out_specs=[HB] * 4,
        scratch_shapes=[
            pltpu.VMEM((D, FF), F32),
            pltpu.VMEM((2048, 256), F32),
            pltpu.SemaphoreType.DMA((9,)),
        ],
        input_output_aliases={1 + n + i: i for i in range(len(held))},
        compiler_params=pltpu.CompilerParams(vmem_limit_bytes=52 * 2**20),
        cost_estimate=pl.CostEstimate(flops=int(flops), bytes_accessed=9000000, transcendentals=0),
    )(sec, *grads, *held)


def per_device(
    tokens,
    cotangent,
    seq_lengths,
    attn_gain,
    attn_shift,
    attn_weight,
    attn_bias,
    dense_weight,
    dense_bias,
    mlp_gain,
    mlp_shift,
    expand_weight,
    expand_bias,
    shrink_weight,
    shrink_bias,
):
    sec = lax.axis_index("section")
    mp = lax.axis_index("mp")
    on0 = sec == 0

    own_qkv = jnp.transpose(attn_weight[0], (1, 0, 2))
    own_w = [own_qkv, dense_weight[0], expand_weight[0], shrink_weight[0]]
    vectors = jnp.concatenate(
        [attn_gain, attn_shift, dense_bias, mlp_gain, mlp_shift, shrink_bias, expand_bias]
        + [jnp.pad(attn_bias.reshape(1, -1), ((0, 0), (0, 512)))],
        axis=0,
    )
    got_vec = swap(vectors)
    got_w = [swap(w) for w in own_w]

    def pick(layer, own, got):
        return jnp.where(on0, own, got) if layer == 0 else jnp.where(on0, got, own)

    vec0 = pick(0, vectors, got_vec)
    vec1 = pick(1, vectors, got_vec)
    qkv, dense, expand, shrink = [(o, g) for o, g in zip(own_w, got_w)]
    sec_flag = sec.astype(jnp.int32).reshape(1)

    def rel(x):
        x = lax.dynamic_slice_in_dim(x, 2 * sec, 2, 0).reshape(2, 4, 32, -1)
        parts = [lax.dynamic_index_in_dim(x, (mp - k) % 4, 1, keepdims=False) for k in range(4)]
        return jnp.concatenate(parts, axis=0).reshape(256, -1)

    lengths = lax.dynamic_slice_in_dim(seq_lengths, 2 * sec, 2, 0)
    bounds = jnp.cumsum(lengths, axis=1)
    pos = (32 * ((mp - jnp.arange(4)) % 4)[:, None] + jnp.arange(32)[None]).reshape(128)
    segment = jnp.sum((pos[None, :, None] >= bounds[:, None, :]).astype(jnp.int32), axis=2)
    segment = segment + jnp.array([0, 8], jnp.int32)[:, None]

    def spread(x):
        return jnp.broadcast_to(x, (2, 128)).reshape(2, 4, 32).transpose(1, 0, 2).reshape(256)

    seg_rows, pos_rows = spread(segment), spread(pos[None])
    allowed = (seg_rows[:, None] == seg_rows[None, :]) & (pos_rows[None, :] <= pos_rows[:, None])
    dist = jnp.where(allowed, (pos_rows[:, None] - pos_rows[None, :]).astype(F32), 1e33)
    live = (pos[None] < bounds[:, -1:]).astype(F32)
    live_rows = live.reshape(2, 4, 32).transpose(1, 0, 2).reshape(256, 1)
    live_own = live_rows[:64]
    heads_local = attn_weight.shape[3] // HEAD
    head_ids = mp * heads_local + jnp.arange(heads_local)
    slopes = jnp.exp2(-8.0 * (head_ids + 1).astype(F32) / HEADS)

    x_all = rel(tokens)
    x_own0 = x_all[:OWN]
    branch1 = rel(cotangent) * live_rows.astype(BF)

    partial, keep0 = attn_forward(0, sec_flag, slopes, [x_all], vec0, dist, qkv, dense)
    hidden0, second = after_attn(scatter_rows(partial), x_own0, vec0)
    got_f0, got_c0 = swap(keep0["send_f"]), swap(keep0["context"])
    partial, act_grad0, hold_l0, send_l0 = mlp_forward(
        0, sec_flag, gather_rows(second), vec0, expand, shrink
    )
    got_l0 = swap(send_l0)
    out0, first = after_mlp(scatter_rows(partial), hidden0, live_own, vec0, vec1)
    partial, keep1 = attn_forward(
        1, sec_flag, slopes, gather_rows(first), vec1, dist, qkv, dense
    )
    got_f1, got_c1 = swap(keep1["send_f"]), swap(keep1["context"])
    hidden1, second = after_attn(scatter_rows(partial), out0, vec1)
    pre1 = branch1[:OWN]
    partial, (act1, hold_l1, send_l1, hold_r1, send_r1, ebias1) = mlp_backward_last(
        1, sec_flag, gather_rows(second), branch1, vec1, expand, shrink
    )
    got_l1, got_r1 = swap(send_l1), swap(send_r1)
    grad_hidden, low1, sums_f1 = after_mlp_backward(scatter_rows(partial), hidden1, pre1, vec1)
    mlp1 = mlp_weight_grad(hold_l1, got_l1, hold_r1, got_r1)
    partial, (grads1, hold_d1, send_d1, abias1) = attn_backward(
        1, sec_flag, gather_rows(low1), keep1, qkv, dense
    )
    got_g1, got_d1 = swap(grads1), swap(send_d1)
    g1, pre0, sums_i1 = after_attn_backward(
        scatter_rows(partial), grad_hidden, out0, live_own, vec1
    )
    attn1 = attn_weight_grad(
        keep1["hold_f"], got_f1, grads1, got_g1, keep1["context"], got_c1, hold_d1, got_d1
    )
    branch0 = gather_rows(pre0)
    branch0, mlp1, attn1 = lax.optimization_barrier((branch0, mlp1, attn1))
    mlp1, attn1 = dp_total_far(mlp1), dp_total_far(attn1)
    partial, (hold_r0, send_r0, ebias0) = mlp_backward(
        0, sec_flag, branch0, act_grad0, expand, shrink
    )
    got_r0 = swap(send_r0)
    grad_hidden, low0, sums_f0 = after_mlp_backward(scatter_rows(partial), hidden0, pre0, vec0)
    mlp0 = mlp_weight_grad(hold_l0, got_l0, hold_r0, got_r0)
    low_blocks = gather_rows(low0)
    partial, (grads0, hold_d0, send_d0, abias0) = attn_backward(
        0, sec_flag, low_blocks, keep0, qkv, dense
    )
    got_g0, got_d0 = swap(grads0), swap(send_d0)
    g0, _, sums_i0 = after_attn_backward(
        scatter_rows(partial), grad_hidden, x_own0, live_own, vec0
    )
    blocks1 = scatter_rows(mlp_out(1, sec_flag, act1, shrink))
    out1, _ = after_mlp(blocks1, hidden1, live_own, vec1, vec1)

    def small_rows(sums_i, sums_f, ebias, abias):
        last = jnp.pad(abias.reshape(1, 512), ((0, 0), (0, 512)))
        return jnp.concatenate([sums_i, sums_f, ebias, last], axis=0)

    small0 = small_rows(sums_i0, sums_f0, ebias0, abias0)
    small1 = small_rows(sums_i1, sums_f1, ebias1, abias1)
    small = jnp.where(on0, small0, small1) + swap(jnp.where(on0, small1, small0))
    small = jnp.pad(small.astype(BF).reshape(16, 2, 256), ((0, 0), (0, 14), (0, 0)))
    parts0 = (
        keep0["hold_f"], got_f0, grads0, got_g0, keep0["context"], got_c0, hold_d0, got_d0
    )
    joint = attn_weight_grad_joint(parts0, mlp0, small)

    def all_slots(held0, held1):
        mine = jnp.where(on0, held0, held1).reshape(2, 32, -1)
        other = swap(jnp.where(on0, held1, held0)).reshape(2, 32, -1)
        return jnp.concatenate(
            [jnp.where(on0, mine, other), jnp.where(on0, other, mine)], axis=0
        )

    layer_out = all_slots(out0, out1)
    input_grad = all_slots(g0, g1)

    joint = lax.all_to_all(joint, "dp", 0, 0)
    joint, layer_out, input_grad = lax.optimization_barrier((joint, layer_out, input_grad))
    joint = lax.all_to_all(spread_sums(joint), "dp", 0, 0)

    wide = write_out(1, sec_flag, False, [mlp1, attn1], [], FLOPS_FAR)
    wide = write_out(1, sec_flag, True, [swap(mlp1), swap(attn1)], wide, FLOPS_FAR)
    joint, *wide = lax.optimization_barrier((joint, *wide))
    small = joint[:, 256 + 128 : 256 + 130].reshape(8, 1024)
    mixed = small[:6].astype(F32)
    mixed = mixed + sum(
        lax.ppermute(small[:6], "mp", ring("mp", k)).astype(F32) for k in (1, 2, 3)
    )
    alone = small[6:].astype(F32)
    wide = write_out(0, sec_flag, False, [joint], wide, 1e6)
    wide = write_out(0, sec_flag, True, [swap(joint)], wide, 1e6)

    return (
        layer_out[None],
        input_grad[None],
        mixed[0:1],
        mixed[1:2],
        jnp.transpose(wide[2], (1, 0, 2))[None],
        alone[1, :512].reshape(1, 2, 256),
        wide[3][None],
        mixed[2:3],
        mixed[3:4],
        mixed[4:5],
        wide[0][None],
        alone[0:1],
        wide[1][None],
        mixed[5:6],
    )


def solution(mesh):
    return jax.shard_map(
        per_device,
        mesh=mesh,
        in_specs=(
            P("dp", None, None),
            P("dp", None, None),
            P("dp", None),
            P("section", None),
            P("section", None),
            P("section", None, None, "mp"),
            P("section", None, "mp"),
            P("section", "mp", None),
            P("section", None),
            P("section", None),
            P("section", None),
            P("section", None, "mp"),
            P("section", "mp"),
            P("section", "mp", None),
            P("section", None),
        ),
        out_specs=(
            P("section", "dp", "mp", None),
            P("section", "dp", "mp", None),
            P("section", None),
            P("section", None),
            P("section", None, None, "mp"),
            P("section", None, "mp"),
            P("section", "mp", None),
            P("section", None),
            P("section", None),
            P("section", None),
            P("section", None, "mp"),
            P("section", "mp"),
            P("section", "mp", None),
            P("section", None),
        ),
        check_vma=False,
    )
```

```python
import jax
import jax.numpy as jnp
from jax import lax
from jax.experimental import pallas as pl
from jax.experimental.pallas import tpu as pltpu
from jax.sharding import PartitionSpec as P

HEADS = 16
HEAD = 64
EPS = 1e-05
BF = jnp.bfloat16
F32 = jnp.float32


def dot(a, b):
    return jnp.dot(a, b, preferred_element_type=F32)


def dot_t(a, b):
    return lax.dot_general(a, b, (((1,), (1,)), ((), ())), preferred_element_type=F32)


def t_dot(a, b):
    return lax.dot_general(a, b, (((0,), (0,)), ((), ())), preferred_element_type=F32)


def normalize(h):
    center = h - jnp.mean(h, axis=-1, keepdims=True)
    inverse = lax.rsqrt(jnp.mean(center * center, axis=-1, keepdims=True) + EPS)
    return center * inverse, inverse


def norm_back(normed, inverse, gain, grad):
    z = grad * gain
    return inverse * (
        z
        - jnp.mean(z, axis=-1, keepdims=True)
        - normed * jnp.mean(z * normed, axis=-1, keepdims=True)
    )


def ring(axis, steps):
    n = lax.axis_size(axis)
    return [(i, (i + steps) % n) for i in range(n)]


def swap(x):
    return lax.ppermute(x, "section", [(0, 1), (1, 0)])


FLOPS_FAR = 2e11


def dp_total_far(x):
    return lax.psum(x, "dp")


def gather_rows(own):
    return [own] + [lax.ppermute(own, "mp", ring("mp", k)) for k in (1, 2, 3)]


def scatter_rows(blocks):
    return [blocks[0]] + [lax.ppermute(blocks[k], "mp", ring("mp", -k)) for k in (1, 2, 3)]


GELU_C = 0.7978845608
GELU_A = 0.044715
ROWS = 256
OWN = 64
D = 1024
FF = 1024
TILE = 256
SCALE = HEAD**-0.5


def gelu_pair(u):
    t = jnp.tanh(GELU_C * (u + GELU_A * u * u * u))
    act = 0.5 * u * (1 + t)
    grad = 0.5 * (1 + t) + 0.5 * u * (1 - t * t) * (GELU_C * (1 + 3 * GELU_A * u * u))
    return act, grad


def sds(shape, dtype):
    return jax.ShapeDtypeStruct(shape, dtype)


PARTIAL = [sds((OWN, D), F32)] + [sds((OWN, D), BF)] * 3
PARTIAL_TWO = [sds((2 * OWN, D), F32)] + [sds((2 * OWN, D), BF)] * 3
VM = pl.BlockSpec(memory_space=pltpu.VMEM)
SM = pl.BlockSpec(memory_space=pltpu.SMEM)
HB = pl.BlockSpec(memory_space=pltpu.HBM)


def call(kernel, outs, ins, scratch=(), flops=1e9, limit=52):
    specs = [HB if kind == "h" else SM if kind == "s" else VM for kind, _ in ins]
    arrays = [a for _, a in ins]
    size = sum(a.size * a.dtype.itemsize for a in arrays) + sum(
        o.size * o.dtype.itemsize for o in outs
    )
    return pl.pallas_call(
        kernel,
        out_shape=list(outs),
        in_specs=specs,
        out_specs=[VM] * len(outs),
        scratch_shapes=list(scratch),
        compiler_params=pltpu.CompilerParams(vmem_limit_bytes=limit * 2**20),
        cost_estimate=pl.CostEstimate(
            flops=int(flops), bytes_accessed=int(size), transcendentals=0
        ),
    )(*arrays)


def fetch(sec, layer, own, got, dst, sem):
    mine = sec[0] == layer

    @pl.when(mine)
    def _():
        pltpu.make_async_copy(own, dst, sem).start()

    @pl.when(jnp.logical_not(mine))
    def _():
        pltpu.make_async_copy(got, dst, sem).start()

    return pltpu.make_async_copy(own, dst, sem)


def put_partial(outs, cols, value, at=0):
    rows = pl.ds(at, OWN)
    outs[0][rows, cols] = value[:OWN]
    for k in (1, 2, 3):
        outs[k][rows, cols] = value[OWN * k : OWN * (k + 1)].astype(BF)


def tiles(width):
    return [pl.ds(i * TILE, TILE) for i in range(width // TILE)]


def lane_low():
    return lax.broadcasted_iota(jnp.int32, (ROWS, 128), 1) < HEAD


def attn_forward(layer, sec, slopes, source, vec, dist, qkv, dense):
    def kernel(*refs):
        n = len(source)
        sec, slopes, src = refs[0], refs[1], refs[2 : 2 + n]
        vec, dist, qo, qg, do, dg = refs[2 + n : 8 + n]
        o0, o1, o2, o3, proj, probs, context, hold, send = refs[8 + n : 17 + n]
        first, wq, wd, sem = refs[-4:]
        get_q = fetch(sec, layer, qo, qg, wq, sem.at[0])
        get_d = fetch(sec, layer, do, dg, wd, sem.at[1])
        if n == 1:
            normed, _ = normalize(src[0][...].astype(F32))
            first[...] = (normed * vec[0:1] + vec[1:2]).astype(BF)
            refs[17 + n][...] = normed.astype(BF)
        else:
            for k in range(4):
                first[pl.ds(OWN * k, OWN)] = src[k][...]
        on0 = sec[0] == 0
        hold[...] = jnp.where(on0, first[:, :512], first[:, 512:])
        send[...] = jnp.where(on0, first[:, 512:], first[:, :512])
        get_q.wait()
        f = first[...]
        proj[0] = (dot(f, wq[0]) + vec[7:8, 0:256]).astype(BF)
        proj[1] = dot(f, wq[1]).astype(BF)
        proj[2] = (dot(f, wq[2]) + vec[7:8, 256:512]).astype(BF)
        low = lane_low()
        for pair in range(2):
            cols = pl.ds(128 * pair, 128)
            q, k, v = proj[0, :, cols], proj[1, :, cols], proj[2, :, cols]
            ctx = []
            for h in range(2):
                picked = jnp.where(low if h == 0 else jnp.logical_not(low), q, jnp.zeros_like(q))
                s = dot_t(picked, k) * SCALE - slopes[2 * pair + h] * dist[...]
                e = jnp.exp(s - jnp.max(s, axis=-1, keepdims=True))
                p = e / jnp.sum(e, axis=-1, keepdims=True)
                p = p.astype(BF)
                probs[2 * pair + h] = p
                ctx.append(dot(p, v))
            context[:, cols] = jnp.where(low, ctx[0], ctx[1]).astype(BF)
        get_d.wait()
        c = context[...]
        for cols in tiles(D):
            put_partial((o0, o1, o2, o3), cols, dot(c, wd[:, cols]))

    outs = PARTIAL + [
        sds((3, ROWS, 256), BF),
        sds((4, ROWS, ROWS), BF),
        sds((ROWS, 256), BF),
        sds((ROWS, 512), BF),
        sds((ROWS, 512), BF),
    ] + [sds((ROWS, D), BF)] * (len(source) == 1)
    ins = [("s", sec), ("s", slopes)] + [("v", a) for a in source]
    ins += [("v", vec), ("v", dist), ("h", qkv[0]), ("h", qkv[1]), ("h", dense[0]), ("h", dense[1])]
    scratch = [
        pltpu.VMEM((ROWS, D), BF),
        pltpu.VMEM((3, D, 256), BF),
        pltpu.VMEM((256, D), BF),
        pltpu.SemaphoreType.DMA((2,)),
    ]
    r = call(kernel, outs, ins, scratch, 8e8)
    keep = dict(proj=r[4], probs=r[5], context=r[6], hold_f=r[7], send_f=r[8])
    if len(source) == 1:
        keep["normed"] = r[9]
    return r[:4], keep


def total(refs, at=0):
    rows = pl.ds(at, OWN)
    return refs[0][rows, :] + sum(r[rows, :].astype(F32) for r in refs[1:])


def after_attn(blocks, x_own, vec):
    def kernel(a, b, c, d, x, vec, hidden, second):
        h = x[...].astype(F32) + total((a, b, c, d)) + vec[2:3]
        hidden[...] = h
        normed, _ = normalize(h)
        second[...] = (normed * vec[3:4] + vec[4:5]).astype(BF)

    return call(
        kernel,
        [sds((OWN, D), F32), sds((OWN, D), BF)],
        [("v", a) for a in (*blocks, x_own, vec)],
        flops=2e6,
    )


def mlp_forward(layer, sec, blocks, vec, expand, shrink):
    def kernel(sec, b0, b1, b2, b3, vec, eo, eg, so, sg, o0, o1, o2, o3, act_grad, hold, send, second, act, we, ws, sem):
        get_e = fetch(sec, layer, eo, eg, we, sem.at[0])
        get_s = fetch(sec, layer, so, sg, ws, sem.at[1])
        for k, b in enumerate((b0, b1, b2, b3)):
            second[pl.ds(OWN * k, OWN)] = b[...]
        get_e.wait()
        x = second[...]
        for cols in tiles(FF):
            a, g = gelu_pair(dot(x, we[:, cols]) + vec[6:7, cols])
            act[:, cols] = a.astype(BF)
            act_grad[:, cols] = g.astype(BF)
        get_s.wait()
        a = act[...]
        on0 = sec[0] == 0
        for cols in tiles(D):
            put_partial((o0, o1, o2, o3), cols, dot(a, ws[:, cols]))
            hold[:, cols] = jnp.where(on0, second[:, cols], act[:, cols])
            send[:, cols] = jnp.where(on0, act[:, cols], second[:, cols])

    wide = sds((ROWS, FF), BF)
    ins = [("s", sec)] + [("v", a) for a in (*blocks, vec)]
    ins += [("h", a) for a in (*expand, *shrink)]
    big = pltpu.VMEM((D, FF), BF)
    r = call(
        kernel,
        PARTIAL + [wide, wide, wide],
        ins,
        [pltpu.VMEM((ROWS, D), BF), pltpu.VMEM((ROWS, FF), BF), big, big, pltpu.SemaphoreType.DMA((2,))],
        1.1e9,
    )
    return r[:4], r[4], r[5], r[6]


def after_mlp(blocks, hidden, live, vec, vec_next, at=0):
    def kernel(a, b, c, d, hidden, live, vec, vec_next, out, first):
        o = (live[...] * (hidden[...] + total((a, b, c, d), at) + vec[5:6])).astype(BF)
        out[...] = o
        normed, _ = normalize(o.astype(F32))
        first[...] = (normed * vec_next[0:1] + vec_next[1:2]).astype(BF)

    return call(
        kernel,
        [sds((OWN, D), BF), sds((OWN, D), BF)],
        [("v", a) for a in (*blocks, hidden, live, vec, vec_next)],
        flops=2e6,
    )


def mlp_backward_last(layer, sec, blocks, branch, vec, expand, shrink):
    def kernel(
        sec, b0, b1, b2, b3, branch, vec, eo, eg, so, sg,
        o0, o1, o2, o3, hold_l, send_l, hold_r, send_r, bias, second, up_grad, act, we, ws, sem,
    ):
        get_e = fetch(sec, layer, eo, eg, we, sem.at[0])
        get_s = fetch(sec, layer, so, sg, ws, sem.at[1])
        for k, b in enumerate((b0, b1, b2, b3)):
            second[pl.ds(OWN * k, OWN)] = b[...]
        get_e.wait()
        get_s.wait()
        x = second[...]
        br = branch[...]
        on0 = sec[0] == 0
        for cols in tiles(FF):
            a, g = gelu_pair(dot(x, we[:, cols]) + vec[6:7, cols])
            a = a.astype(BF)
            act[:, cols] = a
            u = (dot_t(br, ws[cols, :]) * g).astype(BF)
            up_grad[:, cols] = u
            bias[:, cols] = jnp.sum(u.astype(F32), axis=0, keepdims=True)
            hold_l[:, cols] = jnp.where(on0, x_tile(second, cols), a)
            send_l[:, cols] = jnp.where(on0, a, x_tile(second, cols))
            hold_r[:, cols] = jnp.where(on0, u, x_tile(branch, cols))
            send_r[:, cols] = jnp.where(on0, x_tile(branch, cols), u)
        u = up_grad[...]
        for cols in tiles(D):
            put_partial((o0, o1, o2, o3), cols, dot_t(u, we[cols, :]))
            put_partial((o0, o1, o2, o3), cols, dot(act[...], ws[:, cols]), OWN)

    wide = sds((ROWS, FF), BF)
    ins = [("s", sec)] + [("v", a) for a in (*blocks, branch, vec)]
    ins += [("h", a) for a in (*expand, *shrink)]
    big = pltpu.VMEM((D, FF), BF)
    r = call(
        kernel,
        PARTIAL_TWO + [wide] * 4 + [sds((1, FF), F32)],
        ins,
        [pltpu.VMEM((ROWS, D), BF)]
        + [pltpu.VMEM((ROWS, FF), BF)] * 2
        + [big, big, pltpu.SemaphoreType.DMA((2,))],
        1.6e9,
    )
    return r[:4], r[4:]


def x_tile(ref, cols):
    return ref[:, cols]


def mlp_backward(layer, sec, blocks, act_grad, expand, shrink):
    def kernel(
        sec, b0, b1, b2, b3, act_grad, eo, eg, so, sg,
        o0, o1, o2, o3, hold_r, send_r, bias, branch, up_grad, we, ws, sem,
    ):
        get_s = fetch(sec, layer, so, sg, ws, sem.at[1])
        get_e = fetch(sec, layer, eo, eg, we, sem.at[0])
        for k, b in enumerate((b0, b1, b2, b3)):
            branch[pl.ds(OWN * k, OWN)] = b[...]
        get_s.wait()
        br = branch[...]
        on0 = sec[0] == 0
        for cols in tiles(FF):
            u = (dot_t(br, ws[cols, :]) * act_grad[:, cols].astype(F32)).astype(BF)
            up_grad[:, cols] = u
            bias[:, cols] = jnp.sum(u.astype(F32), axis=0, keepdims=True)
            hold_r[:, cols] = jnp.where(on0, u, branch[:, cols])
            send_r[:, cols] = jnp.where(on0, branch[:, cols], u)
        get_e.wait()
        u = up_grad[...]
        for cols in tiles(D):
            put_partial((o0, o1, o2, o3), cols, dot_t(u, we[cols, :]))

    wide = sds((ROWS, FF), BF)
    ins = [("s", sec)] + [("v", a) for a in (*blocks, act_grad)]
    ins += [("h", a) for a in (*expand, *shrink)]
    big = pltpu.VMEM((D, FF), BF)
    r = call(
        kernel,
        PARTIAL + [wide] * 2 + [sds((1, FF), F32)],
        ins,
        [pltpu.VMEM((ROWS, D), BF), pltpu.VMEM((ROWS, FF), BF), big, big, pltpu.SemaphoreType.DMA((2,))],
        1.1e9,
    )
    return r[:4], r[4:]


def after_mlp_backward(blocks, hidden, grad_own, vec):
    def kernel(a, b, c, d, hidden, grad_own, vec, grad_hidden, low, sums):
        gs = total((a, b, c, d))
        pre = grad_own[...].astype(F32)
        normed, inverse = normalize(hidden[...])
        gh = pre + norm_back(normed, inverse, vec[3:4], gs)
        grad_hidden[...] = gh
        lo = gh.astype(BF)
        low[...] = lo
        sums[0:1] = jnp.sum(lo.astype(F32), axis=0, keepdims=True)
        sums[1:2] = jnp.sum(gs * normed, axis=0, keepdims=True)
        sums[2:3] = jnp.sum(gs, axis=0, keepdims=True)
        sums[3:4] = jnp.sum(pre, axis=0, keepdims=True)

    return call(
        kernel,
        [sds((OWN, D), F32), sds((OWN, D), BF), sds((4, D), F32)],
        [("v", a) for a in (*blocks, hidden, grad_own, vec)],
        flops=2e6,
    )


def attn_backward(layer, sec, blocks, keep, qkv, dense):
    summed = "normed" in keep

    def kernel(sec, b0, b1, b2, b3, proj, probs, *refs):
        normed = refs[0] if summed else None
        qo, qg, do, dg, o0, o1, o2, o3, grads, hold, send, bias = refs[summed : 12 + summed]
        full, wq, wd, sem = refs[-4:]
        get_d = fetch(sec, layer, do, dg, wd, sem.at[1])
        get_q = fetch(sec, layer, qo, qg, wq, sem.at[0])
        for k, b in enumerate((b0, b1, b2, b3)):
            full[pl.ds(OWN * k, OWN)] = b[...]
        on0 = sec[0] == 0
        hold[...] = jnp.where(on0, full[:, :512], full[:, 512:])
        send[...] = jnp.where(on0, full[:, 512:], full[:, :512])
        get_d.wait()
        gc = dot_t(full[...], wd[...]).astype(BF)
        low = lane_low()
        for pair in range(2):
            cols = pl.ds(128 * pair, 128)
            q, k, v = proj[0, :, cols], proj[1, :, cols], proj[2, :, cols]
            g = gc[:, 128 * pair : 128 * pair + 128]
            parts = []
            for h in range(2):
                p_low = probs[2 * pair + h]
                p = p_low.astype(F32)
                picked = jnp.where(low if h == 0 else jnp.logical_not(low), g, jnp.zeros_like(g))
                gp = dot_t(picked, v)
                gs = (p * (gp - jnp.sum(p * gp, axis=-1, keepdims=True))).astype(BF)
                parts.append((dot(gs, k) * SCALE, t_dot(gs, q) * SCALE, t_dot(p_low, g)))
            for c in range(3):
                grads[:, pl.ds(256 * c + 128 * pair, 128)] = jnp.where(
                    low, parts[0][c], parts[1][c]
                ).astype(BF)
        bias[0:1] = jnp.sum(grads[:, 0:256].astype(F32), axis=0, keepdims=True)
        bias[1:2] = jnp.sum(grads[:, 512:768].astype(F32), axis=0, keepdims=True)
        get_q.wait()
        gr = [grads[:, 256 * c : 256 * c + 256] for c in range(3)]
        for cols in tiles(D):
            o = dot_t(gr[0], wq[0, cols]) + dot_t(gr[1], wq[1, cols]) + dot_t(gr[2], wq[2, cols])
            put_partial((o0, o1, o2, o3), cols, o)
            if summed:
                sums = refs[12 + summed]
                sums[0:1, cols] = jnp.sum(o * normed[:, cols].astype(F32), axis=0, keepdims=True)
                sums[1:2, cols] = jnp.sum(o, axis=0, keepdims=True)

    half = sds((ROWS, 512), BF)
    ins = [("s", sec)] + [("v", a) for a in (*blocks, keep["proj"], keep["probs"])]
    if summed:
        ins += [("v", keep["normed"])]
    ins += [("h", a) for a in (*qkv, *dense)]
    r = call(
        kernel,
        PARTIAL
        + [sds((ROWS, 768), BF), half, half, sds((2, 256), F32)]
        + [sds((2, D), F32)] * summed,
        ins,
        [
            pltpu.VMEM((ROWS, D), BF),
            pltpu.VMEM((3, D, 256), BF),
            pltpu.VMEM((256, D), BF),
            pltpu.SemaphoreType.DMA((2,)),
        ],
        1.2e9,
    )
    return r[:4], r[4:]


def after_attn_backward(blocks, grad_hidden, x_own, live, vec):
    def kernel(a, b, c, d, grad_hidden, x, live, vec, out, pre, sums):
        gf = total((a, b, c, d))
        normed, inverse = normalize(x[...].astype(F32))
        g = (grad_hidden[...] + norm_back(normed, inverse, vec[0:1], gf)).astype(BF)
        out[...] = g
        pre[...] = (live[...] * g.astype(F32)).astype(BF)
        sums[0:1] = jnp.sum(gf * normed, axis=0, keepdims=True)
        sums[1:2] = jnp.sum(gf, axis=0, keepdims=True)

    return call(
        kernel,
        [sds((OWN, D), BF), sds((OWN, D), BF), sds((2, D), F32)],
        [("v", a) for a in (*blocks, grad_hidden, x_own, live, vec)],
        flops=2e6,
    )


def mlp_weight_grad(left, got_left, right, got_right):
    def kernel(l, gl, r, gr, out):
        rv, grv = r[...], gr[...]
        for t in range(4):
            rows = pl.ds(t * TILE, TILE)
            g = (t_dot(l[:, rows], rv) + t_dot(gl[:, rows], grv)).astype(BF)
            for i in range(4):
                for c in range(4):
                    out[4 * t + i, pl.ds(64 * c, 64), :] = g[
                        64 * i : 64 * i + 64, 256 * c : 256 * c + 256
                    ]

    return call(
        kernel,
        [sds((16, 256, 256), BF)],
        [("v", a) for a in (left, got_left, right, got_right)],
        flops=1.1e9,
    )[0]


def attn_weight_grad(first, got_first, grads, got_grads, ctx, got_ctx, low, got_low):
    def kernel(f, gf, g, gg, c, gc, d, gd, out):
        def put(at, value):
            value = value.astype(BF)
            out[at // 128] = value[:128]
            out[at // 128 + 1] = value[128:]

        for half in range(2):
            rows = slice(256 * half, 256 * half + 256)
            for part in range(3):
                cols = slice(256 * part, 256 * part + 256)
                put(
                    512 * part + 256 * half,
                    t_dot(f[:, rows], g[:, cols]) + t_dot(gf[:, rows], gg[:, cols]),
                )
            put(1536 + 256 * half, t_dot(c[...], d[:, rows]) + t_dot(gc[...], gd[:, rows]))

    return call(
        kernel,
        [sds((16, 128, 256), BF)],
        [("v", a) for a in (first, got_first, grads, got_grads, ctx, got_ctx, low, got_low)],
        flops=5.4e8,
    )[0]


SUB = 208


def cyc(i, k):
    return lax.rem(i + k + 4, 4)


def dp_perm(axis, steps):
    if axis == "y":
        return [(i, (i // 4) * 4 + (i % 4 + steps) % 4) for i in range(16)]
    return [(i, ((i // 4 + steps) % 4) * 4 + i % 4) for i in range(16)]


def dp_send(blocks, swapped):
    out = []
    for half, axis in enumerate(("y", "z") if swapped else ("z", "y")):
        for k in range(4):
            b = blocks[4 * half + k]
            out.append(b if k == 0 else lax.ppermute(b, "dp", dp_perm(axis, k)))
    return out


def dp_share(shares, swapped):
    return dp_send([shares[0]] * 4 + [shares[1]] * 4, swapped)


def mlp_weight_grad_zy(left, got_left, right, got_right):
    def kernel(l, gl, r, gr, full):
        rv, grv = r[...], gr[...]
        for t in range(4):
            rows = pl.ds(t * TILE, TILE)
            g = (t_dot(l[:, rows], rv) + t_dot(gl[:, rows], grv)).astype(BF)
            for u in range(2):
                for c in range(4):
                    full[2 * t + u, c] = g[128 * u : 128 * u + 128, 256 * c : 256 * c + 256]

    return call(
        kernel,
        [sds((8, 4, 128, 256), BF)],
        [("v", a) for a in (left, got_left, right, got_right)],
        flops=1.1e9,
    )[0]


def joint_blocks(zy, parts, small, mlp):
    def kernel(zy, f, gf, g, gg, c, gc, d, gd, sm, mlp, *rest):
        full = rest[8]
        full[:, :, pl.ds(64, 16)] = sm[...]

        def put(at, value):
            value = value.astype(BF)
            for i in range(4):
                full[at // 256, i, pl.ds(0, 64)] = value[64 * i : 64 * i + 64]

        for half in range(2):
            rows = slice(256 * half, 256 * half + 256)
            for part in range(3):
                cols = slice(256 * part, 256 * part + 256)
                put(
                    512 * part + 256 * half,
                    t_dot(f[:, rows], g[:, cols]) + t_dot(gf[:, rows], gg[:, cols]),
                )
            put(1536 + 256 * half, t_dot(c[...], d[:, rows]) + t_dot(gc[...], gd[:, rows]))
        for half in range(2):
            for k in range(4):
                b = 4 * half + cyc(zy[half], k)
                rest[4 * half + k][:, pl.ds(0, 128)] = mlp[b]
                rest[4 * half + k][:, pl.ds(128, 80)] = full[b]

    return call(
        kernel,
        [sds((4, SUB, 256), BF)] * 8,
        [("s", zy)] + [("v", a) for a in (*parts, small, mlp)],
        [pltpu.VMEM((8, 4, 80, 256), BF)],
        flops=5.4e8,
    )


def fold(zy, blocks):
    def kernel(zy, *refs):
        for half in range(2):
            for k in range(4):
                j = cyc(zy[1 - half], k)
                src = refs[4 * half : 4 * half + 4]
                refs[8 + 4 * half + k][...] = sum(r[j].astype(F32) for r in src).astype(BF)

    return call(
        kernel,
        [sds((SUB, 256), BF)] * 8,
        [("s", zy)] + [("v", a) for a in blocks],
        flops=2e6,
    )


def fold_last(blocks):
    def kernel(*refs):
        for half in range(2):
            src = refs[4 * half : 4 * half + 4]
            refs[8 + half][...] = sum(r[...].astype(F32) for r in src).astype(BF)

    return call(kernel, [sds((SUB, 256), BF)] * 2, [("v", a) for a in blocks], flops=1e6)


def assemble(zy, blocks):
    def kernel(zy, *refs):
        for half in range(2):
            for k in range(4):
                refs[8 + half][cyc(zy[1 - half], -k)] = refs[4 * half + k][...]

    return call(
        kernel,
        [sds((4, SUB, 256), BF)] * 2,
        [("s", zy)] + [("v", a) for a in blocks],
        flops=1e6,
    )


def small_out(zy, blocks):
    def kernel(zy, *refs):
        for half in range(2):
            for k in range(4):
                refs[8][4 * half + cyc(zy[half], -k)] = refs[4 * half + k][:, pl.ds(192, 16), :]

    return call(
        kernel,
        [sds((8, 4, 16, 256), BF)],
        [("s", zy)] + [("v", a) for a in blocks],
        flops=1e6,
    )[0]


WIDE_OUT = [sds((D, FF), F32), sds((D, FF), F32), sds((3, D, 256), F32), sds((256, D), F32)]


def write_out(layer, sec, zy, far, grads, held, flops):
    n = len(grads)

    def kernel(sec, zy, *refs):
        src = refs[:n]
        outs = refs[n + len(held) : n + len(held) + 4]
        wide, tall, sem = refs[n + len(held) + 4 :]

        @pl.when(sec[0] == layer)
        def _():
            which = (1 - layer) if far else layer
            target = outs[which]
            copies = []
            if n == 2:
                for i in range(16):
                    for c in range(4):
                        wide[pl.ds(64 * i, 64), pl.ds(256 * c, 256)] = src[0][
                            i, pl.ds(64 * c, 64), :
                        ].astype(F32)
                    tall[pl.ds(128 * i, 128)] = src[1][i].astype(F32)
            else:
                for half in range(2):
                    for k in range(4):
                        b = 4 * half + cyc(zy[half], -k)
                        ref = src[4 * half + k]
                        for c in range(4):
                            at = pl.ds(pl.multiple_of(128 * b, 128), 128)
                            wide[at, pl.ds(256 * c, 256)] = ref[c, pl.ds(0, 128), :].astype(F32)
                            at = pl.ds(pl.multiple_of(256 * b + 64 * c, 64), 64)
                            tall[at, :] = ref[c, pl.ds(128, 64), :].astype(F32)
            for i in range(4):
                rows = pl.ds(256 * i, 256)
                copies.append(pltpu.make_async_copy(wide.at[rows], target.at[rows], sem.at[i]))
                copies[-1].start()
            for p in range(3):
                copies.append(
                    pltpu.make_async_copy(
                        tall.at[pl.ds(512 * p, 512)],
                        outs[2].at[p, pl.ds(512 * which, 512)],
                        sem.at[4 + p],
                    )
                )
                copies[-1].start()
            for h in range(2):
                copies.append(
                    pltpu.make_async_copy(
                        tall.at[pl.ds(1536 + 256 * h, 256)],
                        outs[3].at[:, pl.ds(512 * which + 256 * h, 256)],
                        sem.at[7 + h],
                    )
                )
                copies[-1].start()
            for c in copies:
                c.wait()

    return pl.pallas_call(
        kernel,
        out_shape=WIDE_OUT,
        in_specs=[SM, SM] + [VM] * n + [HB] * len(held),
        out_specs=[HB] * 4,
        scratch_shapes=[
            pltpu.VMEM((D, FF), F32),
            pltpu.VMEM((2048, 256), F32),
            pltpu.SemaphoreType.DMA((9,)),
        ],
        input_output_aliases={2 + n + i: i for i in range(len(held))},
        compiler_params=pltpu.CompilerParams(vmem_limit_bytes=52 * 2**20),
        cost_estimate=pl.CostEstimate(flops=int(flops), bytes_accessed=9000000, transcendentals=0),
    )(sec, zy, *grads, *held)


def per_device(
    tokens,
    cotangent,
    seq_lengths,
    attn_gain,
    attn_shift,
    attn_weight,
    attn_bias,
    dense_weight,
    dense_bias,
    mlp_gain,
    mlp_shift,
    expand_weight,
    expand_bias,
    shrink_weight,
    shrink_bias,
):
    sec = lax.axis_index("section")
    mp = lax.axis_index("mp")
    on0 = sec == 0

    own_qkv = jnp.transpose(attn_weight[0], (1, 0, 2))
    own_w = [own_qkv, dense_weight[0], expand_weight[0], shrink_weight[0]]
    vectors = jnp.concatenate(
        [attn_gain, attn_shift, dense_bias, mlp_gain, mlp_shift, shrink_bias, expand_bias]
        + [jnp.pad(attn_bias.reshape(1, -1), ((0, 0), (0, 512)))],
        axis=0,
    )
    got_vec = swap(vectors)
    got_w = [swap(w) for w in own_w]

    def pick(layer, own, got):
        return jnp.where(on0, own, got) if layer == 0 else jnp.where(on0, got, own)

    vec0 = pick(0, vectors, got_vec)
    vec1 = pick(1, vectors, got_vec)
    qkv, dense, expand, shrink = [(o, g) for o, g in zip(own_w, got_w)]
    sec_flag = sec.astype(jnp.int32).reshape(1)

    def rel(x):
        x = lax.dynamic_slice_in_dim(x, 2 * sec, 2, 0).reshape(2, 4, 32, -1)
        parts = [lax.dynamic_index_in_dim(x, (mp - k) % 4, 1, keepdims=False) for k in range(4)]
        return jnp.concatenate(parts, axis=0).reshape(256, -1)

    lengths = lax.dynamic_slice_in_dim(seq_lengths, 2 * sec, 2, 0)
    bounds = jnp.cumsum(lengths, axis=1)
    pos = (32 * ((mp - jnp.arange(4)) % 4)[:, None] + jnp.arange(32)[None]).reshape(128)
    segment = jnp.sum((pos[None, :, None] >= bounds[:, None, :]).astype(jnp.int32), axis=2)
    segment = segment + jnp.array([0, 8], jnp.int32)[:, None]

    def spread(x):
        return jnp.broadcast_to(x, (2, 128)).reshape(2, 4, 32).transpose(1, 0, 2).reshape(256)

    seg_rows, pos_rows = spread(segment), spread(pos[None])
    allowed = (seg_rows[:, None] == seg_rows[None, :]) & (pos_rows[None, :] <= pos_rows[:, None])
    dist = jnp.where(allowed, (pos_rows[:, None] - pos_rows[None, :]).astype(F32), 1e33)
    live = (pos[None] < bounds[:, -1:]).astype(F32)
    live_rows = live.reshape(2, 4, 32).transpose(1, 0, 2).reshape(256, 1)
    live_own = live_rows[:64]
    heads_local = attn_weight.shape[3] // HEAD
    head_ids = mp * heads_local + jnp.arange(heads_local)
    slopes = jnp.exp2(-8.0 * (head_ids + 1).astype(F32) / HEADS)

    x_all = rel(tokens)
    x_own0 = x_all[:OWN]
    branch1 = rel(cotangent) * live_rows.astype(BF)

    dp = lax.axis_index("dp")
    zy = jnp.stack([dp // 4, dp % 4]).astype(jnp.int32)

    partial, keep0 = attn_forward(0, sec_flag, slopes, [x_all], vec0, dist, qkv, dense)
    hidden0, second = after_attn(scatter_rows(partial), x_own0, vec0)
    got_f0, got_c0 = swap(keep0["send_f"]), swap(keep0["context"])
    partial, act_grad0, hold_l0, send_l0 = mlp_forward(
        0, sec_flag, gather_rows(second), vec0, expand, shrink
    )
    got_l0 = swap(send_l0)
    out0, first = after_mlp(scatter_rows(partial), hidden0, live_own, vec0, vec1)
    partial, keep1 = attn_forward(
        1, sec_flag, slopes, gather_rows(first), vec1, dist, qkv, dense
    )
    got_f1, got_c1 = swap(keep1["send_f"]), swap(keep1["context"])
    hidden1, second = after_attn(scatter_rows(partial), out0, vec1)
    pre1 = branch1[:OWN]
    partial, (hold_l1, send_l1, hold_r1, send_r1, ebias1) = mlp_backward_last(
        1, sec_flag, gather_rows(second), branch1, vec1, expand, shrink
    )
    got_l1, got_r1 = swap(send_l1), swap(send_r1)
    blocks1 = scatter_rows(partial)
    grad_hidden, low1, sums_f1 = after_mlp_backward(blocks1, hidden1, pre1, vec1)
    out1, _ = after_mlp(blocks1, hidden1, live_own, vec1, vec1, OWN)
    mlp1 = mlp_weight_grad(hold_l1, got_l1, hold_r1, got_r1)
    partial, (grads1, hold_d1, send_d1, abias1) = attn_backward(
        1, sec_flag, gather_rows(low1), keep1, qkv, dense
    )
    got_g1, got_d1 = swap(grads1), swap(send_d1)
    g1, pre0, sums_i1 = after_attn_backward(
        scatter_rows(partial), grad_hidden, out0, live_own, vec1
    )
    attn1 = attn_weight_grad(
        keep1["hold_f"], got_f1, grads1, got_g1, keep1["context"], got_c1, hold_d1, got_d1
    )
    branch0 = gather_rows(pre0)
    branch0, mlp1, attn1 = lax.optimization_barrier((branch0, mlp1, attn1))
    mlp1, attn1 = dp_total_far(mlp1), dp_total_far(attn1)
    partial, (hold_r0, send_r0, ebias0) = mlp_backward(
        0, sec_flag, branch0, act_grad0, expand, shrink
    )
    got_r0 = swap(send_r0)
    grad_hidden, low0, sums_f0 = after_mlp_backward(scatter_rows(partial), hidden0, pre0, vec0)
    mlp0 = mlp_weight_grad_zy(hold_l0, got_l0, hold_r0, got_r0)
    low_blocks, mlp0 = lax.optimization_barrier((gather_rows(low0), mlp0))
    partial, (grads0, hold_d0, send_d0, abias0, sums_h0) = attn_backward(
        0, sec_flag, low_blocks, keep0, qkv, dense
    )
    got_g0, got_d0 = swap(grads0), swap(send_d0)
    g0, _, _ = after_attn_backward(
        scatter_rows(partial), grad_hidden, x_own0, live_own, vec0
    )
    def small_rows(sums_i, sums_f, ebias, abias):
        last = jnp.pad(abias.reshape(1, 512), ((0, 0), (0, 512)))
        return jnp.concatenate([sums_i, sums_f, ebias, last], axis=0)

    small0 = small_rows(sums_h0, sums_f0, ebias0, abias0)
    small1 = small_rows(sums_i1, sums_f1, ebias1, abias1)
    small = jnp.where(on0, small0, small1) + swap(jnp.where(on0, small1, small0))
    small = jnp.pad(small.astype(BF).reshape(8, 4, 1, 256), ((0, 0), (0, 0), (0, 15), (0, 0)))
    parts0 = (
        keep0["hold_f"], got_f0, grads0, got_g0, keep0["context"], got_c0, hold_d0, got_d0
    )
    joint = dp_send(joint_blocks(zy, parts0, small, mlp0), False)

    def all_slots(held0, held1):
        mine = jnp.where(on0, held0, held1).reshape(2, 32, -1)
        other = swap(jnp.where(on0, held1, held0)).reshape(2, 32, -1)
        return jnp.concatenate(
            [jnp.where(on0, mine, other), jnp.where(on0, other, mine)], axis=0
        )

    layer_out = all_slots(out0, out1)
    input_grad = all_slots(g0, g1)

    joint = dp_send(fold(zy, joint), True)
    joint = dp_share(fold_last(joint), True)
    wide = write_out(1, sec_flag, zy, False, [mlp1, attn1], [], FLOPS_FAR)
    wide = write_out(1, sec_flag, zy, True, [swap(mlp1), swap(attn1)], wide, FLOPS_FAR)
    joint, wide, layer_out, input_grad = lax.optimization_barrier(
        (joint, wide, layer_out, input_grad)
    )
    joint = dp_share(assemble(zy, joint), False)
    far = [swap(b) for b in joint]
    small = small_out(zy, joint)[:, :, 0].reshape(8, 1024)
    mixed = small[:6].astype(F32)
    mixed = mixed + sum(
        lax.ppermute(small[:6], "mp", ring("mp", k)).astype(F32) for k in (1, 2, 3)
    )
    alone = small[6:].astype(F32)
    wide = write_out(0, sec_flag, zy, False, joint, wide, 1e6)
    wide = write_out(0, sec_flag, zy, True, far, wide, 1e6)

    return (
        layer_out[None],
        input_grad[None],
        mixed[0:1],
        mixed[1:2],
        jnp.transpose(wide[2], (1, 0, 2))[None],
        alone[1, :512].reshape(1, 2, 256),
        wide[3][None],
        mixed[2:3],
        mixed[3:4],
        mixed[4:5],
        wide[0][None],
        alone[0:1],
        wide[1][None],
        mixed[5:6],
    )


def solution(mesh):
    return jax.shard_map(
        per_device,
        mesh=mesh,
        in_specs=(
            P("dp", None, None),
            P("dp", None, None),
            P("dp", None),
            P("section", None),
            P("section", None),
            P("section", None, None, "mp"),
            P("section", None, "mp"),
            P("section", "mp", None),
            P("section", None),
            P("section", None),
            P("section", None),
            P("section", None, "mp"),
            P("section", "mp"),
            P("section", "mp", None),
            P("section", None),
        ),
        out_specs=(
            P("section", "dp", "mp", None),
            P("section", "dp", "mp", None),
            P("section", None),
            P("section", None),
            P("section", None, None, "mp"),
            P("section", None, "mp"),
            P("section", "mp", None),
            P("section", None),
            P("section", None),
            P("section", None),
            P("section", None, "mp"),
            P("section", "mp"),
            P("section", "mp", None),
            P("section", None),
        ),
        check_vma=False,
    )
```

```python
import jax
import jax.numpy as jnp
from jax import lax
from jax.experimental import pallas as pl
from jax.experimental.pallas import tpu as pltpu
from jax.sharding import PartitionSpec as P

HEADS = 16
HEAD = 64
EPS = 1e-05
BF = jnp.bfloat16
F32 = jnp.float32


def dot(a, b):
    return jnp.dot(a, b, preferred_element_type=F32)


def dot_t(a, b):
    return lax.dot_general(a, b, (((1,), (1,)), ((), ())), preferred_element_type=F32)


def t_dot(a, b):
    return lax.dot_general(a, b, (((0,), (0,)), ((), ())), preferred_element_type=F32)


def normalize(h):
    center = h - jnp.mean(h, axis=-1, keepdims=True)
    inverse = lax.rsqrt(jnp.mean(center * center, axis=-1, keepdims=True) + EPS)
    return center * inverse, inverse


def norm_back(normed, inverse, gain, grad):
    z = grad * gain
    return inverse * (
        z
        - jnp.mean(z, axis=-1, keepdims=True)
        - normed * jnp.mean(z * normed, axis=-1, keepdims=True)
    )


def ring(axis, steps):
    n = lax.axis_size(axis)
    return [(i, (i + steps) % n) for i in range(n)]


def swap(x):
    return lax.ppermute(x, "section", [(0, 1), (1, 0)])


def gather_rows(own):
    return [own] + [lax.ppermute(own, "mp", ring("mp", k)) for k in (1, 2, 3)]


def scatter_rows(blocks):
    return [blocks[0]] + [lax.ppermute(blocks[k], "mp", ring("mp", -k)) for k in (1, 2, 3)]


GELU_C = 0.7978845608
GELU_A = 0.044715
ROWS = 256
OWN = 64
D = 1024
FF = 1024
TILE = 256
SCALE = HEAD**-0.5


def gelu_pair(u):
    t = jnp.tanh(GELU_C * (u + GELU_A * u * u * u))
    act = 0.5 * u * (1 + t)
    grad = 0.5 * (1 + t) + 0.5 * u * (1 - t * t) * (GELU_C * (1 + 3 * GELU_A * u * u))
    return act, grad


def sds(shape, dtype):
    return jax.ShapeDtypeStruct(shape, dtype)


PARTIAL = [sds((OWN, D), F32)] + [sds((OWN, D), BF)] * 3
PARTIAL_TWO = [sds((2 * OWN, D), F32)] + [sds((2 * OWN, D), BF)] * 3
VM = pl.BlockSpec(memory_space=pltpu.VMEM)
SM = pl.BlockSpec(memory_space=pltpu.SMEM)
HB = pl.BlockSpec(memory_space=pltpu.HBM)


def call(kernel, outs, ins, scratch=(), flops=1e9, limit=52):
    specs = [HB if kind == "h" else SM if kind == "s" else VM for kind, _ in ins]
    arrays = [a for _, a in ins]
    size = sum(a.size * a.dtype.itemsize for a in arrays) + sum(
        o.size * o.dtype.itemsize for o in outs
    )
    return pl.pallas_call(
        kernel,
        out_shape=list(outs),
        in_specs=specs,
        out_specs=[VM] * len(outs),
        scratch_shapes=list(scratch),
        compiler_params=pltpu.CompilerParams(vmem_limit_bytes=limit * 2**20),
        cost_estimate=pl.CostEstimate(
            flops=int(flops), bytes_accessed=int(size), transcendentals=0
        ),
    )(*arrays)


def fetch(sec, layer, own, got, dst, sem):
    mine = sec[0] == layer

    @pl.when(mine)
    def _():
        pltpu.make_async_copy(own, dst, sem).start()

    @pl.when(jnp.logical_not(mine))
    def _():
        pltpu.make_async_copy(got, dst, sem).start()

    return pltpu.make_async_copy(own, dst, sem)


def put_partial(outs, cols, value, at=0):
    rows = pl.ds(at, OWN)
    outs[0][rows, cols] = value[:OWN]
    for k in (1, 2, 3):
        outs[k][rows, cols] = value[OWN * k : OWN * (k + 1)].astype(BF)


def tiles(width):
    return [pl.ds(i * TILE, TILE) for i in range(width // TILE)]


def lane_low():
    return lax.broadcasted_iota(jnp.int32, (ROWS, 128), 1) < HEAD


def attn_forward(layer, sec, slopes, source, vec, dist, qkv, dense):
    def kernel(*refs):
        n = len(source)
        sec, slopes, src = refs[0], refs[1], refs[2 : 2 + n]
        vec, dist, qo, qg, do, dg = refs[2 + n : 8 + n]
        o0, o1, o2, o3, proj, probs, context, hold, send = refs[8 + n : 17 + n]
        first, wq, wd, sem = refs[-4:]
        get_q = fetch(sec, layer, qo, qg, wq, sem.at[0])
        get_d = fetch(sec, layer, do, dg, wd, sem.at[1])
        if n == 1:
            normed, _ = normalize(src[0][...].astype(F32))
            first[...] = (normed * vec[0:1] + vec[1:2]).astype(BF)
            refs[17 + n][...] = normed.astype(BF)
        else:
            for k in range(4):
                first[pl.ds(OWN * k, OWN)] = src[k][...]
        on0 = sec[0] == 0
        hold[...] = jnp.where(on0, first[:, :512], first[:, 512:])
        send[...] = jnp.where(on0, first[:, 512:], first[:, :512])
        get_q.wait()
        f = first[...]
        proj[0] = (dot(f, wq[0]) + vec[7:8, 0:256]).astype(BF)
        proj[1] = dot(f, wq[1]).astype(BF)
        proj[2] = (dot(f, wq[2]) + vec[7:8, 256:512]).astype(BF)
        low = lane_low()
        for pair in range(2):
            cols = pl.ds(128 * pair, 128)
            q, k, v = proj[0, :, cols], proj[1, :, cols], proj[2, :, cols]
            ctx = []
            for h in range(2):
                picked = jnp.where(low if h == 0 else jnp.logical_not(low), q, jnp.zeros_like(q))
                s = dot_t(picked, k) * SCALE - slopes[2 * pair + h] * dist[...]
                e = jnp.exp(s - jnp.max(s, axis=-1, keepdims=True))
                p = e / jnp.sum(e, axis=-1, keepdims=True)
                p = p.astype(BF)
                probs[2 * pair + h] = p
                ctx.append(dot(p, v))
            context[:, cols] = jnp.where(low, ctx[0], ctx[1]).astype(BF)
        get_d.wait()
        c = context[...]
        for cols in tiles(D):
            put_partial((o0, o1, o2, o3), cols, dot(c, wd[:, cols]))

    outs = PARTIAL + [
        sds((3, ROWS, 256), BF),
        sds((4, ROWS, ROWS), BF),
        sds((ROWS, 256), BF),
        sds((ROWS, 512), BF),
        sds((ROWS, 512), BF),
    ] + [sds((ROWS, D), BF)] * (len(source) == 1)
    ins = [("s", sec), ("s", slopes)] + [("v", a) for a in source]
    ins += [("v", vec), ("v", dist), ("h", qkv[0]), ("h", qkv[1]), ("h", dense[0]), ("h", dense[1])]
    scratch = [
        pltpu.VMEM((ROWS, D), BF),
        pltpu.VMEM((3, D, 256), BF),
        pltpu.VMEM((256, D), BF),
        pltpu.SemaphoreType.DMA((2,)),
    ]
    r = call(kernel, outs, ins, scratch, 8e8)
    keep = dict(proj=r[4], probs=r[5], context=r[6], hold_f=r[7], send_f=r[8])
    if len(source) == 1:
        keep["normed"] = r[9]
    return r[:4], keep


def total(refs, at=0):
    rows = pl.ds(at, OWN)
    return refs[0][rows, :] + sum(r[rows, :].astype(F32) for r in refs[1:])


def after_attn(blocks, x_own, vec):
    def kernel(a, b, c, d, x, vec, hidden, second):
        h = x[...].astype(F32) + total((a, b, c, d)) + vec[2:3]
        hidden[...] = h
        normed, _ = normalize(h)
        second[...] = (normed * vec[3:4] + vec[4:5]).astype(BF)

    return call(
        kernel,
        [sds((OWN, D), F32), sds((OWN, D), BF)],
        [("v", a) for a in (*blocks, x_own, vec)],
        flops=2e6,
    )


def mlp_forward(layer, sec, blocks, vec, expand, shrink):
    def kernel(sec, b0, b1, b2, b3, vec, eo, eg, so, sg, o0, o1, o2, o3, act_grad, hold, send, second, act, we, ws, sem):
        get_e = fetch(sec, layer, eo, eg, we, sem.at[0])
        get_s = fetch(sec, layer, so, sg, ws, sem.at[1])
        for k, b in enumerate((b0, b1, b2, b3)):
            second[pl.ds(OWN * k, OWN)] = b[...]
        get_e.wait()
        x = second[...]
        for cols in tiles(FF):
            a, g = gelu_pair(dot(x, we[:, cols]) + vec[6:7, cols])
            act[:, cols] = a.astype(BF)
            act_grad[:, cols] = g.astype(BF)
        get_s.wait()
        a = act[...]
        on0 = sec[0] == 0
        for cols in tiles(D):
            put_partial((o0, o1, o2, o3), cols, dot(a, ws[:, cols]))
            hold[:, cols] = jnp.where(on0, second[:, cols], act[:, cols])
            send[:, cols] = jnp.where(on0, act[:, cols], second[:, cols])

    wide = sds((ROWS, FF), BF)
    ins = [("s", sec)] + [("v", a) for a in (*blocks, vec)]
    ins += [("h", a) for a in (*expand, *shrink)]
    big = pltpu.VMEM((D, FF), BF)
    r = call(
        kernel,
        PARTIAL + [wide, wide, wide],
        ins,
        [pltpu.VMEM((ROWS, D), BF), pltpu.VMEM((ROWS, FF), BF), big, big, pltpu.SemaphoreType.DMA((2,))],
        1.1e9,
    )
    return r[:4], r[4], r[5], r[6]


def after_mlp(blocks, hidden, live, vec, vec_next, at=0):
    def kernel(a, b, c, d, hidden, live, vec, vec_next, out, first):
        o = (live[...] * (hidden[...] + total((a, b, c, d), at) + vec[5:6])).astype(BF)
        out[...] = o
        normed, _ = normalize(o.astype(F32))
        first[...] = (normed * vec_next[0:1] + vec_next[1:2]).astype(BF)

    return call(
        kernel,
        [sds((OWN, D), BF), sds((OWN, D), BF)],
        [("v", a) for a in (*blocks, hidden, live, vec, vec_next)],
        flops=2e6,
    )


def mlp_backward_last(layer, sec, blocks, branch, vec, expand, shrink):
    def kernel(
        sec, b0, b1, b2, b3, branch, vec, eo, eg, so, sg,
        o0, o1, o2, o3, hold_l, send_l, hold_r, send_r, bias, second, up_grad, act, we, ws, sem,
    ):
        get_e = fetch(sec, layer, eo, eg, we, sem.at[0])
        get_s = fetch(sec, layer, so, sg, ws, sem.at[1])
        for k, b in enumerate((b0, b1, b2, b3)):
            second[pl.ds(OWN * k, OWN)] = b[...]
        get_e.wait()
        get_s.wait()
        x = second[...]
        br = branch[...]
        on0 = sec[0] == 0
        for cols in tiles(FF):
            a, g = gelu_pair(dot(x, we[:, cols]) + vec[6:7, cols])
            a = a.astype(BF)
            act[:, cols] = a
            u = (dot_t(br, ws[cols, :]) * g).astype(BF)
            up_grad[:, cols] = u
            bias[:, cols] = jnp.sum(u.astype(F32), axis=0, keepdims=True)
            hold_l[:, cols] = jnp.where(on0, x_tile(second, cols), a)
            send_l[:, cols] = jnp.where(on0, a, x_tile(second, cols))
            hold_r[:, cols] = jnp.where(on0, u, x_tile(branch, cols))
            send_r[:, cols] = jnp.where(on0, x_tile(branch, cols), u)
        u = up_grad[...]
        for cols in tiles(D):
            put_partial((o0, o1, o2, o3), cols, dot_t(u, we[cols, :]))
            put_partial((o0, o1, o2, o3), cols, dot(act[...], ws[:, cols]), OWN)

    wide = sds((ROWS, FF), BF)
    ins = [("s", sec)] + [("v", a) for a in (*blocks, branch, vec)]
    ins += [("h", a) for a in (*expand, *shrink)]
    big = pltpu.VMEM((D, FF), BF)
    r = call(
        kernel,
        PARTIAL_TWO + [wide] * 4 + [sds((1, FF), F32)],
        ins,
        [pltpu.VMEM((ROWS, D), BF)]
        + [pltpu.VMEM((ROWS, FF), BF)] * 2
        + [big, big, pltpu.SemaphoreType.DMA((2,))],
        1.6e9,
    )
    return r[:4], r[4:]


def x_tile(ref, cols):
    return ref[:, cols]


def mlp_backward(layer, sec, blocks, act_grad, expand, shrink):
    def kernel(
        sec, b0, b1, b2, b3, act_grad, eo, eg, so, sg,
        o0, o1, o2, o3, hold_r, send_r, bias, branch, up_grad, we, ws, sem,
    ):
        get_s = fetch(sec, layer, so, sg, ws, sem.at[1])
        get_e = fetch(sec, layer, eo, eg, we, sem.at[0])
        for k, b in enumerate((b0, b1, b2, b3)):
            branch[pl.ds(OWN * k, OWN)] = b[...]
        get_s.wait()
        br = branch[...]
        on0 = sec[0] == 0
        for cols in tiles(FF):
            u = (dot_t(br, ws[cols, :]) * act_grad[:, cols].astype(F32)).astype(BF)
            up_grad[:, cols] = u
            bias[:, cols] = jnp.sum(u.astype(F32), axis=0, keepdims=True)
            hold_r[:, cols] = jnp.where(on0, u, branch[:, cols])
            send_r[:, cols] = jnp.where(on0, branch[:, cols], u)
        get_e.wait()
        u = up_grad[...]
        for cols in tiles(D):
            put_partial((o0, o1, o2, o3), cols, dot_t(u, we[cols, :]))

    wide = sds((ROWS, FF), BF)
    ins = [("s", sec)] + [("v", a) for a in (*blocks, act_grad)]
    ins += [("h", a) for a in (*expand, *shrink)]
    big = pltpu.VMEM((D, FF), BF)
    r = call(
        kernel,
        PARTIAL + [wide] * 2 + [sds((1, FF), F32)],
        ins,
        [pltpu.VMEM((ROWS, D), BF), pltpu.VMEM((ROWS, FF), BF), big, big, pltpu.SemaphoreType.DMA((2,))],
        1.1e9,
    )
    return r[:4], r[4:]


def after_mlp_backward(blocks, hidden, grad_own, vec):
    def kernel(a, b, c, d, hidden, grad_own, vec, grad_hidden, low, sums):
        gs = total((a, b, c, d))
        pre = grad_own[...].astype(F32)
        normed, inverse = normalize(hidden[...])
        gh = pre + norm_back(normed, inverse, vec[3:4], gs)
        grad_hidden[...] = gh
        lo = gh.astype(BF)
        low[...] = lo
        sums[0:1] = jnp.sum(lo.astype(F32), axis=0, keepdims=True)
        sums[1:2] = jnp.sum(gs * normed, axis=0, keepdims=True)
        sums[2:3] = jnp.sum(gs, axis=0, keepdims=True)
        sums[3:4] = jnp.sum(pre, axis=0, keepdims=True)

    return call(
        kernel,
        [sds((OWN, D), F32), sds((OWN, D), BF), sds((4, D), F32)],
        [("v", a) for a in (*blocks, hidden, grad_own, vec)],
        flops=2e6,
    )


def attn_backward(layer, sec, blocks, keep, qkv, dense):
    summed = "normed" in keep

    def kernel(sec, b0, b1, b2, b3, proj, probs, *refs):
        normed = refs[0] if summed else None
        qo, qg, do, dg, o0, o1, o2, o3, grads, hold, send, bias = refs[summed : 12 + summed]
        full, wq, wd, sem = refs[-4:]
        get_d = fetch(sec, layer, do, dg, wd, sem.at[1])
        get_q = fetch(sec, layer, qo, qg, wq, sem.at[0])
        for k, b in enumerate((b0, b1, b2, b3)):
            full[pl.ds(OWN * k, OWN)] = b[...]
        on0 = sec[0] == 0
        hold[...] = jnp.where(on0, full[:, :512], full[:, 512:])
        send[...] = jnp.where(on0, full[:, 512:], full[:, :512])
        get_d.wait()
        gc = dot_t(full[...], wd[...]).astype(BF)
        low = lane_low()
        for pair in range(2):
            cols = pl.ds(128 * pair, 128)
            q, k, v = proj[0, :, cols], proj[1, :, cols], proj[2, :, cols]
            g = gc[:, 128 * pair : 128 * pair + 128]
            parts = []
            for h in range(2):
                p_low = probs[2 * pair + h]
                p = p_low.astype(F32)
                picked = jnp.where(low if h == 0 else jnp.logical_not(low), g, jnp.zeros_like(g))
                gp = dot_t(picked, v)
                gs = (p * (gp - jnp.sum(p * gp, axis=-1, keepdims=True))).astype(BF)
                parts.append((dot(gs, k) * SCALE, t_dot(gs, q) * SCALE, t_dot(p_low, g)))
            for c in range(3):
                grads[:, pl.ds(256 * c + 128 * pair, 128)] = jnp.where(
                    low, parts[0][c], parts[1][c]
                ).astype(BF)
        bias[0:1] = jnp.sum(grads[:, 0:256].astype(F32), axis=0, keepdims=True)
        bias[1:2] = jnp.sum(grads[:, 512:768].astype(F32), axis=0, keepdims=True)
        get_q.wait()
        gr = [grads[:, 256 * c : 256 * c + 256] for c in range(3)]
        for cols in tiles(D):
            o = dot_t(gr[0], wq[0, cols]) + dot_t(gr[1], wq[1, cols]) + dot_t(gr[2], wq[2, cols])
            put_partial((o0, o1, o2, o3), cols, o)
            if summed:
                sums = refs[12 + summed]
                sums[0:1, cols] = jnp.sum(o * normed[:, cols].astype(F32), axis=0, keepdims=True)
                sums[1:2, cols] = jnp.sum(o, axis=0, keepdims=True)

    half = sds((ROWS, 512), BF)
    ins = [("s", sec)] + [("v", a) for a in (*blocks, keep["proj"], keep["probs"])]
    if summed:
        ins += [("v", keep["normed"])]
    ins += [("h", a) for a in (*qkv, *dense)]
    r = call(
        kernel,
        PARTIAL
        + [sds((ROWS, 768), BF), half, half, sds((2, 256), F32)]
        + [sds((2, D), F32)] * summed,
        ins,
        [
            pltpu.VMEM((ROWS, D), BF),
            pltpu.VMEM((3, D, 256), BF),
            pltpu.VMEM((256, D), BF),
            pltpu.SemaphoreType.DMA((2,)),
        ],
        1.2e9,
    )
    return r[:4], r[4:]


def after_attn_backward(blocks, grad_hidden, x_own, live, vec):
    def kernel(a, b, c, d, grad_hidden, x, live, vec, out, pre, sums):
        gf = total((a, b, c, d))
        normed, inverse = normalize(x[...].astype(F32))
        g = (grad_hidden[...] + norm_back(normed, inverse, vec[0:1], gf)).astype(BF)
        out[...] = g
        pre[...] = (live[...] * g.astype(F32)).astype(BF)
        sums[0:1] = jnp.sum(gf * normed, axis=0, keepdims=True)
        sums[1:2] = jnp.sum(gf, axis=0, keepdims=True)

    return call(
        kernel,
        [sds((OWN, D), BF), sds((OWN, D), BF), sds((2, D), F32)],
        [("v", a) for a in (*blocks, grad_hidden, x_own, live, vec)],
        flops=2e6,
    )


def mlp_weight_grad(left, got_left, right, got_right):
    def kernel(l, gl, r, gr, out):
        rv, grv = r[...], gr[...]
        for t in range(4):
            rows = pl.ds(t * TILE, TILE)
            g = (t_dot(l[:, rows], rv) + t_dot(gl[:, rows], grv)).astype(BF)
            for i in range(4):
                for c in range(4):
                    out[4 * t + i, pl.ds(64 * c, 64), :] = g[
                        64 * i : 64 * i + 64, 256 * c : 256 * c + 256
                    ]

    return call(
        kernel,
        [sds((16, 256, 256), BF)],
        [("v", a) for a in (left, got_left, right, got_right)],
        flops=1.1e9,
    )[0]


def attn_weight_grad(first, got_first, grads, got_grads, ctx, got_ctx, low, got_low):
    def kernel(f, gf, g, gg, c, gc, d, gd, out):
        def put(at, value):
            value = value.astype(BF)
            out[at // 128] = value[:128]
            out[at // 128 + 1] = value[128:]

        for half in range(2):
            rows = slice(256 * half, 256 * half + 256)
            for part in range(3):
                cols = slice(256 * part, 256 * part + 256)
                put(
                    512 * part + 256 * half,
                    t_dot(f[:, rows], g[:, cols]) + t_dot(gf[:, rows], gg[:, cols]),
                )
            put(1536 + 256 * half, t_dot(c[...], d[:, rows]) + t_dot(gc[...], gd[:, rows]))

    return call(
        kernel,
        [sds((16, 128, 256), BF)],
        [("v", a) for a in (first, got_first, grads, got_grads, ctx, got_ctx, low, got_low)],
        flops=5.4e8,
    )[0]


def attn_weight_joint(parts, small):
    def kernel(f, gf, g, gg, c, gc, d, gd, sm, out):
        out[:, pl.ds(128, 16)] = sm[...]

        def put(at, value):
            value = value.astype(BF)
            out[at // 128, pl.ds(0, 128)] = value[:128]
            out[at // 128 + 1, pl.ds(0, 128)] = value[128:]

        for half in range(2):
            rows = slice(256 * half, 256 * half + 256)
            for part in range(3):
                cols = slice(256 * part, 256 * part + 256)
                put(
                    512 * part + 256 * half,
                    t_dot(f[:, rows], g[:, cols]) + t_dot(gf[:, rows], gg[:, cols]),
                )
            put(1536 + 256 * half, t_dot(c[...], d[:, rows]) + t_dot(gc[...], gd[:, rows]))

    return call(
        kernel, [sds((16, 144, 256), BF)], [("v", a) for a in (*parts, small)], flops=5.4e8
    )[0]


def spread_sums(got):
    def kernel(m, out):
        share = jnp.sum(m[...].astype(F32), axis=0).astype(BF)
        for i in range(16):
            out[i] = share

    return call(kernel, [sds((16, 144, 256), BF)], [("v", got)], flops=1e6)[0]


def write_call(layer, sec, kernel, grads, held, shapes, scratch, flops):
    n, m = len(grads), len(held)

    def body(sec, *refs):
        @pl.when(sec[0] == layer)
        def _():
            kernel(refs[:n], refs[n + m : n + m + len(shapes)], *refs[n + m + len(shapes) :])

    return pl.pallas_call(
        body,
        out_shape=shapes,
        in_specs=[SM] + [VM] * n + [HB] * m,
        out_specs=[HB] * len(shapes),
        scratch_shapes=[scratch, pltpu.SemaphoreType.DMA((5,))],
        input_output_aliases={1 + n + i: i for i in range(m)},
        compiler_params=pltpu.CompilerParams(vmem_limit_bytes=52 * 2**20),
        cost_estimate=pl.CostEstimate(flops=int(flops), bytes_accessed=6000000, transcendentals=0),
    )(sec, *grads, *held)


def write_mlp(sec, far, core0, core1, held):
    m = len(held)

    def kernel(sec, first, second, *refs):
        outs = refs[m : m + 2]
        low, wide, sem = refs[m + 2 :]
        fetch(sec, 0, first, second, low, sem.at[4]).wait()
        copies = [[], []]
        for t in range(4):
            for i in range(4 * t, 4 * t + 4):
                for c in range(4):
                    wide[pl.ds(64 * i, 64), pl.ds(256 * c, 256)] = low[
                        i, pl.ds(64 * c, 64), :
                    ].astype(F32)
            rows = pl.ds(256 * t, 256)
            for core in range(2):
                target = outs[1 - core if far else core]
                move = pltpu.make_async_copy(wide.at[rows], target.at[rows], sem.at[t])
                copies[core].append(move)
                pl.when(sec[0] == core)(move.start)
        for move in copies[0]:
            move.wait()

    return pl.pallas_call(
        kernel,
        out_shape=WIDE_OUT[:2],
        in_specs=[SM] + [HB] * (2 + m),
        out_specs=[HB] * 2,
        scratch_shapes=[
            pltpu.VMEM((16, 256, 256), BF),
            pltpu.VMEM((D, FF), F32),
            pltpu.SemaphoreType.DMA((5,)),
        ],
        input_output_aliases={3 + i: i for i in range(m)},
        compiler_params=pltpu.CompilerParams(vmem_limit_bytes=52 * 2**20),
        cost_estimate=pl.CostEstimate(
            flops=200000000000, bytes_accessed=6000000, transcendentals=0
        ),
    )(sec, core0, core1, *held)


def write_attn(layer, sec, far, grad, held, flops):
    which = (1 - layer) if far else layer

    def kernel(src, outs, tall, sem):
        for i in range(16):
            tall[pl.ds(128 * i, 128)] = src[0][i, pl.ds(0, 128), :].astype(F32)
        copies = []
        for p in range(3):
            piece = tall.at[pl.ds(512 * p, 512)]
            target = outs[0].at[p, pl.ds(512 * which, 512)]
            copies.append(pltpu.make_async_copy(piece, target, sem.at[p]))
        for h in range(2):
            piece = tall.at[pl.ds(1536 + 256 * h, 256)]
            target = outs[1].at[:, pl.ds(512 * which + 256 * h, 256)]
            copies.append(pltpu.make_async_copy(piece, target, sem.at[3 + h]))
        for c in copies:
            c.start()
        for c in copies:
            c.wait()

    return write_call(
        layer, sec, kernel, [grad], held, WIDE_OUT[2:], pltpu.VMEM((2048, 256), F32), flops
    )


WIDE_OUT = [sds((D, FF), F32), sds((D, FF), F32), sds((3, D, 256), F32), sds((256, D), F32)]


def per_device(
    tokens,
    cotangent,
    seq_lengths,
    attn_gain,
    attn_shift,
    attn_weight,
    attn_bias,
    dense_weight,
    dense_bias,
    mlp_gain,
    mlp_shift,
    expand_weight,
    expand_bias,
    shrink_weight,
    shrink_bias,
):
    sec = lax.axis_index("section")
    mp = lax.axis_index("mp")
    on0 = sec == 0

    own_qkv = jnp.transpose(attn_weight[0], (1, 0, 2))
    own_w = [own_qkv, dense_weight[0], expand_weight[0], shrink_weight[0]]
    vectors = jnp.concatenate(
        [attn_gain, attn_shift, dense_bias, mlp_gain, mlp_shift, shrink_bias, expand_bias]
        + [jnp.pad(attn_bias.reshape(1, -1), ((0, 0), (0, 512)))],
        axis=0,
    )
    got_vec = swap(vectors)
    got_w = [swap(w) for w in own_w]

    def pick(layer, own, got):
        return jnp.where(on0, own, got) if layer == 0 else jnp.where(on0, got, own)

    vec0 = pick(0, vectors, got_vec)
    vec1 = pick(1, vectors, got_vec)
    qkv, dense, expand, shrink = [(o, g) for o, g in zip(own_w, got_w)]
    sec_flag = sec.astype(jnp.int32).reshape(1)

    def rel(x):
        x = lax.dynamic_slice_in_dim(x, 2 * sec, 2, 0).reshape(2, 4, 32, -1)
        parts = [lax.dynamic_index_in_dim(x, (mp - k) % 4, 1, keepdims=False) for k in range(4)]
        return jnp.concatenate(parts, axis=0).reshape(256, -1)

    lengths = lax.dynamic_slice_in_dim(seq_lengths, 2 * sec, 2, 0)
    bounds = jnp.cumsum(lengths, axis=1)
    pos = (32 * ((mp - jnp.arange(4)) % 4)[:, None] + jnp.arange(32)[None]).reshape(128)
    segment = jnp.sum((pos[None, :, None] >= bounds[:, None, :]).astype(jnp.int32), axis=2)
    segment = segment + jnp.array([0, 8], jnp.int32)[:, None]

    def spread(x):
        return jnp.broadcast_to(x, (2, 128)).reshape(2, 4, 32).transpose(1, 0, 2).reshape(256)

    seg_rows, pos_rows = spread(segment), spread(pos[None])
    allowed = (seg_rows[:, None] == seg_rows[None, :]) & (pos_rows[None, :] <= pos_rows[:, None])
    dist = jnp.where(allowed, (pos_rows[:, None] - pos_rows[None, :]).astype(F32), 1e33)
    live = (pos[None] < bounds[:, -1:]).astype(F32)
    live_rows = live.reshape(2, 4, 32).transpose(1, 0, 2).reshape(256, 1)
    live_own = live_rows[:64]
    heads_local = attn_weight.shape[3] // HEAD
    head_ids = mp * heads_local + jnp.arange(heads_local)
    slopes = jnp.exp2(-8.0 * (head_ids + 1).astype(F32) / HEADS)

    x_all = rel(tokens)
    x_own0 = x_all[:OWN]
    branch1 = rel(cotangent) * live_rows.astype(BF)

    partial, keep0 = attn_forward(0, sec_flag, slopes, [x_all], vec0, dist, qkv, dense)
    hidden0, second = after_attn(scatter_rows(partial), x_own0, vec0)
    got_f0, got_c0 = swap(keep0["send_f"]), swap(keep0["context"])
    partial, act_grad0, hold_l0, send_l0 = mlp_forward(
        0, sec_flag, gather_rows(second), vec0, expand, shrink
    )
    got_l0 = swap(send_l0)
    out0, first = after_mlp(scatter_rows(partial), hidden0, live_own, vec0, vec1)
    partial, keep1 = attn_forward(
        1, sec_flag, slopes, gather_rows(first), vec1, dist, qkv, dense
    )
    got_f1, got_c1 = swap(keep1["send_f"]), swap(keep1["context"])
    hidden1, second = after_attn(scatter_rows(partial), out0, vec1)
    pre1 = branch1[:OWN]
    partial, (hold_l1, send_l1, hold_r1, send_r1, ebias1) = mlp_backward_last(
        1, sec_flag, gather_rows(second), branch1, vec1, expand, shrink
    )
    got_l1, got_r1 = swap(send_l1), swap(send_r1)
    blocks1 = scatter_rows(partial)
    grad_hidden, low1, sums_f1 = after_mlp_backward(blocks1, hidden1, pre1, vec1)
    out1, _ = after_mlp(blocks1, hidden1, live_own, vec1, vec1, OWN)
    mlp1 = mlp_weight_grad(hold_l1, got_l1, hold_r1, got_r1)
    partial, (grads1, hold_d1, send_d1, abias1) = attn_backward(
        1, sec_flag, gather_rows(low1), keep1, qkv, dense
    )
    got_g1, got_d1 = swap(grads1), swap(send_d1)
    g1, pre0, sums_i1 = after_attn_backward(
        scatter_rows(partial), grad_hidden, out0, live_own, vec1
    )
    attn1 = attn_weight_grad(
        keep1["hold_f"], got_f1, grads1, got_g1, keep1["context"], got_c1, hold_d1, got_d1
    )
    branch0 = gather_rows(pre0)
    branch0, mlp1, attn1 = lax.optimization_barrier((branch0, mlp1, attn1))
    partial, (hold_r0, send_r0, ebias0) = mlp_backward(
        0, sec_flag, branch0, act_grad0, expand, shrink
    )
    got_r0 = swap(send_r0)
    mlp0 = mlp_weight_grad(hold_l0, got_l0, hold_r0, got_r0)
    blocks, mlp0 = lax.optimization_barrier((scatter_rows(partial), mlp0))
    mlp1, attn1, mlp0 = lax.psum((mlp1, attn1, mlp0), "dp")
    grad_hidden, low0, sums_f0 = after_mlp_backward(blocks, hidden0, pre0, vec0)
    low_blocks = gather_rows(low0)
    partial, (grads0, hold_d0, send_d0, abias0, sums_h0) = attn_backward(
        0, sec_flag, low_blocks, keep0, qkv, dense
    )
    got_g0, got_d0 = swap(grads0), swap(send_d0)
    g0, _, _ = after_attn_backward(
        scatter_rows(partial), grad_hidden, x_own0, live_own, vec0
    )
    def small_rows(sums_i, sums_f, ebias, abias):
        last = jnp.pad(abias.reshape(1, 512), ((0, 0), (0, 512)))
        return jnp.concatenate([sums_i, sums_f, ebias, last], axis=0)

    small0 = small_rows(sums_h0, sums_f0, ebias0, abias0)
    small1 = small_rows(sums_i1, sums_f1, ebias1, abias1)
    small = jnp.where(on0, small0, small1) + swap(jnp.where(on0, small1, small0))
    small = jnp.pad(small.astype(BF).reshape(16, 2, 256), ((0, 0), (0, 14), (0, 0)))
    parts0 = (
        keep0["hold_f"], got_f0, grads0, got_g0, keep0["context"], got_c0, hold_d0, got_d0
    )
    attn0 = lax.all_to_all(attn_weight_joint(parts0, small), "dp", 0, 0)

    def all_slots(held0, held1):
        mine = jnp.where(on0, held0, held1).reshape(2, 32, -1)
        other = swap(jnp.where(on0, held1, held0)).reshape(2, 32, -1)
        return jnp.concatenate(
            [jnp.where(on0, mine, other), jnp.where(on0, other, mine)], axis=0
        )

    layer_out = all_slots(out0, out1)
    input_grad = all_slots(g0, g1)

    attn0, layer_out, input_grad = lax.optimization_barrier((attn0, layer_out, input_grad))
    attn0 = lax.all_to_all(spread_sums(attn0), "dp", 0, 0)
    small = attn0[:, 128:130].reshape(8, 1024)
    mixed = small[:6].astype(F32)
    mixed = mixed + sum(
        lax.ppermute(small[:6], "mp", ring("mp", k)).astype(F32) for k in (1, 2, 3)
    )
    alone = small[6:].astype(F32)
    thin = write_attn(0, sec_flag, False, attn0, [], 1e6)
    thin = write_attn(0, sec_flag, True, swap(attn0), thin, 1e6)
    mlp1, attn1, mlp0, mixed, alone, thin = lax.optimization_barrier(
        (mlp1, attn1, mlp0, mixed, alone, thin)
    )
    far = swap(jnp.where(on0, mlp1, mlp0))
    far_attn1 = swap(attn1)
    big = write_mlp(sec_flag, False, mlp0, mlp1, [])
    thin = write_attn(1, sec_flag, False, attn1, thin, 1e6)
    big, thin, far, far_attn1 = lax.optimization_barrier((big, thin, far, far_attn1))
    big = write_mlp(sec_flag, True, far, far, big)
    thin = write_attn(1, sec_flag, True, far_attn1, thin, 1e6)
    wide = [*big, *thin]

    return (
        layer_out[None],
        input_grad[None],
        mixed[0:1],
        mixed[1:2],
        jnp.transpose(wide[2], (1, 0, 2))[None],
        alone[1, :512].reshape(1, 2, 256),
        wide[3][None],
        mixed[2:3],
        mixed[3:4],
        mixed[4:5],
        wide[0][None],
        alone[0:1],
        wide[1][None],
        mixed[5:6],
    )


def solution(mesh):
    return jax.shard_map(
        per_device,
        mesh=mesh,
        in_specs=(
            P("dp", None, None),
            P("dp", None, None),
            P("dp", None),
            P("section", None),
            P("section", None),
            P("section", None, None, "mp"),
            P("section", None, "mp"),
            P("section", "mp", None),
            P("section", None),
            P("section", None),
            P("section", None),
            P("section", None, "mp"),
            P("section", "mp"),
            P("section", "mp", None),
            P("section", None),
        ),
        out_specs=(
            P("section", "dp", "mp", None),
            P("section", "dp", "mp", None),
            P("section", None),
            P("section", None),
            P("section", None, None, "mp"),
            P("section", None, "mp"),
            P("section", "mp", None),
            P("section", None),
            P("section", None),
            P("section", None),
            P("section", None, "mp"),
            P("section", "mp"),
            P("section", "mp", None),
            P("section", None),
        ),
        check_vma=False,
    )
```

```python
import jax
import jax.numpy as jnp
from jax import lax
from jax.experimental import pallas as pl
from jax.experimental.pallas import tpu as pltpu
from jax.sharding import PartitionSpec as P

HEADS = 16
HEAD = 64
EPS = 1e-05
BF = jnp.bfloat16
F32 = jnp.float32


def dot(a, b):
    return jnp.dot(a, b, preferred_element_type=F32)


def dot_t(a, b):
    return lax.dot_general(a, b, (((1,), (1,)), ((), ())), preferred_element_type=F32)


def t_dot(a, b):
    return lax.dot_general(a, b, (((0,), (0,)), ((), ())), preferred_element_type=F32)


def normalize(h):
    center = h - jnp.mean(h, axis=-1, keepdims=True)
    inverse = lax.rsqrt(jnp.mean(center * center, axis=-1, keepdims=True) + EPS)
    return center * inverse, inverse


def norm_back(normed, inverse, gain, grad):
    z = grad * gain
    return inverse * (
        z
        - jnp.mean(z, axis=-1, keepdims=True)
        - normed * jnp.mean(z * normed, axis=-1, keepdims=True)
    )


def ring(axis, steps):
    n = lax.axis_size(axis)
    return [(i, (i + steps) % n) for i in range(n)]


def swap(x):
    return lax.ppermute(x, "section", [(0, 1), (1, 0)])


def gather_rows(own):
    return [own] + [lax.ppermute(own, "mp", ring("mp", k)) for k in (1, 2, 3)]


def scatter_rows(blocks):
    return [blocks[0]] + [lax.ppermute(blocks[k], "mp", ring("mp", -k)) for k in (1, 2, 3)]


GELU_C = 0.7978845608
GELU_A = 0.044715
ROWS = 256
OWN = 64
D = 1024
FF = 1024
TILE = 256
SCALE = HEAD**-0.5


def gelu_pair(u):
    t = jnp.tanh(GELU_C * (u + GELU_A * u * u * u))
    act = 0.5 * u * (1 + t)
    grad = 0.5 * (1 + t) + 0.5 * u * (1 - t * t) * (GELU_C * (1 + 3 * GELU_A * u * u))
    return act, grad


def sds(shape, dtype):
    return jax.ShapeDtypeStruct(shape, dtype)


PARTIAL = [sds((OWN, D), F32)] + [sds((OWN, D), BF)] * 3
PARTIAL_TWO = [sds((2 * OWN, D), F32)] + [sds((2 * OWN, D), BF)] * 3
VM = pl.BlockSpec(memory_space=pltpu.VMEM)
SM = pl.BlockSpec(memory_space=pltpu.SMEM)
HB = pl.BlockSpec(memory_space=pltpu.HBM)


def call(kernel, outs, ins, scratch=(), flops=1e9, limit=52):
    specs = [HB if kind == "h" else SM if kind == "s" else VM for kind, _ in ins]
    arrays = [a for _, a in ins]
    size = sum(a.size * a.dtype.itemsize for a in arrays) + sum(
        o.size * o.dtype.itemsize for o in outs
    )
    return pl.pallas_call(
        kernel,
        out_shape=list(outs),
        in_specs=specs,
        out_specs=[VM] * len(outs),
        scratch_shapes=list(scratch),
        compiler_params=pltpu.CompilerParams(vmem_limit_bytes=limit * 2**20),
        cost_estimate=pl.CostEstimate(
            flops=int(flops), bytes_accessed=int(size), transcendentals=0
        ),
    )(*arrays)


def fetch(sec, layer, own, got, dst, sem):
    mine = sec[0] == layer

    @pl.when(mine)
    def _():
        pltpu.make_async_copy(own, dst, sem).start()

    @pl.when(jnp.logical_not(mine))
    def _():
        pltpu.make_async_copy(got, dst, sem).start()

    return pltpu.make_async_copy(own, dst, sem)


def put_partial(outs, cols, value, at=0):
    rows = pl.ds(at, OWN)
    outs[0][rows, cols] = value[:OWN]
    for k in (1, 2, 3):
        outs[k][rows, cols] = value[OWN * k : OWN * (k + 1)].astype(BF)


def tiles(width):
    return [pl.ds(i * TILE, TILE) for i in range(width // TILE)]


def lane_low():
    return lax.broadcasted_iota(jnp.int32, (ROWS, 128), 1) < HEAD


def attn_forward(layer, sec, slopes, source, vec, dist, qkv, dense):
    def kernel(*refs):
        n = len(source)
        sec, slopes, src = refs[0], refs[1], refs[2 : 2 + n]
        vec, dist, qo, qg, do, dg = refs[2 + n : 8 + n]
        o0, o1, o2, o3, proj, probs, context, hold, send = refs[8 + n : 17 + n]
        first, wq, wd, sem = refs[-4:]
        get_q = fetch(sec, layer, qo, qg, wq, sem.at[0])
        get_d = fetch(sec, layer, do, dg, wd, sem.at[1])
        if n == 1:
            normed, _ = normalize(src[0][...].astype(F32))
            first[...] = (normed * vec[0:1] + vec[1:2]).astype(BF)
            refs[17 + n][...] = normed.astype(BF)
        else:
            for k in range(4):
                first[pl.ds(OWN * k, OWN)] = src[k][...]
        on0 = sec[0] == 0
        hold[...] = jnp.where(on0, first[:, :512], first[:, 512:])
        send[...] = jnp.where(on0, first[:, 512:], first[:, :512])
        get_q.wait()
        f = first[...]
        proj[0] = (dot(f, wq[0]) + vec[7:8, 0:256]).astype(BF)
        proj[1] = dot(f, wq[1]).astype(BF)
        proj[2] = (dot(f, wq[2]) + vec[7:8, 256:512]).astype(BF)
        low = lane_low()
        for pair in range(2):
            cols = pl.ds(128 * pair, 128)
            q, k, v = proj[0, :, cols], proj[1, :, cols], proj[2, :, cols]
            ctx = []
            for h in range(2):
                picked = jnp.where(low if h == 0 else jnp.logical_not(low), q, jnp.zeros_like(q))
                s = dot_t(picked, k) * SCALE - slopes[2 * pair + h] * dist[...]
                e = jnp.exp(s - jnp.max(s, axis=-1, keepdims=True))
                p = e / jnp.sum(e, axis=-1, keepdims=True)
                p = p.astype(BF)
                probs[2 * pair + h] = p
                ctx.append(dot(p, v))
            context[:, cols] = jnp.where(low, ctx[0], ctx[1]).astype(BF)
        get_d.wait()
        c = context[...]
        for cols in tiles(D):
            put_partial((o0, o1, o2, o3), cols, dot(c, wd[:, cols]))

    outs = PARTIAL + [
        sds((3, ROWS, 256), BF),
        sds((4, ROWS, ROWS), BF),
        sds((ROWS, 256), BF),
        sds((ROWS, 512), BF),
        sds((ROWS, 512), BF),
    ] + [sds((ROWS, D), BF)] * (len(source) == 1)
    ins = [("s", sec), ("s", slopes)] + [("v", a) for a in source]
    ins += [("v", vec), ("v", dist), ("h", qkv[0]), ("h", qkv[1]), ("h", dense[0]), ("h", dense[1])]
    scratch = [
        pltpu.VMEM((ROWS, D), BF),
        pltpu.VMEM((3, D, 256), BF),
        pltpu.VMEM((256, D), BF),
        pltpu.SemaphoreType.DMA((2,)),
    ]
    r = call(kernel, outs, ins, scratch, 8e8)
    keep = dict(proj=r[4], probs=r[5], context=r[6], hold_f=r[7], send_f=r[8])
    if len(source) == 1:
        keep["normed"] = r[9]
    return r[:4], keep


def total(refs, at=0):
    rows = pl.ds(at, OWN)
    return refs[0][rows, :] + sum(r[rows, :].astype(F32) for r in refs[1:])


def after_attn(blocks, x_own, vec):
    def kernel(a, b, c, d, x, vec, hidden, second):
        h = x[...].astype(F32) + total((a, b, c, d)) + vec[2:3]
        hidden[...] = h
        normed, _ = normalize(h)
        second[...] = (normed * vec[3:4] + vec[4:5]).astype(BF)

    return call(
        kernel,
        [sds((OWN, D), F32), sds((OWN, D), BF)],
        [("v", a) for a in (*blocks, x_own, vec)],
        flops=2e6,
    )


def mlp_forward(layer, sec, blocks, vec, expand, shrink):
    def kernel(sec, b0, b1, b2, b3, vec, eo, eg, so, sg, o0, o1, o2, o3, act_grad, hold, send, second, act, we, ws, sem):
        get_e = fetch(sec, layer, eo, eg, we, sem.at[0])
        get_s = fetch(sec, layer, so, sg, ws, sem.at[1])
        for k, b in enumerate((b0, b1, b2, b3)):
            second[pl.ds(OWN * k, OWN)] = b[...]
        get_e.wait()
        x = second[...]
        for cols in tiles(FF):
            a, g = gelu_pair(dot(x, we[:, cols]) + vec[6:7, cols])
            act[:, cols] = a.astype(BF)
            act_grad[:, cols] = g.astype(BF)
        get_s.wait()
        a = act[...]
        on0 = sec[0] == 0
        for cols in tiles(D):
            put_partial((o0, o1, o2, o3), cols, dot(a, ws[:, cols]))
            hold[:, cols] = jnp.where(on0, second[:, cols], act[:, cols])
            send[:, cols] = jnp.where(on0, act[:, cols], second[:, cols])

    wide = sds((ROWS, FF), BF)
    ins = [("s", sec)] + [("v", a) for a in (*blocks, vec)]
    ins += [("h", a) for a in (*expand, *shrink)]
    big = pltpu.VMEM((D, FF), BF)
    r = call(
        kernel,
        PARTIAL + [wide, wide, wide],
        ins,
        [pltpu.VMEM((ROWS, D), BF), pltpu.VMEM((ROWS, FF), BF), big, big, pltpu.SemaphoreType.DMA((2,))],
        1.1e9,
    )
    return r[:4], r[4], r[5], r[6]


def after_mlp(blocks, hidden, live, vec, vec_next, at=0):
    def kernel(a, b, c, d, hidden, live, vec, vec_next, out, first):
        o = (live[...] * (hidden[...] + total((a, b, c, d), at) + vec[5:6])).astype(BF)
        out[...] = o
        normed, _ = normalize(o.astype(F32))
        first[...] = (normed * vec_next[0:1] + vec_next[1:2]).astype(BF)

    return call(
        kernel,
        [sds((OWN, D), BF), sds((OWN, D), BF)],
        [("v", a) for a in (*blocks, hidden, live, vec, vec_next)],
        flops=2e6,
    )


def mlp_backward_last(layer, sec, blocks, branch, vec, expand, shrink):
    def kernel(
        sec, b0, b1, b2, b3, branch, vec, eo, eg, so, sg,
        o0, o1, o2, o3, hold_l, send_l, hold_r, send_r, bias, second, up_grad, act, we, ws, sem,
    ):
        get_e = fetch(sec, layer, eo, eg, we, sem.at[0])
        get_s = fetch(sec, layer, so, sg, ws, sem.at[1])
        for k, b in enumerate((b0, b1, b2, b3)):
            second[pl.ds(OWN * k, OWN)] = b[...]
        get_e.wait()
        get_s.wait()
        x = second[...]
        br = branch[...]
        on0 = sec[0] == 0
        for cols in tiles(FF):
            a, g = gelu_pair(dot(x, we[:, cols]) + vec[6:7, cols])
            a = a.astype(BF)
            act[:, cols] = a
            u = (dot_t(br, ws[cols, :]) * g).astype(BF)
            up_grad[:, cols] = u
            bias[:, cols] = jnp.sum(u.astype(F32), axis=0, keepdims=True)
            hold_l[:, cols] = jnp.where(on0, x_tile(second, cols), a)
            send_l[:, cols] = jnp.where(on0, a, x_tile(second, cols))
            hold_r[:, cols] = jnp.where(on0, u, x_tile(branch, cols))
            send_r[:, cols] = jnp.where(on0, x_tile(branch, cols), u)
        u = up_grad[...]
        for cols in tiles(D):
            put_partial((o0, o1, o2, o3), cols, dot_t(u, we[cols, :]))
            put_partial((o0, o1, o2, o3), cols, dot(act[...], ws[:, cols]), OWN)

    wide = sds((ROWS, FF), BF)
    ins = [("s", sec)] + [("v", a) for a in (*blocks, branch, vec)]
    ins += [("h", a) for a in (*expand, *shrink)]
    big = pltpu.VMEM((D, FF), BF)
    r = call(
        kernel,
        PARTIAL_TWO + [wide] * 4 + [sds((1, FF), F32)],
        ins,
        [pltpu.VMEM((ROWS, D), BF)]
        + [pltpu.VMEM((ROWS, FF), BF)] * 2
        + [big, big, pltpu.SemaphoreType.DMA((2,))],
        1.6e9,
    )
    return r[:4], r[4:]


def x_tile(ref, cols):
    return ref[:, cols]


def mlp_backward(layer, sec, blocks, act_grad, expand, shrink):
    def kernel(
        sec, b0, b1, b2, b3, act_grad, eo, eg, so, sg,
        o0, o1, o2, o3, hold_r, send_r, bias, branch, up_grad, we, ws, sem,
    ):
        get_s = fetch(sec, layer, so, sg, ws, sem.at[1])
        get_e = fetch(sec, layer, eo, eg, we, sem.at[0])
        for k, b in enumerate((b0, b1, b2, b3)):
            branch[pl.ds(OWN * k, OWN)] = b[...]
        get_s.wait()
        br = branch[...]
        on0 = sec[0] == 0
        for cols in tiles(FF):
            u = (dot_t(br, ws[cols, :]) * act_grad[:, cols].astype(F32)).astype(BF)
            up_grad[:, cols] = u
            bias[:, cols] = jnp.sum(u.astype(F32), axis=0, keepdims=True)
            hold_r[:, cols] = jnp.where(on0, u, branch[:, cols])
            send_r[:, cols] = jnp.where(on0, branch[:, cols], u)
        get_e.wait()
        u = up_grad[...]
        for cols in tiles(D):
            put_partial((o0, o1, o2, o3), cols, dot_t(u, we[cols, :]))

    wide = sds((ROWS, FF), BF)
    ins = [("s", sec)] + [("v", a) for a in (*blocks, act_grad)]
    ins += [("h", a) for a in (*expand, *shrink)]
    big = pltpu.VMEM((D, FF), BF)
    r = call(
        kernel,
        PARTIAL + [wide] * 2 + [sds((1, FF), F32)],
        ins,
        [pltpu.VMEM((ROWS, D), BF), pltpu.VMEM((ROWS, FF), BF), big, big, pltpu.SemaphoreType.DMA((2,))],
        1.1e9,
    )
    return r[:4], r[4:]


def after_mlp_backward(blocks, hidden, grad_own, vec):
    def kernel(a, b, c, d, hidden, grad_own, vec, grad_hidden, low, sums):
        gs = total((a, b, c, d))
        pre = grad_own[...].astype(F32)
        normed, inverse = normalize(hidden[...])
        gh = pre + norm_back(normed, inverse, vec[3:4], gs)
        grad_hidden[...] = gh
        lo = gh.astype(BF)
        low[...] = lo
        sums[0:1] = jnp.sum(lo.astype(F32), axis=0, keepdims=True)
        sums[1:2] = jnp.sum(gs * normed, axis=0, keepdims=True)
        sums[2:3] = jnp.sum(gs, axis=0, keepdims=True)
        sums[3:4] = jnp.sum(pre, axis=0, keepdims=True)

    return call(
        kernel,
        [sds((OWN, D), F32), sds((OWN, D), BF), sds((4, D), F32)],
        [("v", a) for a in (*blocks, hidden, grad_own, vec)],
        flops=2e6,
    )


def attn_backward(layer, sec, blocks, keep, qkv, dense):
    summed = "normed" in keep

    def kernel(sec, b0, b1, b2, b3, proj, probs, *refs):
        normed = refs[0] if summed else None
        qo, qg, do, dg, o0, o1, o2, o3, grads, hold, send, bias = refs[summed : 12 + summed]
        full, wq, wd, sem = refs[-4:]
        get_d = fetch(sec, layer, do, dg, wd, sem.at[1])
        get_q = fetch(sec, layer, qo, qg, wq, sem.at[0])
        for k, b in enumerate((b0, b1, b2, b3)):
            full[pl.ds(OWN * k, OWN)] = b[...]
        on0 = sec[0] == 0
        hold[...] = jnp.where(on0, full[:, :512], full[:, 512:])
        send[...] = jnp.where(on0, full[:, 512:], full[:, :512])
        get_d.wait()
        gc = dot_t(full[...], wd[...]).astype(BF)
        low = lane_low()
        for pair in range(2):
            cols = pl.ds(128 * pair, 128)
            q, k, v = proj[0, :, cols], proj[1, :, cols], proj[2, :, cols]
            g = gc[:, 128 * pair : 128 * pair + 128]
            parts = []
            for h in range(2):
                p_low = probs[2 * pair + h]
                p = p_low.astype(F32)
                picked = jnp.where(low if h == 0 else jnp.logical_not(low), g, jnp.zeros_like(g))
                gp = dot_t(picked, v)
                gs = (p * (gp - jnp.sum(p * gp, axis=-1, keepdims=True))).astype(BF)
                parts.append((dot(gs, k) * SCALE, t_dot(gs, q) * SCALE, t_dot(p_low, g)))
            for c in range(3):
                grads[:, pl.ds(256 * c + 128 * pair, 128)] = jnp.where(
                    low, parts[0][c], parts[1][c]
                ).astype(BF)
        bias[0:1] = jnp.sum(grads[:, 0:256].astype(F32), axis=0, keepdims=True)
        bias[1:2] = jnp.sum(grads[:, 512:768].astype(F32), axis=0, keepdims=True)
        get_q.wait()
        gr = [grads[:, 256 * c : 256 * c + 256] for c in range(3)]
        for cols in tiles(D):
            o = dot_t(gr[0], wq[0, cols]) + dot_t(gr[1], wq[1, cols]) + dot_t(gr[2], wq[2, cols])
            put_partial((o0, o1, o2, o3), cols, o)
            if summed:
                sums = refs[12 + summed]
                sums[0:1, cols] = jnp.sum(o * normed[:, cols].astype(F32), axis=0, keepdims=True)
                sums[1:2, cols] = jnp.sum(o, axis=0, keepdims=True)

    half = sds((ROWS, 512), BF)
    ins = [("s", sec)] + [("v", a) for a in (*blocks, keep["proj"], keep["probs"])]
    if summed:
        ins += [("v", keep["normed"])]
    ins += [("h", a) for a in (*qkv, *dense)]
    r = call(
        kernel,
        PARTIAL
        + [sds((ROWS, 768), BF), half, half, sds((2, 256), F32)]
        + [sds((2, D), F32)] * summed,
        ins,
        [
            pltpu.VMEM((ROWS, D), BF),
            pltpu.VMEM((3, D, 256), BF),
            pltpu.VMEM((256, D), BF),
            pltpu.SemaphoreType.DMA((2,)),
        ],
        1.2e9,
    )
    return r[:4], r[4:]


def after_attn_backward(blocks, grad_hidden, x_own, live, vec):
    def kernel(a, b, c, d, grad_hidden, x, live, vec, out, pre, sums):
        gf = total((a, b, c, d))
        normed, inverse = normalize(x[...].astype(F32))
        g = (grad_hidden[...] + norm_back(normed, inverse, vec[0:1], gf)).astype(BF)
        out[...] = g
        pre[...] = (live[...] * g.astype(F32)).astype(BF)
        sums[0:1] = jnp.sum(gf * normed, axis=0, keepdims=True)
        sums[1:2] = jnp.sum(gf, axis=0, keepdims=True)

    return call(
        kernel,
        [sds((OWN, D), BF), sds((OWN, D), BF), sds((2, D), F32)],
        [("v", a) for a in (*blocks, grad_hidden, x_own, live, vec)],
        flops=2e6,
    )


def mlp_weight_grad(left, got_left, right, got_right):
    def kernel(l, gl, r, gr, out):
        rv, grv = r[...], gr[...]
        for t in range(4):
            rows = pl.ds(t * TILE, TILE)
            g = (t_dot(l[:, rows], rv) + t_dot(gl[:, rows], grv)).astype(BF)
            for i in range(4):
                for c in range(4):
                    out[4 * t + i, pl.ds(64 * c, 64), :] = g[
                        64 * i : 64 * i + 64, 256 * c : 256 * c + 256
                    ]

    return call(
        kernel,
        [sds((16, 256, 256), BF)],
        [("v", a) for a in (left, got_left, right, got_right)],
        flops=1.1e9,
    )[0]


def mlp_weight_pair(sec, left, got_left, right, got_right, other):
    def kernel(sec, l, gl, r, gr, other, mine, away):
        rv, grv = r[...], gr[...]
        on0 = sec[0] == 0
        for t in range(4):
            rows = pl.ds(t * TILE, TILE)
            g = (t_dot(l[:, rows], rv) + t_dot(gl[:, rows], grv)).astype(BF)
            for i in range(4):
                for c in range(4):
                    at = pl.ds(64 * c, 64)
                    fresh = g[64 * i : 64 * i + 64, 256 * c : 256 * c + 256]
                    old = other[4 * t + i, at, :]
                    mine[4 * t + i, at, :] = jnp.where(on0, fresh, old)
                    away[4 * t + i, at, :] = jnp.where(on0, old, fresh)

    return call(
        kernel,
        [sds((16, 256, 256), BF)] * 2,
        [("s", sec)] + [("v", a) for a in (left, got_left, right, got_right, other)],
        flops=1.1e9,
    )


def attn_weight_grad(first, got_first, grads, got_grads, ctx, got_ctx, low, got_low):
    def kernel(f, gf, g, gg, c, gc, d, gd, out):
        def put(at, value):
            value = value.astype(BF)
            out[at // 128] = value[:128]
            out[at // 128 + 1] = value[128:]

        for half in range(2):
            rows = slice(256 * half, 256 * half + 256)
            for part in range(3):
                cols = slice(256 * part, 256 * part + 256)
                put(
                    512 * part + 256 * half,
                    t_dot(f[:, rows], g[:, cols]) + t_dot(gf[:, rows], gg[:, cols]),
                )
            put(1536 + 256 * half, t_dot(c[...], d[:, rows]) + t_dot(gc[...], gd[:, rows]))

    return call(
        kernel,
        [sds((16, 128, 256), BF)],
        [("v", a) for a in (first, got_first, grads, got_grads, ctx, got_ctx, low, got_low)],
        flops=5.4e8,
    )[0]


def attn_weight_joint(parts, small):
    def kernel(f, gf, g, gg, c, gc, d, gd, sm, out):
        out[:, pl.ds(128, 16)] = sm[...]

        def put(at, value):
            value = value.astype(BF)
            out[at // 128, pl.ds(0, 128)] = value[:128]
            out[at // 128 + 1, pl.ds(0, 128)] = value[128:]

        for half in range(2):
            rows = slice(256 * half, 256 * half + 256)
            for part in range(3):
                cols = slice(256 * part, 256 * part + 256)
                put(
                    512 * part + 256 * half,
                    t_dot(f[:, rows], g[:, cols]) + t_dot(gf[:, rows], gg[:, cols]),
                )
            put(1536 + 256 * half, t_dot(c[...], d[:, rows]) + t_dot(gc[...], gd[:, rows]))

    return call(
        kernel, [sds((16, 144, 256), BF)], [("v", a) for a in (*parts, small)], flops=5.4e8
    )[0]


def spread_sums(got):
    def kernel(m, out):
        share = jnp.sum(m[...].astype(F32), axis=0).astype(BF)
        for i in range(16):
            out[i] = share

    return call(kernel, [sds((16, 144, 256), BF)], [("v", got)], flops=1e6)[0]


def write_call(layer, sec, kernel, grads, held, shapes, scratch, flops):
    n, m = len(grads), len(held)

    def body(sec, *refs):
        @pl.when(sec[0] == layer)
        def _():
            kernel(refs[:n], refs[n + m : n + m + len(shapes)], *refs[n + m + len(shapes) :])

    return pl.pallas_call(
        body,
        out_shape=shapes,
        in_specs=[SM] + [VM] * n + [HB] * m,
        out_specs=[HB] * len(shapes),
        scratch_shapes=[scratch, pltpu.SemaphoreType.DMA((5,))],
        input_output_aliases={1 + n + i: i for i in range(m)},
        compiler_params=pltpu.CompilerParams(vmem_limit_bytes=52 * 2**20),
        cost_estimate=pl.CostEstimate(flops=int(flops), bytes_accessed=6000000, transcendentals=0),
    )(sec, *grads, *held)


def write_mlp(sec, far, core0, core1, held):
    m = len(held)

    def kernel(sec, first, second, *refs):
        outs = refs[m : m + 2]
        low, wide, sem = refs[m + 2 :]
        fetch(sec, 0, first, second, low, sem.at[4]).wait()
        copies = [[], []]
        for t in range(4):
            for i in range(4 * t, 4 * t + 4):
                for c in range(4):
                    wide[pl.ds(64 * i, 64), pl.ds(256 * c, 256)] = low[
                        i, pl.ds(64 * c, 64), :
                    ].astype(F32)
            rows = pl.ds(256 * t, 256)
            for core in range(2):
                target = outs[1 - core if far else core]
                move = pltpu.make_async_copy(wide.at[rows], target.at[rows], sem.at[t])
                copies[core].append(move)
                pl.when(sec[0] == core)(move.start)
        for move in copies[0]:
            move.wait()

    return pl.pallas_call(
        kernel,
        out_shape=WIDE_OUT[:2],
        in_specs=[SM] + [HB] * (2 + m),
        out_specs=[HB] * 2,
        scratch_shapes=[
            pltpu.VMEM((16, 256, 256), BF),
            pltpu.VMEM((D, FF), F32),
            pltpu.SemaphoreType.DMA((5,)),
        ],
        input_output_aliases={3 + i: i for i in range(m)},
        compiler_params=pltpu.CompilerParams(vmem_limit_bytes=52 * 2**20),
        cost_estimate=pl.CostEstimate(
            flops=200000000000, bytes_accessed=6000000, transcendentals=0
        ),
    )(sec, core0, core1, *held)


def write_attn(layer, sec, far, grad, held, flops):
    which = (1 - layer) if far else layer

    def kernel(src, outs, tall, sem):
        for i in range(16):
            tall[pl.ds(128 * i, 128)] = src[0][i, pl.ds(0, 128), :].astype(F32)
        copies = []
        for p in range(3):
            piece = tall.at[pl.ds(512 * p, 512)]
            target = outs[0].at[p, pl.ds(512 * which, 512)]
            copies.append(pltpu.make_async_copy(piece, target, sem.at[p]))
        for h in range(2):
            piece = tall.at[pl.ds(1536 + 256 * h, 256)]
            target = outs[1].at[:, pl.ds(512 * which + 256 * h, 256)]
            copies.append(pltpu.make_async_copy(piece, target, sem.at[3 + h]))
        for c in copies:
            c.start()
        for c in copies:
            c.wait()

    return write_call(
        layer, sec, kernel, [grad], held, WIDE_OUT[2:], pltpu.VMEM((2048, 256), F32), flops
    )


WIDE_OUT = [sds((D, FF), F32), sds((D, FF), F32), sds((3, D, 256), F32), sds((256, D), F32)]


def per_device(
    tokens,
    cotangent,
    seq_lengths,
    attn_gain,
    attn_shift,
    attn_weight,
    attn_bias,
    dense_weight,
    dense_bias,
    mlp_gain,
    mlp_shift,
    expand_weight,
    expand_bias,
    shrink_weight,
    shrink_bias,
):
    sec = lax.axis_index("section")
    mp = lax.axis_index("mp")
    on0 = sec == 0

    own_qkv = jnp.transpose(attn_weight[0], (1, 0, 2))
    own_w = [own_qkv, dense_weight[0], expand_weight[0], shrink_weight[0]]
    vectors = jnp.concatenate(
        [attn_gain, attn_shift, dense_bias, mlp_gain, mlp_shift, shrink_bias, expand_bias]
        + [jnp.pad(attn_bias.reshape(1, -1), ((0, 0), (0, 512)))],
        axis=0,
    )
    got_vec = swap(vectors)
    got_w = [swap(w) for w in own_w]

    def pick(layer, own, got):
        return jnp.where(on0, own, got) if layer == 0 else jnp.where(on0, got, own)

    vec0 = pick(0, vectors, got_vec)
    vec1 = pick(1, vectors, got_vec)
    qkv, dense, expand, shrink = [(o, g) for o, g in zip(own_w, got_w)]
    sec_flag = sec.astype(jnp.int32).reshape(1)

    def rel(x):
        x = lax.dynamic_slice_in_dim(x, 2 * sec, 2, 0).reshape(2, 4, 32, -1)
        parts = [lax.dynamic_index_in_dim(x, (mp - k) % 4, 1, keepdims=False) for k in range(4)]
        return jnp.concatenate(parts, axis=0).reshape(256, -1)

    lengths = lax.dynamic_slice_in_dim(seq_lengths, 2 * sec, 2, 0)
    bounds = jnp.cumsum(lengths, axis=1)
    pos = (32 * ((mp - jnp.arange(4)) % 4)[:, None] + jnp.arange(32)[None]).reshape(128)
    segment = jnp.sum((pos[None, :, None] >= bounds[:, None, :]).astype(jnp.int32), axis=2)
    segment = segment + jnp.array([0, 8], jnp.int32)[:, None]

    def spread(x):
        return jnp.broadcast_to(x, (2, 128)).reshape(2, 4, 32).transpose(1, 0, 2).reshape(256)

    seg_rows, pos_rows = spread(segment), spread(pos[None])
    allowed = (seg_rows[:, None] == seg_rows[None, :]) & (pos_rows[None, :] <= pos_rows[:, None])
    dist = jnp.where(allowed, (pos_rows[:, None] - pos_rows[None, :]).astype(F32), 1e33)
    live = (pos[None] < bounds[:, -1:]).astype(F32)
    live_rows = live.reshape(2, 4, 32).transpose(1, 0, 2).reshape(256, 1)
    live_own = live_rows[:64]
    heads_local = attn_weight.shape[3] // HEAD
    head_ids = mp * heads_local + jnp.arange(heads_local)
    slopes = jnp.exp2(-8.0 * (head_ids + 1).astype(F32) / HEADS)

    x_all = rel(tokens)
    x_own0 = x_all[:OWN]
    branch1 = rel(cotangent) * live_rows.astype(BF)

    partial, keep0 = attn_forward(0, sec_flag, slopes, [x_all], vec0, dist, qkv, dense)
    hidden0, second = after_attn(scatter_rows(partial), x_own0, vec0)
    got_f0, got_c0 = swap(keep0["send_f"]), swap(keep0["context"])
    partial, act_grad0, hold_l0, send_l0 = mlp_forward(
        0, sec_flag, gather_rows(second), vec0, expand, shrink
    )
    got_l0 = swap(send_l0)
    out0, first = after_mlp(scatter_rows(partial), hidden0, live_own, vec0, vec1)
    partial, keep1 = attn_forward(
        1, sec_flag, slopes, gather_rows(first), vec1, dist, qkv, dense
    )
    got_f1, got_c1 = swap(keep1["send_f"]), swap(keep1["context"])
    hidden1, second = after_attn(scatter_rows(partial), out0, vec1)
    pre1 = branch1[:OWN]
    partial, (hold_l1, send_l1, hold_r1, send_r1, ebias1) = mlp_backward_last(
        1, sec_flag, gather_rows(second), branch1, vec1, expand, shrink
    )
    got_l1, got_r1 = swap(send_l1), swap(send_r1)
    blocks1 = scatter_rows(partial)
    grad_hidden, low1, sums_f1 = after_mlp_backward(blocks1, hidden1, pre1, vec1)
    out1, _ = after_mlp(blocks1, hidden1, live_own, vec1, vec1, OWN)
    mlp1 = mlp_weight_grad(hold_l1, got_l1, hold_r1, got_r1)
    partial, (grads1, hold_d1, send_d1, abias1) = attn_backward(
        1, sec_flag, gather_rows(low1), keep1, qkv, dense
    )
    got_g1, got_d1 = swap(grads1), swap(send_d1)
    g1, pre0, sums_i1 = after_attn_backward(
        scatter_rows(partial), grad_hidden, out0, live_own, vec1
    )
    attn1 = attn_weight_grad(
        keep1["hold_f"], got_f1, grads1, got_g1, keep1["context"], got_c1, hold_d1, got_d1
    )
    branch0 = gather_rows(pre0)
    branch0, mlp1, attn1 = lax.optimization_barrier((branch0, mlp1, attn1))
    partial, (hold_r0, send_r0, ebias0) = mlp_backward(
        0, sec_flag, branch0, act_grad0, expand, shrink
    )
    got_r0 = swap(send_r0)
    mine, away = mlp_weight_pair(sec_flag, hold_l0, got_l0, hold_r0, got_r0, mlp1)
    blocks, _ = lax.optimization_barrier((scatter_rows(partial), mine))
    mine, attn1, away = lax.psum((mine, attn1, away), "dp")
    grad_hidden, low0, sums_f0 = after_mlp_backward(blocks, hidden0, pre0, vec0)
    low_blocks = gather_rows(low0)
    partial, (grads0, hold_d0, send_d0, abias0, sums_h0) = attn_backward(
        0, sec_flag, low_blocks, keep0, qkv, dense
    )
    got_g0, got_d0 = swap(grads0), swap(send_d0)
    g0, _, _ = after_attn_backward(
        scatter_rows(partial), grad_hidden, x_own0, live_own, vec0
    )
    def small_rows(sums_i, sums_f, ebias, abias):
        last = jnp.pad(abias.reshape(1, 512), ((0, 0), (0, 512)))
        return jnp.concatenate([sums_i, sums_f, ebias, last], axis=0)

    small0 = small_rows(sums_h0, sums_f0, ebias0, abias0)
    small1 = small_rows(sums_i1, sums_f1, ebias1, abias1)
    small = jnp.where(on0, small0, small1) + swap(jnp.where(on0, small1, small0))
    small = jnp.pad(small.astype(BF).reshape(16, 2, 256), ((0, 0), (0, 14), (0, 0)))
    parts0 = (
        keep0["hold_f"], got_f0, grads0, got_g0, keep0["context"], got_c0, hold_d0, got_d0
    )
    attn0 = lax.all_to_all(attn_weight_joint(parts0, small), "dp", 0, 0)

    def all_slots(held0, held1):
        mine = jnp.where(on0, held0, held1).reshape(2, 32, -1)
        other = swap(jnp.where(on0, held1, held0)).reshape(2, 32, -1)
        return jnp.concatenate(
            [jnp.where(on0, mine, other), jnp.where(on0, other, mine)], axis=0
        )

    layer_out = all_slots(out0, out1)
    input_grad = all_slots(g0, g1)

    attn0, layer_out, input_grad = lax.optimization_barrier((attn0, layer_out, input_grad))
    attn0 = lax.all_to_all(spread_sums(attn0), "dp", 0, 0)
    small = attn0[:, 128:130].reshape(8, 1024)
    mixed = small[:6].astype(F32)
    mixed = mixed + sum(
        lax.ppermute(small[:6], "mp", ring("mp", k)).astype(F32) for k in (1, 2, 3)
    )
    alone = small[6:].astype(F32)
    thin = write_attn(0, sec_flag, False, attn0, [], 1e6)
    thin = write_attn(0, sec_flag, True, swap(attn0), thin, 1e6)
    mine, attn1, away, mixed, alone, thin = lax.optimization_barrier(
        (mine, attn1, away, mixed, alone, thin)
    )
    far = swap(away)
    far_attn1 = swap(attn1)
    big = write_mlp(sec_flag, False, mine, mine, [])
    thin = write_attn(1, sec_flag, False, attn1, thin, 1e6)
    big, thin, far, far_attn1 = lax.optimization_barrier((big, thin, far, far_attn1))
    big = write_mlp(sec_flag, True, far, far, big)
    thin = write_attn(1, sec_flag, True, far_attn1, thin, 1e6)
    wide = [*big, *thin]

    return (
        layer_out[None],
        input_grad[None],
        mixed[0:1],
        mixed[1:2],
        jnp.transpose(wide[2], (1, 0, 2))[None],
        alone[1, :512].reshape(1, 2, 256),
        wide[3][None],
        mixed[2:3],
        mixed[3:4],
        mixed[4:5],
        wide[0][None],
        alone[0:1],
        wide[1][None],
        mixed[5:6],
    )


def solution(mesh):
    return jax.shard_map(
        per_device,
        mesh=mesh,
        in_specs=(
            P("dp", None, None),
            P("dp", None, None),
            P("dp", None),
            P("section", None),
            P("section", None),
            P("section", None, None, "mp"),
            P("section", None, "mp"),
            P("section", "mp", None),
            P("section", None),
            P("section", None),
            P("section", None),
            P("section", None, "mp"),
            P("section", "mp"),
            P("section", "mp", None),
            P("section", None),
        ),
        out_specs=(
            P("section", "dp", "mp", None),
            P("section", "dp", "mp", None),
            P("section", None),
            P("section", None),
            P("section", None, None, "mp"),
            P("section", None, "mp"),
            P("section", "mp", None),
            P("section", None),
            P("section", None),
            P("section", None),
            P("section", None, "mp"),
            P("section", "mp"),
            P("section", "mp", None),
            P("section", None),
        ),
        check_vma=False,
    )
```
